128 devices in a mesh: dp: 8 (over x_hi, z), row: 4 (over y), col: 4 (over x_lo, core).
Axes of the slice: x: 4 (x_hi: 2, x_lo: 2; x = x_hi * 2 + x_lo), y: 4, z: 4, core: 2. Of those that a mesh axis runs over, the one named last changes fastest.
Arguments:
- inputs: bfloat16 [8192, 2048], P(('dp', 'row'), 'col'), may hold values from -6 to 6
- attention_gain: bfloat16 [2048], P('col'), may hold values from 0.5 to 1.5
- query_weight: bfloat16 [2048, 3072], P('col', 'row'), may hold values from -0.125 to 0.125
- latent_weight: bfloat16 [2048, 576], P('col'), may hold values from -0.125 to 0.125
- latent_gain: bfloat16 [512], replicated, may hold values from 0.5 to 1.5
- expand_weight: bfloat16 [512, 4096], P(None, ('row', 'col')), may hold values from -0.25 to 0.25
- output_weight: bfloat16 [2048, 2048], P('row', 'col'), may hold values from -0.5 to 0.5
- feedforward_gain: bfloat16 [2048], P('col'), may hold values from 0.5 to 1.5
- router_weight: bfloat16 [2048, 8], P('col'), may hold values from -0.25 to 0.25
- shared_gate: bfloat16 [2048, 2816], P('col', 'row'), may hold values from -0.125 to 0.125
- shared_up: bfloat16 [2048, 2816], P('col', 'row'), may hold values from -0.125 to 0.125
- shared_down: bfloat16 [2816, 2048], P('row', 'col'), may hold values from -0.109375 to 0.109375
- expert_gate: bfloat16 [8, 2048, 1408], P(None, 'col', 'row'), may hold values from -0.125 to 0.125
- expert_up: bfloat16 [8, 2048, 1408], P(None, 'col', 'row'), may hold values from -0.125 to 0.125
- expert_down: bfloat16 [8, 1408, 2048], P(None, 'row', 'col'), may hold values from -0.625 to 0.625
- routes: int32 [8192, 6], P('dp'), may hold values from 0 to 7, all different within a row; in each aligned block of 1024 rows (0 to 1023, 1024 to 2047, ...) at most 832 rows name the same one
- prefix: int32 [8], P('dp'), may hold values from 102 to 512
- cotangent: bfloat16 [8192, 2048], P(('dp', 'row'), 'col'), may hold values from -6 to 6
Outputs:
- output: bfloat16 [8192, 2048], P(('dp', 'row'), 'col')
- inputs_grad: bfloat16 [8192, 2048], P(('dp', 'row'), 'col')
- attention_gain_grad: float32 [2048], P('col')
- query_weight_grad: float32 [2048, 3072], P('col', 'row')
- latent_weight_grad: float32 [2048, 576], P('col')
- latent_gain_grad: float32 [512], replicated
- expand_weight_grad: float32 [512, 4096], P(None, ('row', 'col'))
- output_weight_grad: float32 [2048, 2048], P('row', 'col')
- feedforward_gain_grad: float32 [2048], P('col')
- router_weight_grad: float32 [2048, 8], P('col')
- shared_gate_grad: float32 [2048, 2816], P('col', 'row')
- shared_up_grad: float32 [2048, 2816], P('col', 'row')
- shared_down_grad: float32 [2816, 2048], P('row', 'col')
- expert_gate_grad: float32 [8, 2048, 1408], P('dp', 'col', 'row')
- expert_up_grad: float32 [8, 2048, 1408], P('dp', 'col', 'row')
- expert_down_grad: float32 [8, 1408, 2048], P('dp', 'row', 'col')
The draws below stay inside these ranges and needn't reach their ends.
Inputs may be any that keep to these rules, and one draw needn't show every extreme that they name: `routes`: within the 1024 rows of one sequence no expert is named by more than 832 rows, a bound that some block reaches; a row names 6 different experts.
All inputs are finite; a program needn't handle non-finite values.
Results may differ from the reference program's by a relative error of at most 0.019.
Values may be sent and summed in bfloat16 or wider, within the bound.
A program may use at most 256 MiB of HBM per device.

```python
import math
import jax
import jax.numpy as jnp
import numpy as np
from jax import lax

D = 2048
HEADS = 16
NOPE = 128
ROPE = 64
VDIM = 128
RANK = 512
FF = 1408
TOPK = 6
EXPERTS = 8
SEQ = 1024
SFF = 2816
CAP = 832
TOKENS = 8192
N_DP = 8


def with_ends(values, stream_key, low, top_value):
    longest = values.shape.index(max(values.shape))
    spots = []
    for shift in (0, 1):
        where = [jax.random.randint(jax.random.fold_in(stream_key, axis), (), 0, length) for axis, length in enumerate(values.shape)]
        where[longest] = (where[longest] + shift) % values.shape[longest]
        spots.append(tuple(where))
    return values.at[spots[0]].set(low).at[spots[1]].set(top_value)


def block_scale(stream_key, extent, pieces, least, high):
    level, own = 1.0, jax.random.fold_in(stream_key, 6)
    for axis_at, shards_of in pieces:
        draws = jnp.exp(jax.random.uniform(jax.random.fold_in(own, axis_at), (shards_of,), jnp.float32, least / len(pieces), high / len(pieces)))
        level = level * jnp.repeat(draws, extent[axis_at] // shards_of).reshape([-1 if axis == axis_at else 1 for axis in range(len(extent))])
    return level


def shared_out(stream_key, own, number, rows, amount, top, bound, lean):
    sequence = jax.random.permutation(stream_key, amount)
    packed, ordinary = portions_of(amount, rows * top, bound, lean, True), portions_of(amount, rows * top, bound, lean, False)
    places = jnp.arange(amount)

    def named(lengths, offset_by):
        used = int((lengths > 0).sum())
        fixed = max(1, used // 4)
        shifted = fixed + (places - fixed + offset_by * (used - fixed)) % max(1, amount - fixed)
        return jnp.zeros((amount,), jnp.int32).at[sequence[jnp.where(places < fixed, places, shifted)]].set(jnp.asarray(lengths, jnp.int32))

    lengths = jnp.where(number % 4 == 0, named(packed, number // 4), named(ordinary, number - number // 4 - 1))
    mixed = jax.random.permutation(jax.random.fold_in(own, 3), amount)
    source_of, receiver = mixed[0:amount // 2 * 2:2], mixed[1:amount // 2 * 2:2]
    room = jnp.minimum(lengths[source_of] - 1, bound - lengths[receiver]) // 2
    room = jnp.where((source_of == sequence[0]) | (receiver == sequence[0]) | (lengths[receiver] == 0), 0, jnp.maximum(room, 0))
    shifted = jax.random.randint(jax.random.fold_in(own, 4), (amount // 2,), 0, 1 << 20) % (room + 1)
    lengths = lengths.at[source_of].add(-shifted).at[receiver].add(shifted)
    labels = jnp.searchsorted(jnp.cumsum(lengths), jnp.arange(rows * top), side="right").astype(jnp.int32)
    listing = labels.reshape(top, rows).T
    listing = listing[jax.random.permutation(jax.random.fold_in(own, 1), rows)]
    offset_by = jax.random.randint(jax.random.fold_in(own, 2), (rows, 1), 0, top)
    return jnp.take_along_axis(listing, (jnp.arange(top)[None, :] + offset_by) % top, axis=1)


def portions_of(count, total, reach, lean, full):
    portions = [(1 << 20) // math.isqrt(grade ** lean) + 1 for grade in range(1, count + 1)]
    largest = reach if full else min(reach, max(-(-total // count), total * portions[0] // sum(portions)))
    least = 1 if total - largest >= count - 1 else 0
    holding, surplus = [largest] + [least] * (count - 1), total - largest - least * (count - 1)
    while surplus > 0:
        free = [i for i in range(1, count) if holding[i] < largest] or [i for i in range(1, count) if holding[i] < reach]
        mass, budget = sum([portions[i] for i in free]), surplus
        for i in free:
            extra = min(reach - holding[i], max(1, budget * portions[i] // mass), surplus)
            holding[i] = holding[i] + extra
            surplus = surplus - extra
    return np.array(holding)


def gaussian(stream_key, extent, spread, limit, pieces=(), kind=jnp.bfloat16):
    factor_of = block_scale(stream_key, extent, pieces, -0.22, 0.18) if pieces else 1.0
    values = jax.random.normal(stream_key, extent, jnp.float32) * spread * factor_of
    return jnp.minimum(jnp.maximum(values, -limit), limit).astype(kind)


def setup_inputs(seed: int = 0) -> dict:
    streams_of = jax.random.split(jax.random.key(seed), 19)
    inputs = gaussian(streams_of[0], (TOKENS, D), 1.0, 6.0, ((0, 32), (1, 4)))
    attention_gain = jnp.clip(1.0 + 0.1 * jax.random.normal(streams_of[1], (D,), jnp.float32), 0.5, 1.5).astype(jnp.bfloat16)
    query_weight = gaussian(streams_of[2], (D, HEADS * (NOPE + ROPE)), D ** -0.5, 0.125, ((0, 4), (1, 4)))
    latent_weight = gaussian(streams_of[3], (D, RANK + ROPE), D ** -0.5, 0.125, ((0, 4),))
    latent_gain = jnp.clip(1.0 + 0.1 * jax.random.normal(streams_of[4], (RANK,), jnp.float32), 0.5, 1.5).astype(jnp.bfloat16)
    expand_weight = gaussian(streams_of[5], (RANK, HEADS * (NOPE + VDIM)), RANK ** -0.5, 0.25, ((1, 16),))
    output_weight = gaussian(streams_of[6], (HEADS * VDIM, D), (HEADS * VDIM // 16) ** -0.5, 0.5, ((0, 4), (1, 4)))
    feedforward_gain = jnp.clip(1.0 + 0.1 * jax.random.normal(streams_of[7], (D,), jnp.float32), 0.5, 1.5).astype(jnp.bfloat16)
    router_weight = gaussian(streams_of[8], (D, EXPERTS), (D // 4) ** -0.5, 0.25, ((0, 4),))
    shared_gate = gaussian(streams_of[9], (D, SFF), D ** -0.5, 0.125, ((0, 4), (1, 4)))
    shared_up = gaussian(streams_of[10], (D, SFF), D ** -0.5, 0.125, ((0, 4), (1, 4)))
    shared_down = gaussian(streams_of[11], (SFF, D), SFF ** -0.5, 0.109375, ((0, 4), (1, 4)))
    expert_gate = gaussian(streams_of[12], (EXPERTS, D, FF), D ** -0.5, 0.125, ((1, 4), (2, 4)))
    expert_up = gaussian(streams_of[13], (EXPERTS, D, FF), D ** -0.5, 0.125, ((1, 4), (2, 4)))
    expert_down = gaussian(streams_of[14], (EXPERTS, FF, D), (FF // 16) ** -0.5, 0.625, ((1, 4), (2, 4)))
    routes_keys = jax.random.split(jax.random.fold_in(streams_of[15], 1), TOKENS // SEQ)
    routes_turns = jax.random.permutation(jax.random.fold_in(streams_of[15], 3), TOKENS // SEQ)
    routes = jax.vmap(lambda own, number: shared_out(jax.random.fold_in(streams_of[15], 2), own, number, SEQ, EXPERTS, TOPK, CAP, 1))(routes_keys, routes_turns).reshape((TOKENS, TOPK))
    prefix = with_ends(jax.random.randint(streams_of[16], (N_DP,), SEQ // 10, SEQ // 2 + 1), jax.random.fold_in(streams_of[16], 1), SEQ // 10, (SEQ // 2 + 1) - 1).astype(jnp.int32)
    cotangent = gaussian(streams_of[17], (TOKENS, D), 1.0, 6.0, ((0, 32), (1, 4)))
    return {"inputs": inputs, "attention_gain": attention_gain, "query_weight": query_weight, "latent_weight": latent_weight, "latent_gain": latent_gain, "expand_weight": expand_weight, "output_weight": output_weight, "feedforward_gain": feedforward_gain, "router_weight": router_weight, "shared_gate": shared_gate, "shared_up": shared_up, "shared_down": shared_down, "expert_gate": expert_gate, "expert_up": expert_up, "expert_down": expert_down, "routes": routes, "prefix": prefix, "cotangent": cotangent}


norm_eps = 1e-06
highest = lax.Precision.HIGHEST
masked_score = -1e+30

@jax.custom_vjp
def low(v):
    return lax.optimization_barrier(v.astype(jnp.bfloat16)).astype(jnp.float32)

@jax.custom_vjp
def low_back(v):
    return v

def low_keep(v):
    return (low(v), None)

def low_pass(kept, grad):
    return (grad,)

def back_keep(v):
    return (v, None)

def back_low(kept, grad):
    return (low(grad),)
low.defvjp(low_keep, low_pass)
low_back.defvjp(back_keep, back_low)

def product(left, right):
    return jnp.dot(left, right, precision=highest, preferred_element_type=jnp.float32)

def rms_norm(values, gain_row):
    return values * lax.rsqrt(lax.optimization_barrier(jnp.mean(values * values, axis=-1, keepdims=True)) + norm_eps) * gain_row

def rotary_tables(length, half_width):
    position = jnp.arange(length, dtype=jnp.float32)[:, None]
    frequency = jnp.exp(jnp.arange(half_width, dtype=jnp.float32) * (-math.log(10000.0) / half_width))
    angles = position * frequency[None, :]
    return (jnp.cos(angles), jnp.sin(angles))

def rotate(values, cos_table, sin_table):
    half_width = cos_table.shape[-1]
    first_half = values[..., :half_width]
    second_half = values[..., half_width:]
    return jnp.concatenate([first_half * cos_table - second_half * sin_table, second_half * cos_table + first_half * sin_table], axis=-1)

def dispatch(route_rows):
    pair_count = route_rows.shape[0] * TOPK
    flat_routes = route_rows.reshape(-1).astype(jnp.int32)
    one_hot = (flat_routes[:, None] == jnp.arange(EXPERTS, dtype=jnp.int32)[None, :]).astype(jnp.int32)
    before = (jnp.cumsum(one_hot, axis=0) - one_hot).astype(jnp.int32)
    position = lax.optimization_barrier(jnp.sum(before * one_hot, axis=1)).astype(jnp.int32)
    token_ids = (jnp.arange(pair_count, dtype=jnp.int32) // TOPK).astype(jnp.int32)
    slot_token = jnp.zeros((EXPERTS, CAP), jnp.int32).at[flat_routes, position].set(token_ids)
    filled = jnp.zeros((EXPERTS, CAP), jnp.int32).at[flat_routes, position].set(jnp.ones_like(token_ids))
    return (slot_token, filled)

def attend(queries, key_rows, value_rows, prefix_len):
    block_rows = min(512, SEQ)
    score_scale = (NOPE + ROPE) ** (-0.5)
    key_pos = jnp.arange(SEQ, dtype=jnp.int32)

    def one_block(offset):
        query_block = lax.dynamic_slice_in_dim(queries, offset, block_rows, 0)
        scores = jnp.einsum('bhd,khd->hbk', query_block, key_rows, precision=highest) * score_scale
        scores = low_back(scores)
        query_pos = offset + jnp.arange(block_rows, dtype=jnp.int32)
        visible = (key_pos[None, :] <= query_pos[:, None]) | (key_pos[None, :] < prefix_len)
        scores = jnp.where(visible[None, :, :], scores, masked_score)
        weights = low(jax.nn.softmax(scores, axis=-1))
        return jnp.einsum('hbk,khd->bhd', weights, value_rows, precision=highest)
    starts = jnp.arange(SEQ // block_rows, dtype=jnp.int32) * block_rows
    return lax.map(jax.checkpoint(one_block), starts).reshape(SEQ, HEADS * VDIM)

def block_forward(group_inputs, route_rows, prefix_len, attention_gain, query_weight, latent_weight, latent_gain, expand_weight, output_weight, feedforward_gain, router_weight, shared_gate, shared_up, shared_down, expert_gate, expert_up, expert_down):
    cos_table, sin_table = rotary_tables(SEQ, ROPE // 2)
    normed = low(rms_norm(group_inputs, attention_gain))
    queries = low_back(product(normed, query_weight)).reshape(SEQ, HEADS, NOPE + ROPE)
    latent = low_back(product(normed, latent_weight))
    content = latent[:, :RANK]
    shared_key = low(rotate(latent[:, RANK:], cos_table, sin_table))
    compact = low(rms_norm(content, latent_gain))
    key_value = low(low_back(product(compact, expand_weight))).reshape(SEQ, HEADS, NOPE + VDIM)
    query_rot = low(jnp.concatenate([queries[..., :NOPE], rotate(queries[..., NOPE:], cos_table[:, None, :], sin_table[:, None, :])], axis=-1))
    key_rows = jnp.concatenate([key_value[..., :NOPE], jnp.broadcast_to(shared_key[:, None, :], (SEQ, HEADS, ROPE))], axis=-1)
    attended = low(low_back(attend(query_rot, key_rows, key_value[..., NOPE:], prefix_len)))
    residual = group_inputs + low_back(product(attended, output_weight))
    hidden = low(rms_norm(residual, feedforward_gain))
    router_probs = jax.nn.softmax(product(hidden, router_weight), axis=-1)
    slot_token, filled = dispatch(route_rows)
    slot_fill = filled.astype(jnp.float32)
    slot_weight = router_probs[slot_token, jnp.arange(EXPERTS, dtype=jnp.int32)[:, None]] * slot_fill
    slot_rows = hidden[slot_token] * slot_fill[:, :, None]
    gate_pre = low_back(jnp.einsum('ecd,edf->ecf', slot_rows, expert_gate, precision=highest))
    up_pre = low_back(jnp.einsum('ecd,edf->ecf', slot_rows, expert_up, precision=highest))
    expert_act = low(slot_weight[:, :, None] * jax.nn.silu(gate_pre) * up_pre)
    expert_out = jnp.einsum('ecf,efd->ecd', expert_act, expert_down, precision=highest)
    routed = jnp.zeros((SEQ, D), jnp.float32).at[slot_token.reshape(-1)].add(expert_out.reshape(-1, D))
    shared_gate_pre = low_back(product(hidden, shared_gate))
    shared_up_pre = low_back(product(hidden, shared_up))
    shared_act = low(jax.nn.silu(shared_gate_pre) * shared_up_pre)
    return residual + product(shared_act, shared_down) + routed

def reference(inputs, attention_gain, query_weight, latent_weight, latent_gain, expand_weight, output_weight, feedforward_gain, router_weight, shared_gate, shared_up, shared_down, expert_gate, expert_up, expert_down, routes, prefix, cotangent):
    floats = tuple((array.astype(jnp.float32) for array in (inputs, attention_gain, query_weight, latent_weight, latent_gain, expand_weight, output_weight, feedforward_gain, router_weight, shared_gate, shared_up, shared_down, expert_gate, expert_up, expert_down)))
    route_groups = routes.reshape(N_DP, SEQ, TOPK)

    def forward(*weights):
        input_groups = weights[0].reshape(N_DP, SEQ, D)

        def group_step(running, group_item):
            result = jax.checkpoint(block_forward)(group_item[0], group_item[1], group_item[2], *weights[1:])
            return (running, result)
        unused, output_groups = lax.scan(group_step, jnp.zeros((), jnp.float32), (input_groups, route_groups, prefix))
        return output_groups.reshape(N_DP * SEQ, D)
    output, pullback = jax.vjp(forward, *floats)
    gradients = pullback(cotangent.astype(jnp.float32))
    return (output.astype(jnp.bfloat16), gradients[0].astype(jnp.bfloat16), gradients[1], gradients[2], gradients[3], gradients[4], gradients[5], gradients[6], gradients[7], gradients[8], gradients[9], gradients[10], gradients[11], gradients[12], gradients[13], gradients[14])
```

```python
import math

import jax
import jax.numpy as jnp
from jax import lax
from jax.experimental import pallas as pl
from jax.experimental.pallas import tpu as pltpu
from jax.sharding import PartitionSpec as P

D = 2048
NOPE = 128
ROPE = 64
VDIM = 128
RANK = 512
TOPK = 6
EXPERTS = 8
SEQ = 1024

norm_eps = 1e-06
masked_score = -1e30
bf16 = jnp.bfloat16
f32 = jnp.float32
MESH = pl.DeviceIdType.MESH
DMA = pltpu.SemaphoreType.DMA
VMEM = pl.BlockSpec(memory_space=pltpu.VMEM)


def place():
    row = lax.axis_index("row")
    col = lax.axis_index("col")
    sibling = col + 1 - 2 * lax.rem(col, 2)
    across = lax.rem(col + 2, 4)
    return (row, sibling, across)


def greet(row, sibling, across):
    barrier = pltpu.get_barrier_semaphore()
    pl.semaphore_signal(barrier, inc=1, device_id={"col": sibling}, device_id_type=MESH)
    pl.semaphore_signal(barrier, inc=1, device_id={"col": across}, device_id_type=MESH)
    for step in (1, 2, 3):
        pl.semaphore_signal(
            barrier, inc=1, device_id={"row": lax.rem(row + step, 4)}, device_id_type=MESH
        )
    pl.semaphore_wait(barrier, 5)


def starter(pending):
    def go(source, target, send_sem, recv_sem, **device):
        copy = pltpu.make_async_remote_copy(
            src_ref=source,
            dst_ref=target,
            send_sem=send_sem,
            recv_sem=recv_sem,
            device_id=device,
            device_id_type=MESH,
        )
        copy.start()
        pending.append(copy)
        return copy

    return go


def gather_kernel(own, full, xs, xr, ys, yr, cs, cr):
    row, sibling, across = place()
    rows, columns = own.shape
    greet(row, sibling, across)
    pending = []
    go = starter(pending)

    def block(at_row, at_col):
        start = pl.multiple_of(at_row * rows, rows)
        return full.at[pl.ds(start, rows), pl.ds(at_col * columns, columns)]

    side = go(own, block(row, 2), xs, xr, col=across)
    first = [
        go(own, block(row, 0), ys.at[k - 1], yr.at[k - 1], row=lax.rem(row + k, 4))
        for k in (1, 2, 3)
    ]
    arrivals = [go(own, block(row, 1), cs.at[0], cr.at[0], col=sibling)]
    full[pl.ds(pl.multiple_of(row * rows, rows), rows), pl.ds(0, columns)] = own[...]
    side.wait_recv()
    second = [
        go(block(row, 2), block(row, 2), ys.at[2 + k], yr.at[2 + k], row=lax.rem(row + k, 4))
        for k in (1, 2, 3)
    ]
    arrivals.append(go(block(row, 2), block(row, 3), cs.at[1], cr.at[1], col=sibling))
    count = 2
    for group, at_col in ((first, 0), (second, 2)):
        for k in (1, 3, 2):
            group[k - 1].wait_recv()
            source = lax.rem(row + 4 - k, 4)
            arrivals.append(
                go(
                    block(source, at_col),
                    block(source, at_col + 1),
                    cs.at[count],
                    cr.at[count],
                    col=sibling,
                )
            )
            count += 1
    for copy in arrivals:
        copy.wait_recv()
    for copy in pending:
        copy.wait_send()


def gather_grid(own, collective):
    rows, columns = own.shape
    return pl.pallas_call(
        gather_kernel,
        out_shape=jax.ShapeDtypeStruct((4 * rows, 4 * columns), own.dtype),
        in_specs=[VMEM],
        out_specs=VMEM,
        scratch_shapes=[DMA, DMA, DMA((6,)), DMA((6,)), DMA((8,)), DMA((8,))],
        compiler_params=pltpu.CompilerParams(
            collective_id=collective, has_side_effects=True, vmem_limit_bytes=40 << 20
        ),
        cost_estimate=pl.CostEstimate(flops=0, bytes_accessed=80 << 20, transcendentals=0),
        name="gather_grid",
    )(own)


def reduce_kernel(part, total, held, out_buf, in_buf, acc, sx, rx, xs, xr, ys, yr, cs, cr):
    row, sibling, across = place()
    rows, columns = total.shape
    greet(row, sibling, across)
    pending = []
    go = starter(pending)

    def rows_of(k):
        return pl.ds(pl.multiple_of(lax.rem(row + k, 4) * rows, rows), rows)

    order = (2, 1, 3, 0)
    paired = {}
    for k in order:
        for x in (0, 1):
            paired[k, x] = go(
                part.at[rows_of(k), pl.ds((2 * x + 1) * columns, columns)],
                held.at[k, x],
                cs.at[k, x],
                cr.at[k, x],
                col=sibling,
            )
    along = {}
    for k in order:
        for x in (0, 1):
            paired[k, x].wait_recv()
            mine = part[rows_of(k), pl.ds(2 * x * columns, columns)]
            value = mine.astype(f32) + held[k, x].astype(f32)
            if k:
                out_buf[k - 1, x] = value.astype(bf16)
                along[k, x] = go(
                    out_buf.at[k - 1, x],
                    in_buf.at[k - 1, x],
                    ys.at[k - 1, x],
                    yr.at[k - 1, x],
                    row=lax.rem(row + k, 4),
                )
            else:
                acc[x] = value
    for x in (1, 0):
        for k in (1, 3, 2):
            along[k, x].wait_recv()
            acc[x] += in_buf[k - 1, x].astype(f32)
        if x:
            sx[...] = acc[1].astype(bf16)
            side = go(sx, rx, xs, xr, col=across)
    side.wait_recv()
    total[...] = acc[0] + rx[...].astype(f32)
    for copy in pending:
        copy.wait_send()


def reduce_grid(part, collective):
    rows, columns = part.shape[0] // 4, part.shape[1] // 4
    return pl.pallas_call(
        reduce_kernel,
        out_shape=jax.ShapeDtypeStruct((rows, columns), f32),
        in_specs=[VMEM],
        out_specs=VMEM,
        scratch_shapes=[
            pltpu.VMEM((4, 2, rows, columns), bf16),
            pltpu.VMEM((3, 2, rows, columns), bf16),
            pltpu.VMEM((3, 2, rows, columns), bf16),
            pltpu.VMEM((2, rows, columns), f32),
            pltpu.VMEM((rows, columns), bf16),
            pltpu.VMEM((rows, columns), bf16),
            DMA,
            DMA,
            DMA((3, 2)),
            DMA((3, 2)),
            DMA((4, 2)),
            DMA((4, 2)),
        ],
        compiler_params=pltpu.CompilerParams(
            collective_id=collective, has_side_effects=True, vmem_limit_bytes=40 << 20
        ),
        cost_estimate=pl.CostEstimate(flops=0, bytes_accessed=100 << 20, transcendentals=0),
        name="reduce_grid",
    )(part)


def dot(spec, left, right, kind=f32):
    return jnp.einsum(spec, left, right, preferred_element_type=f32).astype(kind)


def rotary_tables(length, half_width):
    position = jnp.arange(length, dtype=f32)[:, None]
    frequency = jnp.exp(jnp.arange(half_width, dtype=f32) * (-math.log(10000.0) / half_width))
    angles = position * frequency[None, :]
    return (jnp.cos(angles), jnp.sin(angles))


def rotate(values, cos_table, sin_table):
    half_width = cos_table.shape[-1]
    first_half = values[..., :half_width]
    second_half = values[..., half_width:]
    return jnp.concatenate(
        [
            first_half * cos_table - second_half * sin_table,
            second_half * cos_table + first_half * sin_table,
        ],
        axis=-1,
    )


def swap_chips(values, distance, other_replica):
    flip = 4 if other_replica else 0
    pairs = [
        (dp * 4 + col, (dp ^ flip) * 4 + (col ^ distance)) for dp in range(8) for col in range(4)
    ]
    return lax.ppermute(values, ("dp", "col"), pairs)


def deal(pieces):
    got = [pieces(0)]
    for k in (1, 2, 3):
        piece = pieces(k)
        if k == 1:
            got.append(swap_chips(piece, k, False))
        else:
            half = piece.shape[0] // 2
            got.append(
                jnp.concatenate(
                    [swap_chips(piece[:half], k, False), swap_chips(piece[half:], k, True)], axis=0
                )
            )
    return got


def pad_to(values, axis, size):
    widths = [(0, 0)] * values.ndim
    widths[axis] = (0, size - values.shape[axis])
    return jnp.pad(values, widths)


def visible_mask(offset, block_rows, prefix_len):
    query_pos = offset + jnp.arange(block_rows, dtype=jnp.int32)
    key_pos = jnp.arange(SEQ, dtype=jnp.int32)
    return (key_pos[None, :] <= query_pos[:, None]) | (key_pos[None, :] < prefix_len)


def attend_forward(queries, key_rows, value_rows, prefix_len):
    score_scale = (NOPE + ROPE) ** (-0.5)
    scores = dot("qd,kd->qk", queries, key_rows) * score_scale
    scores = jnp.where(visible_mask(0, SEQ, prefix_len), scores, masked_score)
    top_score = jnp.max(scores, axis=1, keepdims=True)
    exp_scores = jnp.exp(scores - top_score)
    row_total = jnp.sum(exp_scores, axis=1, keepdims=True)
    weights = (exp_scores / row_total).astype(bf16)
    result = dot("qk,kd->qd", weights, value_rows)
    return (result, (top_score + jnp.log(row_total))[:, 0])


def attend_backward(queries, key_rows, value_rows, log_total, out_grad, prefix_len):
    score_scale = (NOPE + ROPE) ** (-0.5)
    scores = dot("qd,kd->qk", queries, key_rows) * score_scale
    scores = jnp.where(visible_mask(0, SEQ, prefix_len), scores, masked_score)
    weights = jnp.exp(scores - log_total[:, None])
    value_grad = dot("qk,qd->kd", weights.astype(bf16), out_grad)
    weight_grad = dot("qd,kd->qk", out_grad, value_rows)
    centre = jnp.sum(weights * weight_grad, axis=1, keepdims=True)
    score_grad = (weights * (weight_grad - centre)).astype(bf16)
    query_grad = dot("qk,kd->qd", score_grad, key_rows) * score_scale
    key_grad = dot("qk,qd->kd", score_grad, queries) * score_scale
    return (query_grad, key_grad, value_grad)


def norm_back(values, gain_row, scale_row, upstream):
    weighted = upstream * gain_row[None, :]
    inner_sum = lax.psum(jnp.sum(weighted * values, axis=1), "col")
    value_grad = (
        scale_row[:, None] * weighted
        - values * (scale_row * scale_row * scale_row * inner_sum / D)[:, None]
    )
    gain_grad = jnp.sum(upstream * values * scale_row[:, None], axis=0)
    return (value_grad, gain_grad)


def sigmoid(value):
    return jax.nn.sigmoid(value)


def on_device(
    inputs,
    attention_gain,
    query_weight,
    latent_weight,
    latent_gain,
    expand_weight,
    output_weight,
    feedforward_gain,
    router_weight,
    shared_gate,
    shared_up,
    shared_down,
    expert_gate,
    expert_up,
    expert_down,
    routes,
    prefix,
    cotangent,
):
    row = lax.axis_index("row")
    col = lax.axis_index("col")
    prefix_len = prefix[0]
    cos_table, sin_table = rotary_tables(SEQ, ROPE // 2)
    first_gain = attention_gain.astype(f32)
    second_gain = feedforward_gain.astype(f32)
    compact_gain = latent_gain.astype(f32)
    residual_in = inputs.astype(f32)
    rows = inputs.shape[0]
    ff = expert_gate.shape[2]
    ff_pad = -(-ff // 128) * 128
    sff = shared_gate.shape[1] // 4
    sff_pad = 256

    gains = jnp.stack([attention_gain, feedforward_gain], axis=1)
    common = pad_to(jnp.concatenate([latent_weight[:, RANK:], router_weight, gains], axis=1), 1, 192)
    heads = query_weight.reshape(512, 4, NOPE + ROPE)

    def attention_piece(k):
        head = lax.dynamic_index_in_dim(heads, col ^ k, 1, False)
        return jnp.concatenate([latent_weight[:, :RANK], head, common], axis=1)

    attention_weights = jnp.concatenate(deal(attention_piece), axis=0)
    first_all = attention_weights[:, RANK + 256 + 8]
    second_all = attention_weights[:, RANK + 256 + 9]
    project_weight = attention_weights[:, : RANK + 256]

    gate_parts = expert_gate.reshape(4, 2, 512, ff)
    up_parts = expert_up.reshape(4, 2, 512, ff)
    down_parts = expert_down.reshape(4, 2, ff, 512)
    shared_gate_parts = shared_gate.reshape(512, 4, sff)
    shared_up_parts = shared_up.reshape(512, 4, sff)
    shared_down_parts = shared_down.reshape(4, sff, 512)

    def up_piece(k):
        gate = lax.dynamic_index_in_dim(gate_parts, col ^ k, 0, False)
        up = lax.dynamic_index_in_dim(up_parts, col ^ k, 0, False)
        return jnp.concatenate([pad_to(gate, 2, ff_pad), pad_to(up, 2, ff_pad)], axis=2)

    def down_piece(k):
        down = pad_to(lax.dynamic_index_in_dim(down_parts, col ^ k, 0, False), 1, ff_pad)
        low = pad_to(lax.dynamic_index_in_dim(shared_down_parts, col ^ k, 0, False), 0, sff_pad)
        gate = lax.dynamic_index_in_dim(shared_gate_parts, col ^ k, 1, False)
        up = lax.dynamic_index_in_dim(shared_up_parts, col ^ k, 1, False)
        both = jnp.concatenate(
            [pad_to(jnp.concatenate([gate, router_weight], axis=1), 1, sff_pad), pad_to(up, 1, sff_pad)],
            axis=1,
        )
        return jnp.concatenate([down.reshape(2 * ff_pad, 512), low, both], axis=0)

    up_weight = jnp.concatenate(deal(up_piece), axis=1)
    down_got = deal(down_piece)
    down_weight = jnp.concatenate(
        [piece[: 2 * ff_pad].reshape(2, ff_pad, 512) for piece in down_got], axis=2
    )
    shared_down_weight = jnp.concatenate(
        [piece[2 * ff_pad : 2 * ff_pad + sff_pad] for piece in down_got], axis=1
    )
    shared_up_weight = jnp.concatenate([piece[2 * ff_pad + sff_pad :] for piece in down_got], axis=0)

    input_rows = gather_grid(inputs, 0).astype(f32)
    scale_one = lax.rsqrt(jnp.mean(input_rows * input_rows, axis=1) + norm_eps)
    normed = (input_rows * scale_one[:, None] * first_all.astype(f32)[None, :]).astype(bf16)
    projected = dot("td,dq->tq", normed, project_weight)
    content = projected[:, :RANK]
    latent_scale = lax.rsqrt(jnp.mean(content * content, axis=1) + norm_eps)
    compact = (content * latent_scale[:, None] * compact_gain[None, :]).astype(bf16)
    shared_key = rotate(projected[:, RANK + 192 :], cos_table, sin_table).astype(bf16)
    key_value = dot("tr,rk->tk", compact, expand_weight, bf16)
    query_rot = jnp.concatenate(
        [
            projected[:, RANK : RANK + NOPE],
            rotate(projected[:, RANK + NOPE : RANK + 192], cos_table, sin_table),
        ],
        axis=1,
    ).astype(bf16)
    key_rows = jnp.concatenate([key_value[:, :NOPE], shared_key], axis=1)
    value_rows = key_value[:, NOPE:]
    head_result, log_total = attend_forward(query_rot, key_rows, value_rows, prefix_len)
    attended_rows = lax.all_gather(head_result.astype(bf16), "col", axis=1, tiled=True)
    residual_mid = residual_in + lax.psum_scatter(
        dot("th,hd->td", attended_rows, output_weight, bf16), "row", scatter_dimension=0, tiled=True
    ).astype(f32)

    middle_rows = gather_grid(residual_mid.astype(bf16), 0).astype(f32)
    scale_two = lax.rsqrt(jnp.mean(middle_rows * middle_rows, axis=1) + norm_eps)
    hidden = (middle_rows * scale_two[:, None] * second_all.astype(f32)[None, :]).astype(bf16)
    out_grad = gather_grid(cotangent, 0)
    named = jnp.any(
        routes[:, :, None] == jnp.arange(EXPERTS, dtype=jnp.int32)[None, None, :], axis=1
    ).astype(f32)
    shared_pre = dot("td,df->tf", hidden, shared_up_weight)
    router_probs = jax.nn.softmax(shared_pre[:, sff : sff + EXPERTS], axis=1)
    weight_all = router_probs * named
    mine = (
        2 * col + jnp.arange(2, dtype=jnp.int32)[:, None]
        == jnp.arange(EXPERTS, dtype=jnp.int32)[None, :]
    ).astype(f32)
    slot_weight = jnp.sum(weight_all[None] * mine[:, None, :], axis=2)[:, :, None]
    pre = dot("td,edf->etf", hidden, up_weight)
    gate_pre, up_pre = pre[:, :, :ff_pad], pre[:, :, ff_pad:]
    gate_sig = sigmoid(gate_pre)
    gate_silu = gate_pre * gate_sig
    act = (slot_weight * gate_silu * up_pre).astype(bf16)
    shared_gate_pre, shared_up_pre = shared_pre[:, :sff_pad], shared_pre[:, sff_pad:]
    shared_sig = sigmoid(shared_gate_pre)
    shared_silu = shared_gate_pre * shared_sig
    shared_act = (shared_silu * shared_up_pre).astype(bf16)
    combined = dot("etf,efd->td", act, down_weight) + dot(
        "tf,fd->td", shared_act, shared_down_weight
    )
    output = (residual_mid + reduce_grid(combined.astype(bf16), 1)).astype(bf16)
    act_grad = dot("td,efd->etf", out_grad, down_weight)
    shared_act_grad = dot("td,fd->tf", out_grad, shared_down_weight)
    weighted = slot_weight * act_grad
    gate_delta = weighted * up_pre * (gate_sig * (1.0 + gate_pre * (1.0 - gate_sig)))
    up_delta = weighted * gate_silu
    delta = jnp.concatenate([gate_delta, up_delta], axis=2).astype(bf16)
    probs_part = jnp.sum(act_grad * gate_silu * up_pre, axis=2)
    probs_part = jnp.sum(probs_part[:, :, None] * mine[:, None, :], axis=0) * named
    logits_part = router_probs * (
        probs_part - jnp.sum(router_probs * probs_part, axis=1, keepdims=True)
    )
    shared_gate_delta = (
        shared_act_grad
        * shared_up_pre
        * (shared_sig * (1.0 + shared_gate_pre * (1.0 - shared_sig)))
    )
    shared_delta = jnp.concatenate(
        [
            shared_gate_delta[:, :sff],
            logits_part,
            shared_gate_delta[:, sff + EXPERTS :],
            shared_act_grad * shared_silu,
        ],
        axis=1,
    ).astype(bf16)
    hidden_grad = dot("etf,edf->td", delta, up_weight) + dot(
        "tf,df->td", shared_delta, shared_up_weight
    )
    hidden_sum = reduce_grid(hidden_grad.astype(bf16), 1)
    up_grad = dot("td,etf->edf", hidden, delta, bf16)
    down_grad = dot("td,etf->edf", out_grad, act, bf16)
    expert_grad = jnp.concatenate([up_grad, down_grad], axis=2).reshape(8, 512, 3 * ff_pad)
    shared_grad = jnp.concatenate(
        [
            dot("td,tf->df", hidden, shared_delta),
            dot("td,tf->df", out_grad, shared_act),
        ],
        axis=1,
    )

    my_scale_one = lax.dynamic_slice_in_dim(scale_one, row * rows, rows, 0)
    my_scale_two = lax.dynamic_slice_in_dim(scale_two, row * rows, rows, 0)
    mid_norm_grad, second_gain_part = norm_back(residual_mid, second_gain, my_scale_two, hidden_sum)
    residual_grad = cotangent.astype(f32) + mid_norm_grad
    residual_rows = lax.all_gather(residual_grad.astype(bf16), "row", axis=0, tiled=True)
    output_weight_grad = dot("th,td->hd", attended_rows, residual_rows, bf16)
    attended_grad = lax.psum_scatter(
        dot("td,hd->th", residual_rows, output_weight, bf16),
        "col",
        scatter_dimension=1,
        tiled=True,
    )
    query_rot_grad, key_grad, value_grad = attend_backward(
        query_rot, key_rows, value_rows, log_total, attended_grad, prefix_len
    )
    pair_grad = jnp.concatenate([key_grad[:, :NOPE], value_grad], axis=1).astype(bf16)
    expand_grad = dot("tr,tk->rk", compact, pair_grad, bf16)
    compact_grad = dot("tk,rk->tr", pair_grad, expand_weight)
    weighted_compact = compact_grad * compact_gain[None, :]
    inner_sum = jnp.sum(weighted_compact * content, axis=1)
    content_grad = (
        latent_scale[:, None] * weighted_compact
        - content * (latent_scale * latent_scale * latent_scale * inner_sum / RANK)[:, None]
    )
    latent_gain_part = jnp.sum(compact_grad * content * latent_scale[:, None], axis=0)
    project_grad = jnp.concatenate(
        [
            content_grad,
            query_rot_grad[:, :NOPE],
            rotate(query_rot_grad[:, NOPE:], cos_table, -sin_table),
            rotate(key_grad[:, NOPE:], cos_table, -sin_table),
        ],
        axis=1,
    ).astype(bf16)
    latent_part = jnp.concatenate([project_grad[:, :RANK], project_grad[:, RANK + 192 :]], axis=1)
    normed_grad = dot("tq,dq->td", project_grad, project_weight, bf16)
    latent_weight_part = dot("tl,td->ld", latent_part, normed, bf16)
    tail = jnp.concatenate(
        [normed_grad.reshape(4, rows, D), latent_weight_part.reshape(4, -1, D)], axis=1
    )
    tail_rows = tail.shape[1]
    tail_sum = reduce_grid(tail.reshape(4 * tail_rows, D), 2)
    input_norm_grad, first_gain_part = norm_back(
        residual_in, first_gain, my_scale_one, tail_sum[:rows]
    )
    inputs_grad = (residual_grad + input_norm_grad).astype(bf16)
    query_rows = lax.all_gather(project_grad[:, RANK : RANK + 192], "col", axis=1, tiled=True)
    query_weight_grad = dot("td,tq->dq", normed[:, :512], query_rows, bf16)

    expert_sum = lax.psum_scatter(expert_grad, "dp", scatter_dimension=0, tiled=True)[0]
    pairs = [
        (dp * 4 + c, (2 * c + dp // 4) * 4 + (c ^ (dp % 4))) for dp in range(8) for c in range(4)
    ]
    expert_sum = lax.ppermute(expert_sum, ("dp", "col"), pairs).astype(f32)
    expert_gate_grad = expert_sum[None, :, :ff]
    expert_up_grad = expert_sum[None, :, ff_pad : ff_pad + ff]
    expert_down_grad = expert_sum[None, :, 2 * ff_pad : 2 * ff_pad + ff].transpose(0, 2, 1)

    order = col ^ jnp.arange(4, dtype=jnp.int32)
    router_part = shared_grad[:, sff : sff + EXPERTS].reshape(4, 512, EXPERTS)[order]
    small = lax.psum(
        jnp.concatenate([router_part.reshape(-1), latent_gain_part]), ("dp", "row", "col")
    )
    router_grad = lax.dynamic_index_in_dim(
        small[: D * EXPERTS].reshape(4, 512, EXPERTS), col, 0, False
    )
    latent_gain_grad = small[D * EXPERTS :]
    shared_sum = lax.psum(shared_grad.astype(bf16), "dp").reshape(4, 512, 3 * sff_pad)
    shared_got = jnp.stack(
        [shared_sum[0]] + [swap_chips(shared_sum[k], k, False) for k in (1, 2, 3)]
    )[order].astype(f32)
    shared_gate_grad = shared_got[:, :, :sff].transpose(1, 0, 2).reshape(512, 4 * sff)
    shared_up_grad = (
        shared_got[:, :, sff_pad : sff_pad + sff].transpose(1, 0, 2).reshape(512, 4 * sff)
    )
    shared_down_grad = (
        shared_got[:, :, 2 * sff_pad : 2 * sff_pad + sff].transpose(0, 2, 1).reshape(4 * sff, 512)
    )
    summed = lax.psum(
        jnp.concatenate(
            [
                query_weight_grad.reshape(-1, 512),
                expand_grad.reshape(-1, 512),
                output_weight_grad,
                tail_sum[rows:].astype(bf16),
            ],
            axis=0,
        ),
        "dp",
    )
    query_weight_grad = summed[:768].reshape(512, 768).astype(f32)
    expand_grad = summed[768:1024].reshape(512, 256).astype(f32)
    output_weight_grad = summed[1024:1536].astype(f32)
    latent_weight_grad = (
        lax.all_gather(summed[1536:], "row", axis=0, tiled=True).transpose(1, 0).astype(f32)
    )
    first_gain_grad, second_gain_grad = lax.psum((first_gain_part, second_gain_part), ("dp", "row"))
    return (
        output,
        inputs_grad,
        first_gain_grad,
        query_weight_grad,
        latent_weight_grad,
        latent_gain_grad,
        expand_grad,
        output_weight_grad,
        second_gain_grad,
        router_grad,
        shared_gate_grad,
        shared_up_grad,
        shared_down_grad,
        expert_gate_grad,
        expert_up_grad,
        expert_down_grad,
    )


def solution(mesh):
    placed = (
        P(("dp", "row"), "col"),
        P("col"),
        P("col", "row"),
        P("col", None),
        P(),
        P(None, ("row", "col")),
        P("row", "col"),
        P("col"),
        P("col", None),
        P("col", "row"),
        P("col", "row"),
        P("row", "col"),
        P(None, "col", "row"),
        P(None, "col", "row"),
        P(None, "row", "col"),
        P("dp", None),
        P("dp"),
        P(("dp", "row"), "col"),
    )
    return jax.shard_map(
        on_device,
        mesh=mesh,
        in_specs=placed,
        out_specs=(
            P(("dp", "row"), "col"),
            P(("dp", "row"), "col"),
            P("col"),
            P("col", "row"),
            P("col", None),
            P(),
            P(None, ("row", "col")),
            P("row", "col"),
            P("col"),
            P("col", None),
            P("col", "row"),
            P("col", "row"),
            P("row", "col"),
            P("dp", "col", "row"),
            P("dp", "col", "row"),
            P("dp", "row", "col"),
        ),
        check_vma=False,
    )
```

```python
import functools
import math

import jax
import jax.numpy as jnp
from jax import lax
from jax.experimental import pallas as pl
from jax.experimental.pallas import tpu as pltpu
from jax.sharding import PartitionSpec as P

D = 2048
NOPE = 128
ROPE = 64
VDIM = 128
RANK = 512
TOPK = 6
EXPERTS = 8
SEQ = 1024

norm_eps = 1e-06
masked_score = -1e30
bf16 = jnp.bfloat16
f32 = jnp.float32
MESH = pl.DeviceIdType.MESH
DMA = pltpu.SemaphoreType.DMA
VMEM = pl.BlockSpec(memory_space=pltpu.VMEM)


def place():
    row = lax.axis_index("row")
    col = lax.axis_index("col")
    sibling = col + 1 - 2 * lax.rem(col, 2)
    across = lax.rem(col + 2, 4)
    return (row, sibling, across, lax.rem(sibling + 2, 4))


def greet(columns, row, over_dp=False):
    barrier = pltpu.get_barrier_semaphore()
    count = 3 + len(columns)
    for column in columns:
        pl.semaphore_signal(barrier, inc=1, device_id={"col": column}, device_id_type=MESH)
    for step in (1, 2, 3):
        pl.semaphore_signal(
            barrier, inc=1, device_id={"row": lax.rem(row + step, 4)}, device_id_type=MESH
        )
    if over_dp:
        dp = lax.axis_index("dp")
        count += 7
        for step in range(1, 8):
            pl.semaphore_signal(
                barrier, inc=1, device_id={"dp": lax.rem(dp + step, 8)}, device_id_type=MESH
            )
    pl.semaphore_wait(barrier, count)


def starter(pending):
    def go(source, target, sems, at, **device):
        copy = pltpu.make_async_remote_copy(
            src_ref=source,
            dst_ref=target,
            send_sem=sems[0].at[at],
            recv_sem=sems[1].at[at],
            device_id=device,
            device_id_type=MESH,
        )
        copy.start()
        pending.append(copy)
        return copy

    return go


def pair(*shape):
    return [DMA(shape), DMA(shape)]


def params(collective):
    return pltpu.CompilerParams(
        collective_id=collective, has_side_effects=True, vmem_limit_bytes=52 << 20
    )


def cost(flops, mebibytes):
    return pl.CostEstimate(flops=flops, bytes_accessed=mebibytes << 20, transcendentals=0)


def gather_steps(own, full, go, xs, ys, cs, row, sibling, across):
    rows, columns = own.shape

    def block(at_row, at_col):
        start = pl.multiple_of(at_row * rows, rows)
        return full.at[pl.ds(start, rows), pl.ds(at_col * columns, columns)]

    side = go(own, block(row, 2), xs, 0, col=across)
    first = [go(own, block(row, 0), ys, k - 1, row=lax.rem(row + k, 4)) for k in (1, 2, 3)]
    arrivals = [go(own, block(row, 1), cs, 0, col=sibling)]
    full[pl.ds(pl.multiple_of(row * rows, rows), rows), pl.ds(0, columns)] = own[...]
    side.wait_recv()
    second = [
        go(block(row, 2), block(row, 2), ys, 2 + k, row=lax.rem(row + k, 4)) for k in (1, 2, 3)
    ]
    arrivals.append(go(block(row, 2), block(row, 3), cs, 1, col=sibling))
    count = 2
    for group, at_col in ((first, 0), (second, 2)):
        for k in (1, 3, 2):
            group[k - 1].wait_recv()
            source = lax.rem(row + 4 - k, 4)
            arrivals.append(
                go(block(source, at_col), block(source, at_col + 1), cs, count, col=sibling)
            )
            count += 1
    for copy in arrivals:
        copy.wait_recv()


gather_scratch = pair(1) + pair(6) + pair(8)


def gather_kernel(own, full, *sems):
    row, sibling, across, corner = place()
    greet((sibling, across), row)
    pending = []
    gather_steps(
        own, full, starter(pending), sems[0:2], sems[2:4], sems[4:6], row, sibling, across
    )
    for copy in pending:
        copy.wait_send()


def gather_grid(own, collective):
    rows, columns = own.shape
    return pl.pallas_call(
        gather_kernel,
        out_shape=jax.ShapeDtypeStruct((4 * rows, 4 * columns), own.dtype),
        in_specs=[VMEM],
        out_specs=VMEM,
        scratch_shapes=gather_scratch,
        compiler_params=params(collective),
        cost_estimate=cost(0, 80),
        name="gather_grid",
    )(own)


def reduce_scratch(rows, columns):
    return [
        pltpu.VMEM((4, 2, rows, columns), bf16),
        pltpu.VMEM((3, 2, rows, columns), bf16),
        pltpu.VMEM((3, 2, rows, columns), bf16),
        pltpu.VMEM((2, rows, columns), f32),
        pltpu.VMEM((2, rows, columns), bf16),
        *pair(1),
        *pair(3, 2),
        *pair(4, 2),
    ]


class Reduction:
    order = (2, 1, 3, 0)

    def __init__(self, part, scratch, go, row, sibling, across):
        self.part, self.go = part, go
        self.held, self.out_buf, self.in_buf, self.acc, self.side_buf = scratch[:5]
        self.xs, self.ys, self.cs = scratch[5:7], scratch[7:9], scratch[9:11]
        self.row, self.sibling, self.across = row, sibling, across
        self.rows, self.columns = self.acc.shape[1:]

    def rows_of(self, k):
        start = lax.rem(self.row + k, 4) * self.rows
        return pl.ds(pl.multiple_of(start, self.rows), self.rows)

    def start(self):
        self.paired = {}
        for k in self.order:
            for x in (0, 1):
                self.paired[k, x] = self.go(
                    self.part.at[self.rows_of(k), pl.ds((2 * x + 1) * self.columns, self.columns)],
                    self.held.at[k, x],
                    self.cs,
                    (k, x),
                    col=self.sibling,
                )

    def along(self):
        self.sent = {}
        for k in self.order:
            for x in (0, 1):
                self.paired[k, x].wait_recv()
                mine = self.part[self.rows_of(k), pl.ds(2 * x * self.columns, self.columns)]
                value = mine.astype(f32) + self.held[k, x].astype(f32)
                if k:
                    self.out_buf[k - 1, x] = value.astype(bf16)
                    self.sent[k, x] = self.go(
                        self.out_buf.at[k - 1, x],
                        self.in_buf.at[k - 1, x],
                        self.ys,
                        (k - 1, x),
                        row=lax.rem(self.row + k, 4),
                    )
                else:
                    self.acc[x] = value

    def side(self):
        for x in (1, 0):
            for k in (1, 3, 2):
                self.sent[k, x].wait_recv()
                self.acc[x] += self.in_buf[k - 1, x].astype(f32)
            if x:
                self.side_buf[0] = self.acc[1].astype(bf16)
                self.last = self.go(
                    self.side_buf.at[0], self.side_buf.at[1], self.xs, 0, col=self.across
                )

    def total(self):
        self.last.wait_recv()
        return self.acc[0] + self.side_buf[1].astype(f32)


def reduce_kernel(part, total, *scratch):
    row, sibling, across, corner = place()
    greet((sibling, across), row)
    pending = []
    steps = Reduction(part, scratch, starter(pending), row, sibling, across)
    steps.start()
    steps.along()
    steps.side()
    total[...] = steps.total()
    for copy in pending:
        copy.wait_send()


def reduce_grid(part, collective):
    rows, columns = part.shape[0] // 4, part.shape[1] // 4
    return pl.pallas_call(
        reduce_kernel,
        out_shape=jax.ShapeDtypeStruct((rows, columns), f32),
        in_specs=[VMEM],
        out_specs=VMEM,
        scratch_shapes=reduce_scratch(rows, columns),
        compiler_params=params(collective),
        cost_estimate=cost(0, 100),
        name="reduce_grid",
    )(part)


class ColumnSum:
    def __init__(self, value, buf, sems, go, peers):
        self.buf, self.own = buf, value
        buf[0] = jnp.broadcast_to(value, buf.shape[1:])
        self.sent = [
            go(buf.at[0], buf.at[k + 1], sems, k, col=peer) for k, peer in enumerate(peers)
        ]

    def total(self):
        for copy in self.sent:
            copy.wait_recv()
        buf = self.buf
        return ((buf[0] + buf[1]) + (buf[2] + buf[3]))[:, :1]


def middle_kernel(
    part, middle, cotangent, scale, gain, weight,
    residual_grad, residual_rows, attended_grad, gain_part,
    sum_buf, out_buf, in_buf, acc, ss, sr, rs, rr, hs, hr, *scratch,
):
    row, sibling, across, corner = place()
    peers = (sibling, across, corner)
    greet(peers, row)
    pending = []
    go = starter(pending)
    steps = Reduction(part, scratch, go, row, sibling, across)
    rows, columns = middle.shape
    head = attended_grad.shape[1]
    steps.start()
    steps.along()
    steps.side()
    upstream = steps.total()
    weighted = upstream * gain[...]
    values = middle[...]
    scales = scale[...]
    inner = ColumnSum(
        jnp.sum(weighted * values, axis=1, keepdims=True), sum_buf, (ss, sr), go, peers
    )
    gain_part[...] = jnp.sum(upstream * values * scales, axis=0, keepdims=True)
    base = cotangent[...].astype(f32) + scales * weighted
    grad = base - values * (scales * scales * scales * inner.total() / D)
    residual_grad[...] = grad

    def block(at_row):
        return pl.ds(pl.multiple_of(at_row * rows, rows), rows)

    residual_rows[block(row), :] = grad.astype(bf16)
    sent = [
        go(
            residual_rows.at[block(row)],
            residual_rows.at[block(row)],
            (rs, rr),
            k - 1,
            row=lax.rem(row + k, 4),
        )
        for k in (1, 2, 3)
    ]
    got = []
    for k in (0, 1, 3, 2):
        source = lax.rem(row + 4 - k, 4)
        if k:
            sent[k - 1].wait_recv()
        product = lax.dot_general(
            residual_rows[block(source), :],
            weight[...],
            (((1,), (1,)), ((), ())),
            preferred_element_type=f32,
        )
        acc[block(source), :] = product[:, :head]
        for j, peer in enumerate(peers):
            out_buf[j, block(source), :] = product[:, (j + 1) * head : (j + 2) * head].astype(bf16)
            got.append(
                (
                    source,
                    j,
                    go(
                        out_buf.at[j, block(source)],
                        in_buf.at[j, block(source)],
                        (hs, hr),
                        (j, k),
                        col=peer,
                    ),
                )
            )
    for source, j, copy in got:
        copy.wait_recv()
    attended_grad[...] = (
        acc[...] + in_buf[0].astype(f32) + in_buf[1].astype(f32) + in_buf[2].astype(f32)
    ).astype(bf16)
    for copy in pending:
        copy.wait_send()


def middle_step(part, middle, cotangent, scale, gain, weight):
    rows, columns = middle.shape
    return pl.pallas_call(
        middle_kernel,
        out_shape=(
            jax.ShapeDtypeStruct((rows, columns), f32),
            jax.ShapeDtypeStruct((4 * rows, columns), bf16),
            jax.ShapeDtypeStruct((4 * rows, VDIM), bf16),
            jax.ShapeDtypeStruct((1, columns), f32),
        ),
        in_specs=[VMEM] * 6,
        out_specs=(VMEM,) * 4,
        scratch_shapes=[
            pltpu.VMEM((4, rows, 128), f32),
            pltpu.VMEM((3, 4 * rows, VDIM), bf16),
            pltpu.VMEM((3, 4 * rows, VDIM), bf16),
            pltpu.VMEM((4 * rows, VDIM), f32),
            *pair(3),
            *pair(3),
            *pair(3, 4),
            *reduce_scratch(rows, columns),
        ],
        compiler_params=params(3),
        cost_estimate=cost(1 << 29, 150),
        name="middle_step",
    )(part, middle, cotangent, scale, gain, weight)


def tail_kernel(
    part, query, ready, residual_grad, inputs, scale, gain, gain_part,
    inputs_grad, sums, narrow, gains, latent_gain,
    chunk_in, all_parts, narrow_all, lat_buf, sum_buf,
    qs, qr, ps, pr, as_, ar, ls, lr, ns, nr, ss, sr, gs, gr, *scratch,
):
    row, sibling, across, corner = place()
    col = lax.axis_index("col")
    dp = lax.axis_index("dp")
    peers = (sibling, across, corner)
    greet(peers, row, over_dp=True)
    pending = []
    go = starter(pending)
    steps = Reduction(part, scratch, go, row, sibling, across)
    rows, columns = inputs.shape
    piece = query.shape[0]
    lat = narrow_all.shape[1]

    def chunk(at):
        return pl.ds(pl.multiple_of(at * piece, piece), piece)

    steps.start()
    dealt = [
        go(
            query.at[:, pl.ds((j + 1) * columns, columns)],
            all_parts.at[chunk(4 + col)],
            (qs, qr),
            j,
            col=peer,
        )
        for j, peer in enumerate(peers)
    ]
    all_parts[pl.ds(0, 4 * piece), :] = ready[...]
    all_parts[chunk(4 + col), :] = query[:, pl.ds(0, columns)]
    steps.along()
    for copy in dealt:
        copy.wait_recv()
    scattered = [
        go(
            all_parts.at[chunk(lax.rem(dp + k, 8))],
            chunk_in.at[k - 1],
            (ps, pr),
            k - 1,
            dp=lax.rem(dp + k, 8),
        )
        for k in range(1, 8)
    ]
    steps.side()
    total = all_parts[chunk(dp), :].astype(f32)
    for k in range(1, 8):
        scattered[k - 1].wait_recv()
        total += chunk_in[k - 1].astype(f32)
    sums[chunk(dp), :] = total.astype(bf16)
    shared = [
        go(sums.at[chunk(dp)], sums.at[chunk(dp)], (as_, ar), k - 1, dp=lax.rem(dp + k, 8))
        for k in range(1, 8)
    ]
    whole = steps.total()
    upstream = whole[:rows]
    weighted = upstream * gain[...]
    values = inputs[...].astype(f32)
    scales = scale[...]
    inner = ColumnSum(
        jnp.sum(weighted * values, axis=1, keepdims=True), sum_buf, (ss, sr), go, peers
    )
    first_part = jnp.sum(upstream * values * scales, axis=0, keepdims=True)
    extra = jnp.concatenate(
        [first_part, gain_part[...], jnp.zeros((14, columns), f32)], axis=0
    )
    lat_buf[dp] = jnp.concatenate([whole[rows:], extra], axis=0).astype(bf16)
    along = [
        go(lat_buf.at[dp], lat_buf.at[dp], (ls, lr), k - 1, dp=lax.rem(dp + k, 8))
        for k in range(1, 8)
    ]
    inputs_grad[...] = (
        residual_grad[...]
        + scales * weighted
        - values * (scales * scales * scales * inner.total() / D)
    ).astype(bf16)
    for copy in along:
        copy.wait_recv()
    summed = lat_buf[0].astype(f32)
    for k in range(1, 8):
        summed += lat_buf[k].astype(f32)
    narrow_all[row] = summed.astype(bf16)
    spread = [
        go(narrow_all.at[row], narrow_all.at[row], (ns, nr), k - 1, row=lax.rem(row + k, 4))
        for k in (1, 2, 3)
    ]
    for copy in spread:
        copy.wait_recv()
    keep = lat - 32
    narrow[...] = narrow_all[:, :keep, :]
    small = narrow_all[0, pl.ds(keep, 16), :]
    latent_gain[col] = small
    last = [
        go(latent_gain.at[col], latent_gain.at[col], (gs, gr), j, col=peer)
        for j, peer in enumerate(peers)
    ]
    edge = pl.ds(keep + 16, 16)
    gains[...] = (
        narrow_all[0, edge, :].astype(f32)
        + narrow_all[1, edge, :].astype(f32)
        + narrow_all[2, edge, :].astype(f32)
        + narrow_all[3, edge, :].astype(f32)
    )
    for copy in last + shared:
        copy.wait_recv()
    for copy in pending:
        copy.wait_send()


def tail_step(part, query, ready, residual_grad, inputs, scale, gain, gain_part):
    rows, columns = inputs.shape
    piece = query.shape[0]
    all_rows = part.shape[0] // 4
    lat = all_rows - rows + 16
    return pl.pallas_call(
        tail_kernel,
        out_shape=(
            jax.ShapeDtypeStruct((rows, columns), bf16),
            jax.ShapeDtypeStruct((8 * piece, columns), bf16),
            jax.ShapeDtypeStruct((4, lat - 32, columns), bf16),
            jax.ShapeDtypeStruct((16, columns), f32),
            jax.ShapeDtypeStruct((4, 16, columns), bf16),
        ),
        in_specs=[VMEM] * 8,
        out_specs=(VMEM,) * 5,
        scratch_shapes=[
            pltpu.VMEM((7, piece, columns), bf16),
            pltpu.VMEM((8 * piece, columns), bf16),
            pltpu.VMEM((4, lat, columns), bf16),
            pltpu.VMEM((8, lat, columns), bf16),
            pltpu.VMEM((4, rows, 128), f32),
            *pair(3),
            *pair(7),
            *pair(7),
            *pair(7),
            *pair(3),
            *pair(3),
            *pair(3),
            *reduce_scratch(all_rows, columns),
        ],
        compiler_params=params(4),
        cost_estimate=cost(1 << 20, 200),
        name="tail_step",
    )(part, query, ready, residual_grad, inputs, scale, gain, gain_part)


def front_kernel(
    attended, weight, inputs, middle, full, attended_rows,
    own, out_buf, in_buf, acc, as_, ar, ps, pr, *sems,
):
    row, sibling, across, corner = place()
    greet((sibling, across), row)
    pending = []
    go = starter(pending)
    rows, columns = inputs.shape
    head = attended.shape[1]
    order = (2, 1, 3, 0)

    def block(k):
        return pl.ds(pl.multiple_of(lax.rem(row + k, 4) * rows, rows), rows)

    def slot(k):
        return pl.ds(k * head, head)

    got = {}
    for k in order:
        got[2, k] = go(
            attended.at[block(k)], attended_rows.at[block(k), slot(2)], (as_, ar), (1, k), col=across
        )
    for k in order:
        got[1, k] = go(
            attended.at[block(k)], attended_rows.at[block(k), slot(1)], (as_, ar), (0, k), col=sibling
        )
    attended_rows[:, slot(0)] = attended[...]
    for k in order:
        got[2, k].wait_recv()
        view = attended_rows.at[block(k), slot(2)]
        got[3, k] = go(
            view, attended_rows.at[block(k), slot(3)], (as_, ar), (2, k), col=sibling
        )
    sent = {}
    for k in order:
        got[1, k].wait_recv()
        got[3, k].wait_recv()
        product = jnp.dot(attended_rows[block(k), :], weight[...], preferred_element_type=f32)
        if k:
            out_buf[k - 1] = product.astype(bf16)
            sent[k] = go(
                out_buf.at[k - 1], in_buf.at[k - 1], (ps, pr), k - 1, row=lax.rem(row + k, 4)
            )
        else:
            acc[...] = product + inputs[...].astype(f32)
    total = acc[...]
    for k in (1, 3, 2):
        sent[k].wait_recv()
        total += in_buf[k - 1].astype(f32)
    middle[...] = total
    own[...] = total.astype(bf16)
    gather_steps(own, full, go, sems[0:2], sems[2:4], sems[4:6], row, sibling, across)
    for copy in pending:
        copy.wait_send()


def front_step(attended, weight, inputs):
    rows, columns = inputs.shape
    return pl.pallas_call(
        front_kernel,
        out_shape=(
            jax.ShapeDtypeStruct((rows, columns), f32),
            jax.ShapeDtypeStruct((4 * rows, 4 * columns), bf16),
            jax.ShapeDtypeStruct((4 * rows, columns), bf16),
        ),
        in_specs=[VMEM] * 3,
        out_specs=(VMEM,) * 3,
        scratch_shapes=[
            pltpu.VMEM((rows, columns), bf16),
            pltpu.VMEM((3, rows, columns), bf16),
            pltpu.VMEM((3, rows, columns), bf16),
            pltpu.VMEM((rows, columns), f32),
            *pair(3, 4),
            *pair(3),
            *gather_scratch,
        ],
        compiler_params=params(5),
        cost_estimate=cost(1 << 29, 150),
        name="front_step",
    )(attended, weight, inputs)


def dot(spec, left, right, kind=f32):
    return jnp.einsum(spec, left, right, preferred_element_type=f32).astype(kind)


def rotary_tables(length, half_width):
    position = jnp.arange(length, dtype=f32)[:, None]
    frequency = jnp.exp(jnp.arange(half_width, dtype=f32) * (-math.log(10000.0) / half_width))
    angles = position * frequency[None, :]
    return (jnp.cos(angles), jnp.sin(angles))


def rotate(values, cos_table, sin_table):
    half_width = cos_table.shape[-1]
    first_half = values[..., :half_width]
    second_half = values[..., half_width:]
    return jnp.concatenate(
        [
            first_half * cos_table - second_half * sin_table,
            second_half * cos_table + first_half * sin_table,
        ],
        axis=-1,
    )


def swap_chips(values, distance, other_replica):
    flip = 4 if other_replica else 0
    pairs = [
        (dp * 4 + col, (dp ^ flip) * 4 + (col ^ distance)) for dp in range(8) for col in range(4)
    ]
    return lax.ppermute(values, ("dp", "col"), pairs)


def deal(pieces):
    got = [pieces(0)]
    for k in (1, 2, 3):
        piece = pieces(k)
        if k == 1:
            got.append(swap_chips(piece, k, False))
        else:
            half = piece.shape[0] // 2
            got.append(
                jnp.concatenate(
                    [swap_chips(piece[:half], k, False), swap_chips(piece[half:], k, True)], axis=0
                )
            )
    return got


def pad_to(values, axis, size):
    widths = [(0, 0)] * values.ndim
    widths[axis] = (0, size - values.shape[axis])
    return jnp.pad(values, widths)


def visible_mask(offset, block_rows, prefix_len):
    query_pos = offset + jnp.arange(block_rows, dtype=jnp.int32)
    key_pos = jnp.arange(SEQ, dtype=jnp.int32)
    return (key_pos[None, :] <= query_pos[:, None]) | (key_pos[None, :] < prefix_len)


def attend_forward(queries, key_rows, value_rows, prefix_len):
    score_scale = (NOPE + ROPE) ** (-0.5)
    scores = dot("qd,kd->qk", queries, key_rows) * score_scale
    scores = jnp.where(visible_mask(0, SEQ, prefix_len), scores, masked_score)
    top_score = jnp.max(scores, axis=1, keepdims=True)
    exp_scores = jnp.exp(scores - top_score)
    row_total = jnp.sum(exp_scores, axis=1, keepdims=True)
    weights = (exp_scores / row_total).astype(bf16)
    result = dot("qk,kd->qd", weights, value_rows)
    return (result, (top_score + jnp.log(row_total))[:, 0])


def attend_backward(queries, key_rows, value_rows, log_total, out_grad, prefix_len):
    score_scale = (NOPE + ROPE) ** (-0.5)
    scores = dot("qd,kd->qk", queries, key_rows) * score_scale
    scores = jnp.where(visible_mask(0, SEQ, prefix_len), scores, masked_score)
    weights = jnp.exp(scores - log_total[:, None])
    value_grad = dot("qk,qd->kd", weights.astype(bf16), out_grad)
    weight_grad = dot("qd,kd->qk", out_grad, value_rows)
    centre = jnp.sum(weights * weight_grad, axis=1, keepdims=True)
    score_grad = (weights * (weight_grad - centre)).astype(bf16)
    query_grad = dot("qk,kd->qd", score_grad, key_rows) * score_scale
    key_grad = dot("qk,qd->kd", score_grad, queries) * score_scale
    return (query_grad, key_grad, value_grad)


def across_dp(values, step, flip):
    pairs = [(dp, ((dp // 4) ^ flip) * 4 + (dp + step) % 4) for dp in range(8)]
    return lax.ppermute(values, "dp", pairs)


def sum_sequences(values):
    z = lax.rem(lax.axis_index("dp"), 4)
    total = lax.dynamic_index_in_dim(values, z, 0, False).astype(f32)
    for step in (1, 2, 3):
        chunk = lax.dynamic_index_in_dim(values, lax.rem(z + step, 4), 0, False)
        total = total + across_dp(chunk, step, 0).astype(f32)
    total = total.astype(bf16)
    total = (total.astype(f32) + across_dp(total, 0, 1).astype(f32)).astype(bf16)
    return jnp.stack([total] + [across_dp(total, step, 0) for step in (1, 2, 3)])


def product(left, right):
    return jnp.dot(left, right, preferred_element_type=f32).astype(bf16)


def expert_grad_kernel(hidden, out_grad, delta, act, grads, *, ff, ff_pad):
    grads[0, pl.ds(0, ff), :] = product(delta[pl.ds(0, ff), :], hidden[...])
    grads[0, pl.ds(ff, ff), :] = product(delta[pl.ds(ff_pad, ff), :], hidden[...])
    grads[0, pl.ds(2 * ff, ff), :] = product(act[pl.ds(0, ff), :], out_grad[...])


def expert_grads(hidden, out_grad, delta, act, ff, ff_pad):
    tokens = hidden.shape[0]
    wide = pl.BlockSpec((tokens, 512), lambda e, k: (0, k))
    return pl.pallas_call(
        functools.partial(expert_grad_kernel, ff=ff, ff_pad=ff_pad),
        grid=(2, 4),
        out_shape=jax.ShapeDtypeStruct((8, 3 * ff, 512), bf16),
        in_specs=[
            wide,
            wide,
            pl.BlockSpec((2 * ff_pad, tokens), lambda e, k: (e, 0)),
            pl.BlockSpec((ff_pad, tokens), lambda e, k: (e, 0)),
        ],
        out_specs=pl.BlockSpec((1, 3 * ff, 512), lambda e, k: (e * 4 + k, 0, 0)),
        compiler_params=pltpu.CompilerParams(vmem_limit_bytes=52 << 20),
        cost_estimate=cost(2 * 8 * 3 * ff * 512 * tokens, 20),
        name="expert_grads",
    )(hidden, out_grad, delta, act)


def shared_grad_kernel(hidden, out_grad, delta, act, grads, router, *, sff, sff_pad):
    gate = product(delta[pl.ds(0, sff_pad), :], hidden[...])
    grads[0, pl.ds(0, sff), :] = gate[:sff]
    router[...] = gate[sff : sff + 16]
    grads[0, pl.ds(sff, sff), :] = product(delta[pl.ds(sff_pad, sff), :], hidden[...])
    grads[0, pl.ds(2 * sff, sff), :] = product(act[pl.ds(0, sff), :], out_grad[...])


def shared_grads(hidden, out_grad, delta, act, sff, sff_pad):
    tokens = hidden.shape[0]
    wide = pl.BlockSpec((tokens, 512), lambda k: (0, k))
    return pl.pallas_call(
        functools.partial(shared_grad_kernel, sff=sff, sff_pad=sff_pad),
        grid=(4,),
        out_shape=(
            jax.ShapeDtypeStruct((4, 3 * sff, 512), bf16),
            jax.ShapeDtypeStruct((16, D), bf16),
        ),
        in_specs=[
            wide,
            wide,
            pl.BlockSpec((2 * sff_pad, tokens), lambda k: (3, 0)),
            pl.BlockSpec((sff_pad, tokens), lambda k: (3, 0)),
        ],
        out_specs=(
            pl.BlockSpec((1, 3 * sff, 512), lambda k: (k, 0, 0)),
            pl.BlockSpec((16, 512), lambda k: (0, k)),
        ),
        compiler_params=pltpu.CompilerParams(vmem_limit_bytes=52 << 20),
        cost_estimate=cost(2 * 4 * 3 * sff * 512 * tokens, 10),
        name="shared_grads",
    )(hidden, out_grad, delta, act)


def sigmoid(value):
    return jax.nn.sigmoid(value)


def on_device(
    inputs,
    attention_gain,
    query_weight,
    latent_weight,
    latent_gain,
    expand_weight,
    output_weight,
    feedforward_gain,
    router_weight,
    shared_gate,
    shared_up,
    shared_down,
    expert_gate,
    expert_up,
    expert_down,
    routes,
    prefix,
    cotangent,
):
    row = lax.axis_index("row")
    col = lax.axis_index("col")
    prefix_len = prefix[0]
    cos_table, sin_table = rotary_tables(SEQ, ROPE // 2)
    first_gain = attention_gain.astype(f32)
    second_gain = feedforward_gain.astype(f32)
    compact_gain = latent_gain.astype(f32)
    residual_in = inputs.astype(f32)
    rows = inputs.shape[0]
    ff = expert_gate.shape[2]
    ff_pad = -(-ff // 128) * 128
    sff = shared_gate.shape[1] // 4
    sff_pad = 256

    gains = jnp.stack([attention_gain, feedforward_gain], axis=1)
    common = pad_to(jnp.concatenate([latent_weight[:, RANK:], router_weight, gains], axis=1), 1, 192)
    heads = query_weight.reshape(512, 4, NOPE + ROPE)

    def attention_piece(k):
        head = lax.dynamic_index_in_dim(heads, col ^ k, 1, False)
        return jnp.concatenate([latent_weight[:, :RANK], head, common], axis=1)

    attention_weights = jnp.concatenate(deal(attention_piece), axis=0)
    first_all = attention_weights[:, RANK + 256 + 8]
    second_all = attention_weights[:, RANK + 256 + 9]
    project_weight = attention_weights[:, : RANK + 256]

    gate_parts = expert_gate.reshape(4, 2, 512, ff)
    up_parts = expert_up.reshape(4, 2, 512, ff)
    down_parts = expert_down.reshape(4, 2, ff, 512)
    shared_gate_parts = shared_gate.reshape(512, 4, sff)
    shared_up_parts = shared_up.reshape(512, 4, sff)
    shared_down_parts = shared_down.reshape(4, sff, 512)

    def up_piece(k):
        gate = pad_to(lax.dynamic_index_in_dim(gate_parts, col ^ k, 0, False), 2, ff_pad)
        up = pad_to(lax.dynamic_index_in_dim(up_parts, col ^ k, 0, False), 2, ff_pad)
        low_gate = lax.dynamic_index_in_dim(shared_gate_parts, col ^ k, 1, False)
        low_gate = pad_to(jnp.concatenate([low_gate, router_weight], axis=1), 1, sff_pad)
        low_up = pad_to(
            lax.dynamic_index_in_dim(shared_up_parts, col ^ k, 1, False), 1, sff_pad
        )
        return jnp.concatenate([gate[0], up[0], gate[1], up[1], low_gate, low_up], axis=1)

    def down_piece(k):
        down = pad_to(lax.dynamic_index_in_dim(down_parts, col ^ k, 0, False), 1, ff_pad)
        low = pad_to(lax.dynamic_index_in_dim(shared_down_parts, col ^ k, 0, False), 0, sff_pad)
        return jnp.concatenate([down[0], down[1], low], axis=0)

    up_weight = jnp.concatenate(deal(up_piece), axis=0)
    down_weight = jnp.concatenate(deal(down_piece), axis=1)
    out_weight = jnp.concatenate(
        [lax.dynamic_slice_in_dim(output_weight, (col ^ k) * VDIM, VDIM, 0) for k in range(4)],
        axis=0,
    )
    order = col ^ jnp.arange(4, dtype=jnp.int32)

    input_rows = gather_grid(inputs, 0).astype(f32)
    scale_one = lax.rsqrt(jnp.mean(input_rows * input_rows, axis=1) + norm_eps)
    normed = (input_rows * scale_one[:, None] * first_all.astype(f32)[None, :]).astype(bf16)
    projected = dot("td,dq->tq", normed, project_weight)
    content = projected[:, :RANK]
    latent_scale = lax.rsqrt(jnp.mean(content * content, axis=1) + norm_eps)
    compact = (content * latent_scale[:, None] * compact_gain[None, :]).astype(bf16)
    shared_key = rotate(projected[:, RANK + 192 :], cos_table, sin_table).astype(bf16)
    key_value = dot("tr,rk->tk", compact, expand_weight, bf16)
    query_rot = jnp.concatenate(
        [
            projected[:, RANK : RANK + NOPE],
            rotate(projected[:, RANK + NOPE : RANK + 192], cos_table, sin_table),
        ],
        axis=1,
    ).astype(bf16)
    key_rows = jnp.concatenate([key_value[:, :NOPE], shared_key], axis=1)
    value_rows = key_value[:, NOPE:]
    head_result, log_total = attend_forward(query_rot, key_rows, value_rows, prefix_len)
    residual_mid, middle_rows, attended_rows = front_step(
        head_result.astype(bf16), out_weight, inputs
    )

    middle_rows = middle_rows.astype(f32)
    scale_two = lax.rsqrt(jnp.mean(middle_rows * middle_rows, axis=1) + norm_eps)
    hidden = (middle_rows * scale_two[:, None] * second_all.astype(f32)[None, :]).astype(bf16)
    out_grad = gather_grid(cotangent, 0)
    experts = jnp.arange(EXPERTS, dtype=jnp.int32)
    named = jnp.any(routes.T[None, :, :] == experts[:, None, None], axis=1).astype(f32)
    pre = dot("td,df->ft", hidden, up_weight)
    low = 4 * ff_pad
    router_probs = jax.nn.softmax(pre[low + sff : low + sff + EXPERTS], axis=0)
    weight_all = router_probs * named
    act_grad_all = dot("td,fd->ft", out_grad, down_weight)
    acts, deltas = [], []
    probs_part = jnp.zeros_like(router_probs)
    for e in range(3):
        if e < 2:
            size, base = ff_pad, 2 * e * ff_pad
            mine = (experts == 2 * col + e).astype(f32)[:, None]
            slot_weight = jnp.sum(weight_all * mine, axis=0, keepdims=True)
        else:
            size, base, slot_weight = sff_pad, low, 1.0
        gate_pre, up_pre = pre[base : base + size], pre[base + size : base + 2 * size]
        act_grad = act_grad_all[e * ff_pad : e * ff_pad + size]
        gate_sig = jax.nn.sigmoid(gate_pre)
        gate_silu = gate_pre * gate_sig
        acts.append((slot_weight * gate_silu * up_pre).astype(bf16))
        weighted = slot_weight * act_grad
        gate_delta = weighted * up_pre * (gate_sig * (1.0 + gate_pre * (1.0 - gate_sig)))
        up_delta = weighted * gate_silu
        if e < 2:
            named_sum = jnp.sum(act_grad * gate_silu * up_pre, axis=0, keepdims=True)
            probs_part = probs_part + named_sum * mine * named
            deltas += [gate_delta, up_delta]
        else:
            logits_part = router_probs * (
                probs_part - jnp.sum(router_probs * probs_part, axis=0, keepdims=True)
            )
            gate_delta = jnp.concatenate(
                [gate_delta[:sff], logits_part, gate_delta[sff + EXPERTS :]], axis=0
            )
            deltas += [gate_delta, up_delta]
    act = jnp.concatenate(acts, axis=0)
    delta = jnp.concatenate([value.astype(bf16) for value in deltas], axis=0)
    combined = dot("ft,fd->td", act, down_weight, bf16)
    hidden_grad = dot("ft,df->td", delta, up_weight, bf16)
    expert_grad = expert_grads(hidden, out_grad, delta, act, ff, ff_pad)
    shared_grad, router_part = shared_grads(hidden, out_grad, delta, act, sff, sff_pad)
    hidden_grad, expert_grad, shared_grad, combined = lax.optimization_barrier(
        (hidden_grad, expert_grad, shared_grad, combined)
    )
    expert_sum = lax.psum_scatter(expert_grad, "dp", scatter_dimension=0, tiled=True)[0]
    shared_home = jnp.stack(
        [shared_grad[0]] + [swap_chips(shared_grad[k], k, False) for k in (1, 2, 3)]
    )
    shared_sum = sum_sequences(shared_home)

    my_scale_one = lax.dynamic_slice_in_dim(scale_one, row * rows, rows, 0)[:, None]
    my_scale_two = lax.dynamic_slice_in_dim(scale_two, row * rows, rows, 0)[:, None]
    residual_grad, residual_rows, attended_grad, second_gain_part = middle_step(
        hidden_grad, residual_mid, cotangent, my_scale_two, second_gain[None, :], out_weight
    )
    output = (residual_mid + reduce_grid(combined, 1)).astype(bf16)
    head_grad = dot("th,td->hd", attended_rows, residual_rows, bf16)
    output_weight_grad = head_grad.reshape(4, VDIM, 512)[order].reshape(4 * VDIM, 512)
    query_rot_grad, key_grad, value_grad = attend_backward(
        query_rot, key_rows, value_rows, log_total, attended_grad, prefix_len
    )
    pair_grad = jnp.concatenate([key_grad[:, :NOPE], value_grad], axis=1).astype(bf16)
    expand_part = dot("tk,tr->kr", pair_grad, compact, bf16)
    compact_grad = dot("tk,rk->tr", pair_grad, expand_weight)
    weighted_compact = compact_grad * compact_gain[None, :]
    inner_sum = jnp.sum(weighted_compact * content, axis=1)
    content_grad = (
        latent_scale[:, None] * weighted_compact
        - content * (latent_scale * latent_scale * latent_scale * inner_sum / RANK)[:, None]
    )
    latent_gain_part = jnp.sum(compact_grad * content * latent_scale[:, None], axis=0)
    project_grad = jnp.concatenate(
        [
            content_grad,
            query_rot_grad[:, :NOPE],
            rotate(query_rot_grad[:, NOPE:], cos_table, -sin_table),
            rotate(key_grad[:, NOPE:], cos_table, -sin_table),
        ],
        axis=1,
    ).astype(bf16)
    normed_grad = dot("tq,dq->td", project_grad, project_weight, bf16)
    project_part = dot("tq,td->qd", project_grad, normed, bf16)
    latent_part = jnp.concatenate([project_part[:RANK], project_part[RANK + 192 :]], axis=0)
    extra = jnp.concatenate(
        [
            jnp.tile(latent_gain_part.astype(bf16)[None, :], (1, 4)),
            router_part[:EXPERTS],
            jnp.zeros((7, D), bf16),
        ],
        axis=0,
    )
    tail = jnp.concatenate(
        [
            normed_grad.reshape(4, rows, D),
            latent_part.reshape(4, -1, D),
            jnp.broadcast_to(extra[None], (4, 16, D)),
        ],
        axis=1,
    )
    inputs_grad, sums, narrow, gains, latent_small = tail_step(
        tail.reshape(-1, D),
        project_part[RANK : RANK + 192],
        jnp.concatenate([output_weight_grad, expand_part], axis=0),
        residual_grad,
        inputs,
        my_scale_one,
        first_gain[None, :],
        second_gain_part,
    )
    output_weight_grad = sums[:512].astype(f32)
    expand_grad = sums[512:768].T.astype(f32)
    query_weight_grad = sums[768:].T.astype(f32)
    latent_weight_grad = narrow.reshape(-1, 512).T.astype(f32)
    latent_gain_grad = latent_small[0, 0].astype(f32)
    router_grad = (
        lax.dynamic_index_in_dim(latent_small, col, 0, False)[1 : 1 + EXPERTS].T.astype(f32)
    )
    first_gain_grad, second_gain_grad = gains[0], gains[1]

    pairs = [
        (dp * 4 + c, (2 * c + dp // 4) * 4 + (c ^ (dp % 4))) for dp in range(8) for c in range(4)
    ]
    expert_sum = lax.ppermute(expert_sum, ("dp", "col"), pairs).astype(f32)
    expert_gate_grad = expert_sum[None, :ff].transpose(0, 2, 1)
    expert_up_grad = expert_sum[None, ff : 2 * ff].transpose(0, 2, 1)
    expert_down_grad = expert_sum[None, 2 * ff :]
    z = lax.rem(lax.axis_index("dp"), 4)
    shared_sum = shared_sum[lax.rem(z + 4 - order, 4)].astype(f32)
    shared_gate_grad = shared_sum[:, :sff].reshape(4 * sff, 512).T
    shared_up_grad = shared_sum[:, sff : 2 * sff].reshape(4 * sff, 512).T
    shared_down_grad = shared_sum[:, 2 * sff :].reshape(4 * sff, 512)
    return (
        output,
        inputs_grad,
        first_gain_grad,
        query_weight_grad,
        latent_weight_grad,
        latent_gain_grad,
        expand_grad,
        output_weight_grad,
        second_gain_grad,
        router_grad,
        shared_gate_grad,
        shared_up_grad,
        shared_down_grad,
        expert_gate_grad,
        expert_up_grad,
        expert_down_grad,
    )


def solution(mesh):
    placed = (
        P(("dp", "row"), "col"),
        P("col"),
        P("col", "row"),
        P("col", None),
        P(),
        P(None, ("row", "col")),
        P("row", "col"),
        P("col"),
        P("col", None),
        P("col", "row"),
        P("col", "row"),
        P("row", "col"),
        P(None, "col", "row"),
        P(None, "col", "row"),
        P(None, "row", "col"),
        P("dp", None),
        P("dp"),
        P(("dp", "row"), "col"),
    )
    return jax.shard_map(
        on_device,
        mesh=mesh,
        in_specs=placed,
        out_specs=(
            P(("dp", "row"), "col"),
            P(("dp", "row"), "col"),
            P("col"),
            P("col", "row"),
            P("col", None),
            P(),
            P(None, ("row", "col")),
            P("row", "col"),
            P("col"),
            P("col", None),
            P("col", "row"),
            P("col", "row"),
            P("row", "col"),
            P("dp", "col", "row"),
            P("dp", "col", "row"),
            P("dp", "row", "col"),
        ),
        check_vma=False,
    )
```

```python
import functools
import math

import jax
import jax.numpy as jnp
from jax import lax
from jax.experimental import pallas as pl
from jax.experimental.pallas import tpu as pltpu
from jax.sharding import PartitionSpec as P

D = 2048
NOPE = 128
ROPE = 64
VDIM = 128
RANK = 512
TOPK = 6
EXPERTS = 8
SEQ = 1024

norm_eps = 1e-06
masked_score = -1e30
bf16 = jnp.bfloat16
f32 = jnp.float32
MESH = pl.DeviceIdType.MESH
DMA = pltpu.SemaphoreType.DMA
VMEM = pl.BlockSpec(memory_space=pltpu.VMEM)
HBM = pl.BlockSpec(memory_space=pl.ANY)


def place():
    row = lax.axis_index("row")
    col = lax.axis_index("col")
    sibling = col + 1 - 2 * lax.rem(col, 2)
    across = lax.rem(col + 2, 4)
    return (row, sibling, across, lax.rem(sibling + 2, 4))


def xor(left, right):
    return lax.rem(lax.rem(left, 2) + lax.rem(right, 2), 2) + 2 * lax.rem(left // 2 + right // 2, 2)


def greet(columns, row, others=()):
    barrier = pltpu.get_barrier_semaphore()
    targets = [{"col": column} for column in columns]
    targets += [{"row": lax.rem(row + step, 4)} for step in (1, 2, 3)]
    targets += list(others)
    for target in targets:
        pl.semaphore_signal(barrier, inc=1, device_id=target, device_id_type=MESH)
    pl.semaphore_wait(barrier, len(targets))


def along_z(dp, step):
    return dp // 4 * 4 + lax.rem(lax.rem(dp, 4) + step, 4)


def remote(source, target, sems, at, **device):
    return pltpu.make_async_remote_copy(
        src_ref=source,
        dst_ref=target,
        send_sem=sems[0].at[at],
        recv_sem=sems[1].at[at],
        device_id=device,
        device_id_type=MESH,
    )


def starter(pending):
    def go(*arguments, **device):
        copy = remote(*arguments, **device)
        copy.start()
        pending.append(copy)
        return copy

    return go


def pair(*shape):
    return [DMA(shape), DMA(shape)]


def params(collective):
    return pltpu.CompilerParams(
        collective_id=collective, has_side_effects=True, vmem_limit_bytes=52 << 20
    )


def cost(flops, mebibytes):
    return pl.CostEstimate(flops=flops, bytes_accessed=mebibytes << 20, transcendentals=0)


class Gather:
    def __init__(self, own, full, sems, go, row, sibling, across):
        self.own, self.full, self.go = own, full, go
        self.xs, self.ys, self.cs = sems[0:2], sems[2:4], sems[4:6]
        self.row, self.sibling, self.across = row, sibling, across
        self.arrivals = []

    def block(self, at_row, at_col):
        rows, columns = self.own.shape
        start = pl.multiple_of(at_row * rows, rows)
        return self.full.at[pl.ds(start, rows), pl.ds(at_col * columns, columns)]

    def along(self, source, target, base):
        return [
            self.go(source, target, self.ys, base + k - 1, row=lax.rem(self.row + k, 4))
            for k in (1, 2, 3)
        ]

    def over(self, source, target):
        count = len(self.arrivals)
        self.arrivals.append(self.go(source, target, self.cs, count, col=self.sibling))

    def begin(self):
        row = self.row
        rows, columns = self.own.shape
        self.side = self.go(self.own, self.block(row, 2), self.xs, 0, col=self.across)
        self.first = self.along(self.own, self.block(row, 0), 0)
        self.over(self.own, self.block(row, 1))
        start = pl.multiple_of(row * rows, rows)
        self.full[pl.ds(start, rows), pl.ds(0, columns)] = self.own[...]

    def second(self):
        self.side.wait_recv()
        here = self.block(self.row, 2)
        self.rest = self.along(here, here, 3)
        self.over(here, self.block(self.row, 3))

    def forward(self, group, at_col):
        for k in (1, 3, 2):
            group[k - 1].wait_recv()
            source = lax.rem(self.row + 4 - k, 4)
            self.over(self.block(source, at_col), self.block(source, at_col + 1))

    def forward_first(self):
        self.forward(self.first, 0)

    def forward_rest(self):
        self.forward(self.rest, 2)

    def finish(self):
        for copy in self.arrivals:
            copy.wait_recv()


gather_scratch = pair(1) + pair(6) + pair(8)


class Deal:
    def __init__(self, sems, local_sems, pending, col, peers):
        self.go, self.sems, self.local_sems = starter(pending), sems, local_sems
        self.col, self.peers = col, peers
        self.far = lax.rem(lax.axis_index("dp") + 4, 8)
        self.copies, self.local, self.count = [], [], 0

    def send(self, source, target, flip):
        n = self.count
        self.count += 1
        copy = pltpu.make_async_copy(source(self.col), target(0), self.local_sems.at[n])
        copy.start()
        self.local.append(copy)
        for k, peer in ((2, self.peers[1]), (3, self.peers[2]), (1, self.peers[0])):
            place_at = {"col": peer}
            if flip and k != 1:
                place_at["dp"] = self.far
            self.copies.append(
                self.go(source(peer), target(k), self.sems, (k - 1, n), **place_at)
            )

    def finish(self):
        for copy in self.local:
            copy.wait()
        for copy in self.copies:
            copy.wait_recv()


def deal_scratch(count):
    return pair(3, count) + [DMA((count,))]


def deal_peers(peers):
    far = lax.rem(lax.axis_index("dp") + 4, 8)
    return [{"dp": far, "col": peer} for peer in peers[1:]]


def lanes(array, start, size):
    return lambda k: array.at[pl.ds(start, size), pl.ds(512 * k, 512)]


def rows_at(array, size):
    return lambda column: array.at[pl.ds(pl.multiple_of(column * size, size), size)]


def start_kernel(
    inputs, cotangent, common, query, gate, low_gate, low_up, router, low_down,
    full, out_grad, project, gates, lows, *sems,
):
    row, sibling, across, corner = place()
    col = lax.axis_index("col")
    peers = (sibling, across, corner)
    greet(peers, row, deal_peers(peers))
    pending = []
    go = starter(pending)
    gather = Gather(inputs, full, sems[0:6], go, row, sibling, across)
    beside = Gather(cotangent, out_grad, sems[6:12], go, row, sibling, across)
    deal = Deal(sems[12:14], sems[14], pending, col, peers)
    ff = gate.shape[1]
    low = low_down.shape[0] // 4
    gather.begin()
    deal.send(lambda column: common.at[pl.ds(0, RANK)], lanes(project, 0, RANK), True)
    deal.send(rows_at(query, 192), lanes(project, RANK, 192), False)
    deal.send(lambda column: common.at[pl.ds(RANK, 80)], lanes(project, RANK + 192, 80), False)
    beside.begin()
    gather.second()
    for e in (0, 1):
        deal.send(lambda column, e=e: gate.at[2 * column + e], lanes(gates, e * ff, ff), e == 1)
    beside.second()
    deal.send(rows_at(low_gate, low), lanes(lows, 0, low), True)
    deal.send(rows_at(low_up, low), lanes(lows, low, low), False)
    deal.send(lambda column: router, lanes(lows, 2 * low, 16), True)
    deal.send(rows_at(low_down, low), lanes(lows, 2 * low + 16, low), True)
    gather.forward_first()
    gather.forward_rest()
    beside.forward_first()
    beside.forward_rest()
    gather.finish()
    beside.finish()
    deal.finish()
    for copy in pending:
        copy.wait_send()


def start_step(inputs, cotangent, common, query, gate, low_gate, low_up, router, low_down):
    rows, columns = inputs.shape
    low = low_down.shape[0] // 4
    wide = jax.ShapeDtypeStruct((4 * rows, 4 * columns), bf16)
    return pl.pallas_call(
        start_kernel,
        out_shape=(
            wide,
            wide,
            jax.ShapeDtypeStruct((RANK + 272, 4 * columns), bf16),
            jax.ShapeDtypeStruct((2 * gate.shape[1], 4 * columns), bf16),
            jax.ShapeDtypeStruct((3 * low + 16, 4 * columns), bf16),
        ),
        in_specs=[VMEM] * 2 + [HBM] * 7,
        out_specs=(VMEM, VMEM, HBM, HBM, HBM),
        scratch_shapes=[*gather_scratch, *gather_scratch, *deal_scratch(9)],
        compiler_params=params(0),
        cost_estimate=cost(0, 150),
        name="start_step",
    )(inputs, cotangent, common, query, gate, low_gate, low_up, router, low_down)


def reduce_scratch(rows, columns):
    return [
        pltpu.VMEM((4, 2, rows, columns), bf16),
        pltpu.VMEM((3, 2, rows, columns), bf16),
        pltpu.VMEM((3, 2, rows, columns), bf16),
        pltpu.VMEM((2, rows, columns), f32),
        pltpu.VMEM((2, rows, columns), bf16),
        *pair(1),
        *pair(3, 2),
        *pair(4, 2),
    ]


class Reduction:
    order = (2, 1, 3, 0)

    def __init__(self, part, scratch, row, sibling, across):
        self.part = part
        self.held, self.out_buf, self.in_buf, self.acc, self.side_buf = scratch[:5]
        self.xs, self.ys, self.cs = scratch[5:7], scratch[7:9], scratch[9:11]
        self.row, self.sibling, self.across = row, sibling, across
        self.rows, self.columns = self.acc.shape[1:]

    def rows_of(self, k):
        start = lax.rem(self.row + k, 4) * self.rows
        return pl.ds(pl.multiple_of(start, self.rows), self.rows)

    def pair_copy(self, k, x):
        return remote(
            self.part.at[self.rows_of(k), pl.ds((2 * x + 1) * self.columns, self.columns)],
            self.held.at[k, x],
            self.cs,
            (k, x),
            col=self.sibling,
        )

    def along_copy(self, k, x):
        return remote(
            self.out_buf.at[k - 1, x],
            self.in_buf.at[k - 1, x],
            self.ys,
            (k - 1, x),
            row=lax.rem(self.row + k, 4),
        )

    def side_copy(self):
        return remote(self.side_buf.at[0], self.side_buf.at[1], self.xs, 0, col=self.across)

    def start(self):
        for k in self.order:
            for x in (0, 1):
                self.pair_copy(k, x).start()

    def along(self, order=(2, 1, 3, 0)):
        for k in order:
            for x in (0, 1):
                self.pair_copy(k, x).wait_recv()
                mine = self.part[self.rows_of(k), pl.ds(2 * x * self.columns, self.columns)]
                value = mine.astype(f32) + self.held[k, x].astype(f32)
                if k:
                    self.out_buf[k - 1, x] = value.astype(bf16)
                    self.along_copy(k, x).start()
                else:
                    self.acc[x] = value

    def side(self):
        for x in (1, 0):
            for k in (1, 3, 2):
                self.along_copy(k, x).wait_recv()
                self.acc[x] += self.in_buf[k - 1, x].astype(f32)
            if x:
                self.side_buf[0] = self.acc[1].astype(bf16)
                self.side_copy().start()

    def total(self):
        self.side_copy().wait_recv()
        return self.acc[0] + self.side_buf[1].astype(f32)

    def finish(self):
        for k in self.order:
            for x in (0, 1):
                self.pair_copy(k, x).wait_send()
                if k:
                    self.along_copy(k, x).wait_send()
        self.side_copy().wait_send()


def product(left, right):
    return jnp.dot(left, right, preferred_element_type=f32).astype(bf16)


def times_rows(left, right):
    return lax.dot_general(left, right, (((1,), (1,)), ((), ())), preferred_element_type=f32)


def over_units(left, right):
    return lax.dot_general(left, right, (((0,), (0,)), ((), ())), preferred_element_type=f32)


def expert_kernel(
    middle, out_grad, gates, ups, downs, lows, gain, named, mine, hidden, scale, act, delta
):
    values = middle[...].astype(f32)
    scales = lax.rsqrt(jnp.mean(values * values, axis=1, keepdims=True) + norm_eps)
    scale[...] = jnp.broadcast_to(scales, scale.shape)
    normal = (values * scales * gain[...]).astype(bf16)
    hidden[...] = normal
    upstream = out_grad[...]
    ff = gates.shape[0] // 2
    low = (lows.shape[0] - 16) // 3
    low_pre = times_rows(lows[pl.ds(0, 2 * low + 16), :], normal)
    logits = low_pre[2 * low : 2 * low + EXPERTS]
    powers = jnp.exp(logits - jnp.max(logits, axis=0, keepdims=True))
    probs = powers / jnp.sum(powers, axis=0, keepdims=True)
    names = named[...]
    probs_part = jnp.zeros_like(probs)
    for e in range(3):
        if e < 2:
            size, at = ff, pl.ds(e * ff, ff)
            gate_pre = times_rows(gates[at, :], normal)
            up_pre = times_rows(ups[at, :], normal)
            act_grad = times_rows(downs[at, :], upstream)
            own = mine[:, e : e + 1]
            weight = jnp.sum(probs * names * own, axis=0, keepdims=True)
            gate_at, up_at, act_at = e * ff, (2 + e) * ff, e * ff
        else:
            size = low
            gate_pre, up_pre = low_pre[:low], low_pre[low : 2 * low]
            act_grad = times_rows(lows[pl.ds(2 * low + 16, low), :], upstream)
            weight = 1.0
            gate_at, up_at, act_at = 4 * ff, 4 * ff + low, 2 * ff
        sig = 1.0 / (1.0 + jnp.exp(-gate_pre))
        silu = gate_pre * sig
        both = silu * up_pre
        act[pl.ds(act_at, size), :] = (weight * both).astype(bf16)
        weighted = weight * act_grad
        delta[pl.ds(gate_at, size), :] = (
            weighted * up_pre * (sig * (1.0 + gate_pre * (1.0 - sig)))
        ).astype(bf16)
        delta[pl.ds(up_at, size), :] = (weighted * silu).astype(bf16)
        if e < 2:
            named_sum = jnp.sum(act_grad * both, axis=0, keepdims=True)
            probs_part = probs_part + named_sum * own * names
    logits_part = probs * (probs_part - jnp.sum(probs * probs_part, axis=0, keepdims=True))
    delta[pl.ds(4 * ff + 2 * low, 16), :] = jnp.concatenate(
        [logits_part, jnp.zeros_like(logits_part)], axis=0
    ).astype(bf16)


def whole(value):
    return pl.BlockSpec(value.shape, lambda i: (0,) * len(value.shape))


def expert_step(middle, out_grad, gates, ups, downs, lows, gain, named, mine):
    tile = 256
    tokens, width = middle.shape
    wide = pl.BlockSpec((tile, width), lambda i: (i, 0))

    def tall(rows):
        return pl.BlockSpec((rows, tile), lambda i: (0, i))

    acts = downs.shape[0] + (lows.shape[0] - 16) // 3
    deltas = gates.shape[0] + ups.shape[0] + 2 * (lows.shape[0] - 16) // 3 + 16
    return pl.pallas_call(
        expert_kernel,
        grid=(tokens // tile,),
        out_shape=(
            jax.ShapeDtypeStruct((tokens, width), bf16),
            jax.ShapeDtypeStruct((tokens, 128), f32),
            jax.ShapeDtypeStruct((acts, tokens), bf16),
            jax.ShapeDtypeStruct((deltas, tokens), bf16),
        ),
        in_specs=[
            wide,
            wide,
            whole(gates),
            whole(ups),
            whole(downs),
            whole(lows),
            whole(gain),
            tall(EXPERTS),
            whole(mine),
        ],
        out_specs=(
            wide,
            pl.BlockSpec((tile, 128), lambda i: (i, 0)),
            tall(acts),
            tall(deltas),
        ),
        compiler_params=pltpu.CompilerParams(vmem_limit_bytes=56 << 20),
        cost_estimate=cost(2 * 5 * gates.shape[0] * width * tokens, 30),
        name="expert_step",
    )(middle, out_grad, gates, ups, downs, lows, gain, named, mine)


def back_kernel(act, delta, gates, ups, downs, lows, combined, hidden_grad):
    ff = gates.shape[0]
    low = (lows.shape[0] - 16) // 3
    combined[...] = (
        over_units(act[pl.ds(0, ff), :], downs[...])
        + over_units(act[pl.ds(ff, low), :], lows[pl.ds(2 * low + 16, low), :])
    ).astype(bf16)
    hidden_grad[...] = (
        over_units(delta[pl.ds(0, ff), :], gates[...])
        + over_units(delta[pl.ds(ff, ff), :], ups[...])
        + over_units(delta[pl.ds(2 * ff, 2 * low + 16), :], lows[pl.ds(0, 2 * low + 16), :])
    ).astype(bf16)


def back_step(act, delta, gates, ups, downs, lows):
    tile = 256
    tokens, width = act.shape[1], gates.shape[1]
    wide = pl.BlockSpec((tile, width), lambda i: (i, 0))
    return pl.pallas_call(
        back_kernel,
        grid=(tokens // tile,),
        out_shape=(jax.ShapeDtypeStruct((tokens, width), bf16),) * 2,
        in_specs=[
            pl.BlockSpec((act.shape[0], tile), lambda i: (0, i)),
            pl.BlockSpec((delta.shape[0], tile), lambda i: (0, i)),
            whole(gates),
            whole(ups),
            whole(downs),
            whole(lows),
        ],
        out_specs=(wide, wide),
        compiler_params=pltpu.CompilerParams(vmem_limit_bytes=56 << 20),
        cost_estimate=cost(2 * 4 * gates.shape[0] * width * tokens, 30),
        name="back_step",
    )(act, delta, gates, ups, downs, lows)


def grads_kernel(hidden, out_grad, delta, act, grads, *, ff):
    for e in (0, 1):

        @pl.when(pl.program_id(0) // 4 == e)
        def _(e=e):
            at = e * ff
            grads[0, pl.ds(0, ff), :] = product(delta[pl.ds(at, ff), :], hidden[...])
            grads[0, pl.ds(ff, ff), :] = product(delta[pl.ds(2 * ff + at, ff), :], hidden[...])
            grads[0, pl.ds(2 * ff, ff), :] = product(act[pl.ds(at, ff), :], out_grad[...])


def grads_step(hidden, out_grad, delta, act, ff):
    tokens = hidden.shape[0]
    wide = pl.BlockSpec((tokens, 512), lambda i: (0, i % 4))
    return pl.pallas_call(
        functools.partial(grads_kernel, ff=ff),
        grid=(8,),
        out_shape=jax.ShapeDtypeStruct((8, 3 * ff, 512), bf16),
        in_specs=[wide, wide, whole(delta), whole(act)],
        out_specs=pl.BlockSpec((1, 3 * ff, 512), lambda i: (i, 0, 0)),
        compiler_params=pltpu.CompilerParams(vmem_limit_bytes=56 << 20),
        cost_estimate=cost(2 * 8 * 3 * ff * 512 * tokens, 30),
        name="grads_step",
    )(hidden, out_grad, delta, act)


def shared_kernel(hidden, out_grad, delta, act, grads, router, *, ff, low):
    base = 4 * ff
    grads[0, pl.ds(0, low), :] = product(delta[pl.ds(base, low), :], hidden[...])
    grads[0, pl.ds(low, low), :] = product(delta[pl.ds(base + low, low), :], hidden[...])
    router[...] = product(delta[pl.ds(base + 2 * low, 16), :], hidden[...])
    grads[0, pl.ds(2 * low, low), :] = product(act[pl.ds(2 * ff, low), :], out_grad[...])


def shared_step(hidden, out_grad, delta, act, ff, low):
    tokens = hidden.shape[0]
    wide = pl.BlockSpec((tokens, 512), lambda i: (0, i))
    return pl.pallas_call(
        functools.partial(shared_kernel, ff=ff, low=low),
        grid=(4,),
        out_shape=(
            jax.ShapeDtypeStruct((4, 3 * low, 512), bf16),
            jax.ShapeDtypeStruct((16, D), bf16),
        ),
        in_specs=[wide, wide, whole(delta), whole(act)],
        out_specs=(
            pl.BlockSpec((1, 3 * low, 512), lambda i: (i, 0, 0)),
            pl.BlockSpec((16, 512), lambda i: (0, i)),
        ),
        compiler_params=pltpu.CompilerParams(vmem_limit_bytes=56 << 20),
        cost_estimate=cost(2 * 4 * 3 * low * 512 * tokens, 15),
        name="shared_step",
    )(hidden, out_grad, delta, act)


class ColumnSum:
    def __init__(self, value, buf, sems, go, peers):
        self.buf, self.own = buf, value
        buf[0] = jnp.broadcast_to(value, buf.shape[1:])
        self.sent = [
            go(buf.at[0], buf.at[k + 1], sems, k, col=peer) for k, peer in enumerate(peers)
        ]

    def total(self):
        for copy in self.sent:
            copy.wait_recv()
        buf = self.buf
        return ((buf[0] + buf[1]) + (buf[2] + buf[3]))[:, :1]


def middle_kernel(
    part, combined, middle, cotangent, scale, gain, weight, shared,
    residual_grad, residual_rows, attended_grad, gain_part, shared_sum, output,
    sum_buf, out_buf, in_buf, acc, chunk_in, ss, sr, rs, rr, hs, hr, ps, pr, *scratch,
):
    row, sibling, across, corner = place()
    dp = lax.axis_index("dp")
    z = lax.rem(dp, 4)
    far = lax.rem(dp + 4, 8)
    peers = (sibling, across, corner)
    greet(peers, row, [{"dp": along_z(dp, k)} for k in (1, 2, 3)] + [{"dp": far}])
    pending = []
    go = starter(pending)
    count = len(scratch) // 2
    steps = Reduction(part, scratch[:count], row, sibling, across)
    beside = Reduction(combined, scratch[count:], row, sibling, across)
    rows, columns = middle.shape
    head = attended_grad.shape[1]
    steps.start()
    scattered = [
        go(
            shared.at[lax.rem(z + k, 4)], chunk_in.at[k - 1], (ps, pr), k - 1, dp=along_z(dp, k)
        )
        for k in (1, 2, 3)
    ]
    steps.along()
    beside.start()
    steps.side()
    upstream = steps.total()
    weighted = upstream * gain[...]
    values = middle[...]
    scales = scale[...]
    inner = ColumnSum(
        jnp.sum(weighted * values, axis=1, keepdims=True), sum_buf, (ss, sr), go, peers
    )
    gain_part[...] = jnp.sum(upstream * values * scales, axis=0, keepdims=True)
    base = cotangent[...].astype(f32) + scales * weighted
    grad = base - values * (scales * scales * scales * inner.total() / D)
    residual_grad[...] = grad

    def block(at_row):
        return pl.ds(pl.multiple_of(at_row * rows, rows), rows)

    residual_rows[block(row), :] = grad.astype(bf16)
    sent = [
        go(
            residual_rows.at[block(row)],
            residual_rows.at[block(row)],
            (rs, rr),
            k - 1,
            row=lax.rem(row + k, 4),
        )
        for k in (1, 2, 3)
    ]
    beside.along()
    got = []
    for k in (0, 1, 3, 2):
        source = lax.rem(row + 4 - k, 4)
        if k:
            sent[k - 1].wait_recv()
        result = times_rows(residual_rows[block(source), :], weight[...])
        acc[block(source), :] = result[:, :head]
        for j, peer in enumerate(peers):
            out_buf[j, block(source), :] = result[:, (j + 1) * head : (j + 2) * head].astype(bf16)
            got.append(
                go(
                    out_buf.at[j, block(source)],
                    in_buf.at[j, block(source)],
                    (hs, hr),
                    (j, k),
                    col=peer,
                )
            )
    total = shared[z].astype(f32)
    for k in (1, 2, 3):
        scattered[k - 1].wait_recv()
        total += chunk_in[k - 1].astype(f32)
    chunk_in[3] = total.astype(bf16)
    halves = go(chunk_in.at[3], chunk_in.at[4], (ps, pr), 3, dp=far)
    beside.side()
    for copy in got:
        copy.wait_recv()
    attended_grad[...] = (
        acc[...] + in_buf[0].astype(f32) + in_buf[1].astype(f32) + in_buf[2].astype(f32)
    ).astype(bf16)
    output[...] = (beside.total() + values).astype(bf16)
    halves.wait_recv()
    shared_sum[...] = (chunk_in[3].astype(f32) + chunk_in[4].astype(f32)).astype(bf16)
    for copy in pending:
        copy.wait_send()
    steps.finish()
    beside.finish()


def middle_step(part, combined, middle, cotangent, scale, gain, weight, shared):
    rows, columns = middle.shape
    piece = shared.shape[1]
    return pl.pallas_call(
        middle_kernel,
        out_shape=(
            jax.ShapeDtypeStruct((rows, columns), f32),
            jax.ShapeDtypeStruct((4 * rows, columns), bf16),
            jax.ShapeDtypeStruct((4 * rows, VDIM), bf16),
            jax.ShapeDtypeStruct((1, columns), f32),
            jax.ShapeDtypeStruct((piece, columns), bf16),
            jax.ShapeDtypeStruct((rows, columns), bf16),
        ),
        in_specs=[VMEM] * 8,
        out_specs=(VMEM,) * 6,
        scratch_shapes=[
            pltpu.VMEM((4, rows, 128), f32),
            pltpu.VMEM((3, 4 * rows, VDIM), bf16),
            pltpu.VMEM((3, 4 * rows, VDIM), bf16),
            pltpu.VMEM((4 * rows, VDIM), f32),
            pltpu.VMEM((5, piece, columns), bf16),
            *pair(3),
            *pair(3),
            *pair(3, 4),
            *pair(4),
            *reduce_scratch(rows, columns),
            *reduce_scratch(rows, columns),
        ],
        compiler_params=params(3),
        cost_estimate=cost(1 << 29, 200),
        name="middle_step",
    )(part, combined, middle, cotangent, scale, gain, weight, shared)


def tail_kernel(
    part, query, ready, residual_grad, inputs, scale, gain, gain_part, shared_sum,
    inputs_grad, sums, narrow, gains, latent_gain, shared_all,
    chunk_in, all_parts, narrow_all, lat_buf, lat_half, sum_buf,
    qs, qr, ps, pr, as_, ar, ls, lr, ns, nr, ss, sr, gs, gr, ws, wr, *scratch,
):
    row, sibling, across, corner = place()
    col = lax.axis_index("col")
    dp = lax.axis_index("dp")
    z = lax.rem(dp, 4)
    far = lax.rem(dp + 4, 8)
    peers = (sibling, across, corner)
    others = [{"dp": along_z(dp, k)} for k in (1, 2, 3)] + [{"dp": far}]
    others += [
        {"dp": along_z(dp, 4 - k), "col": xor(col, lax.rem(z + 4 - k, 4))} for k in (1, 2, 3)
    ]
    greet(peers, row, others)
    pending = []
    go = starter(pending)
    steps = Reduction(part, scratch, row, sibling, across)
    rows, columns = inputs.shape
    piece = query.shape[0]
    lat = narrow_all.shape[1]

    def head(at):
        return pl.ds(pl.multiple_of(at * piece, piece), piece)

    def chunk(at):
        return pl.ds(pl.multiple_of(at * 2 * piece, 2 * piece), 2 * piece)

    steps.start()
    dealt = [
        go(
            query.at[:, pl.ds((j + 1) * columns, columns)],
            all_parts.at[head(4 + col)],
            (qs, qr),
            j,
            col=peer,
        )
        for j, peer in enumerate(peers)
    ]
    all_parts[pl.ds(0, 4 * piece), :] = ready[...]
    all_parts[head(4 + col), :] = query[:, pl.ds(0, columns)]
    goal = xor(col, z)
    spread_shared = [
        go(shared_sum, shared_all.at[z], (ws, wr), k - 1, dp=along_z(dp, k), col=goal)
        for k in (1, 2, 3)
    ]

    def own_block():
        return remote(shared_sum, shared_all.at[z], (ws, wr), 3, col=goal)

    @pl.when(z == 0)
    def _():
        shared_all[0] = shared_sum[...]

    @pl.when(z != 0)
    def _():
        own_block().start()

    steps.along()
    for copy in dealt:
        copy.wait_recv()
    scattered = [
        go(
            all_parts.at[chunk(lax.rem(z + k, 4))],
            chunk_in.at[k - 1],
            (ps, pr),
            k - 1,
            dp=along_z(dp, k),
        )
        for k in (1, 2, 3)
    ]
    steps.side()
    total = all_parts[chunk(z), :].astype(f32)
    for k in (1, 2, 3):
        scattered[k - 1].wait_recv()
        total += chunk_in[k - 1].astype(f32)
    chunk_in[3] = total.astype(bf16)
    halves = go(chunk_in.at[3], chunk_in.at[4], (ps, pr), 3, dp=far)
    whole = steps.total()
    upstream = whole[:rows]
    weighted = upstream * gain[...]
    values = inputs[...].astype(f32)
    scales = scale[...]
    inner = ColumnSum(
        jnp.sum(weighted * values, axis=1, keepdims=True), sum_buf, (ss, sr), go, peers
    )
    first_part = jnp.sum(upstream * values * scales, axis=0, keepdims=True)
    extra = jnp.concatenate([first_part, gain_part[...], jnp.zeros((14, columns), f32)], axis=0)
    lat_buf[z] = jnp.concatenate([whole[rows:], extra], axis=0).astype(bf16)
    along = [
        go(lat_buf.at[z], lat_buf.at[z], (ls, lr), k - 1, dp=along_z(dp, k)) for k in (1, 2, 3)
    ]
    halves.wait_recv()
    sums[chunk(z), :] = (chunk_in[3].astype(f32) + chunk_in[4].astype(f32)).astype(bf16)
    shared = [
        go(sums.at[chunk(z)], sums.at[chunk(z)], (as_, ar), k - 1, dp=along_z(dp, k))
        for k in (1, 2, 3)
    ]
    for copy in along:
        copy.wait_recv()
    lat_half[0] = (
        (lat_buf[0].astype(f32) + lat_buf[1].astype(f32))
        + (lat_buf[2].astype(f32) + lat_buf[3].astype(f32))
    ).astype(bf16)
    other = go(lat_half.at[0], lat_half.at[1], (ls, lr), 3, dp=far)
    inputs_grad[...] = (
        residual_grad[...]
        + scales * weighted
        - values * (scales * scales * scales * inner.total() / D)
    ).astype(bf16)
    other.wait_recv()
    narrow_all[row] = (lat_half[0].astype(f32) + lat_half[1].astype(f32)).astype(bf16)
    spread = [
        go(narrow_all.at[row], narrow_all.at[row], (ns, nr), k - 1, row=lax.rem(row + k, 4))
        for k in (1, 2, 3)
    ]
    for copy in spread:
        copy.wait_recv()
    keep = lat - 32
    narrow[...] = narrow_all[:, :keep, :]
    latent_gain[col] = narrow_all[0, pl.ds(keep, 16), :]
    last = [
        go(latent_gain.at[col], latent_gain.at[col], (gs, gr), j, col=peer)
        for j, peer in enumerate(peers)
    ]
    edge = pl.ds(keep + 16, 16)
    gains[...] = (
        narrow_all[0, edge, :].astype(f32)
        + narrow_all[1, edge, :].astype(f32)
        + narrow_all[2, edge, :].astype(f32)
        + narrow_all[3, edge, :].astype(f32)
    )
    for copy in last + shared + spread_shared:
        copy.wait_recv()

    @pl.when(z != 0)
    def _():
        own_block().wait()

    for copy in pending:
        copy.wait_send()
    steps.finish()


def tail_step(part, query, ready, residual_grad, inputs, scale, gain, gain_part, shared_sum):
    rows, columns = inputs.shape
    piece = query.shape[0]
    all_rows = part.shape[0] // 4
    lat = all_rows - rows + 16
    return pl.pallas_call(
        tail_kernel,
        out_shape=(
            jax.ShapeDtypeStruct((rows, columns), bf16),
            jax.ShapeDtypeStruct((8 * piece, columns), bf16),
            jax.ShapeDtypeStruct((4, lat - 32, columns), bf16),
            jax.ShapeDtypeStruct((16, columns), f32),
            jax.ShapeDtypeStruct((4, 16, columns), bf16),
            jax.ShapeDtypeStruct((4,) + shared_sum.shape, bf16),
        ),
        in_specs=[VMEM] * 9,
        out_specs=(VMEM,) * 6,
        scratch_shapes=[
            pltpu.VMEM((5, 2 * piece, columns), bf16),
            pltpu.VMEM((8 * piece, columns), bf16),
            pltpu.VMEM((4, lat, columns), bf16),
            pltpu.VMEM((4, lat, columns), bf16),
            pltpu.VMEM((2, lat, columns), bf16),
            pltpu.VMEM((4, rows, 128), f32),
            *pair(3),
            *pair(4),
            *pair(3),
            *pair(4),
            *pair(3),
            *pair(3),
            *pair(3),
            *pair(4),
            *reduce_scratch(all_rows, columns),
        ],
        compiler_params=params(4),
        cost_estimate=cost(1 << 20, 200),
        name="tail_step",
    )(part, query, ready, residual_grad, inputs, scale, gain, gain_part, shared_sum)


def front_kernel(
    attended, weight, inputs, up, down, middle, full, attended_rows, ups, downs,
    own, out_buf, in_buf, acc, as_, ar, ps, pr, *sems,
):
    row, sibling, across, corner = place()
    peers = (sibling, across, corner)
    greet(peers, row, deal_peers(peers))
    pending = []
    go = starter(pending)
    rows, columns = inputs.shape
    head = attended.shape[1]
    order = (2, 1, 3, 0)

    def block(k):
        return pl.ds(pl.multiple_of(lax.rem(row + k, 4) * rows, rows), rows)

    def slot(k):
        return pl.ds(k * head, head)

    got = {}
    for k in order:
        got[2, k] = go(
            attended.at[block(k)], attended_rows.at[block(k), slot(2)], (as_, ar), (1, k), col=across
        )
    for k in order:
        got[1, k] = go(
            attended.at[block(k)], attended_rows.at[block(k), slot(1)], (as_, ar), (0, k), col=sibling
        )
    attended_rows[:, slot(0)] = attended[...]
    deal = Deal(sems[6:8], sems[8], pending, lax.axis_index("col"), peers)
    ff = up.shape[1]
    for k in order:
        got[2, k].wait_recv()
        view = attended_rows.at[block(k), slot(2)]
        got[3, k] = go(
            view, attended_rows.at[block(k), slot(3)], (as_, ar), (2, k), col=sibling
        )
    for e in (0, 1):
        deal.send(lambda column, e=e: up.at[2 * column + e], lanes(ups, e * ff, ff), e == 1)
        deal.send(lambda column, e=e: down.at[2 * column + e], lanes(downs, e * ff, ff), e == 1)
    sent = {}
    for k in order:
        got[1, k].wait_recv()
        got[3, k].wait_recv()
        product = jnp.dot(attended_rows[block(k), :], weight[...], preferred_element_type=f32)
        if k:
            out_buf[k - 1] = product.astype(bf16)
            sent[k] = go(
                out_buf.at[k - 1], in_buf.at[k - 1], (ps, pr), k - 1, row=lax.rem(row + k, 4)
            )
        else:
            acc[...] = product + inputs[...].astype(f32)
    total = acc[...]
    for k in (1, 3, 2):
        sent[k].wait_recv()
        total += in_buf[k - 1].astype(f32)
    middle[...] = total
    own[...] = total.astype(bf16)
    gather = Gather(own, full, sems[:6], go, row, sibling, across)
    gather.begin()
    gather.second()
    gather.forward_first()
    gather.forward_rest()
    gather.finish()
    deal.finish()
    for copy in pending:
        copy.wait_send()


def front_step(attended, weight, inputs, up, down):
    rows, columns = inputs.shape
    dealt = jax.ShapeDtypeStruct((2 * up.shape[1], 4 * columns), bf16)
    return pl.pallas_call(
        front_kernel,
        out_shape=(
            jax.ShapeDtypeStruct((rows, columns), f32),
            jax.ShapeDtypeStruct((4 * rows, 4 * columns), bf16),
            jax.ShapeDtypeStruct((4 * rows, columns), bf16),
            dealt,
            dealt,
        ),
        in_specs=[VMEM] * 3 + [HBM] * 2,
        out_specs=(VMEM,) * 3 + (HBM,) * 2,
        scratch_shapes=[
            pltpu.VMEM((rows, columns), bf16),
            pltpu.VMEM((3, rows, columns), bf16),
            pltpu.VMEM((3, rows, columns), bf16),
            pltpu.VMEM((rows, columns), f32),
            *pair(3, 4),
            *pair(3),
            *gather_scratch,
            *deal_scratch(4),
        ],
        compiler_params=params(5),
        cost_estimate=cost(1 << 29, 150),
        name="front_step",
    )(attended, weight, inputs, up, down)


def dot(spec, left, right, kind=f32):
    return jnp.einsum(spec, left, right, preferred_element_type=f32).astype(kind)


def rotary_tables(length, half_width):
    position = jnp.arange(length, dtype=f32)[:, None]
    frequency = jnp.exp(jnp.arange(half_width, dtype=f32) * (-math.log(10000.0) / half_width))
    angles = position * frequency[None, :]
    return (jnp.cos(angles), jnp.sin(angles))


def rotate(values, cos_table, sin_table):
    half_width = cos_table.shape[-1]
    first_half = values[..., :half_width]
    second_half = values[..., half_width:]
    return jnp.concatenate(
        [
            first_half * cos_table - second_half * sin_table,
            second_half * cos_table + first_half * sin_table,
        ],
        axis=-1,
    )


def pad_to(values, axis, size):
    widths = [(0, 0)] * values.ndim
    widths[axis] = (0, size - values.shape[axis])
    return jnp.pad(values, widths)


def visible_mask(offset, block_rows, prefix_len):
    query_pos = offset + jnp.arange(block_rows, dtype=jnp.int32)
    key_pos = jnp.arange(SEQ, dtype=jnp.int32)
    return (key_pos[None, :] <= query_pos[:, None]) | (key_pos[None, :] < prefix_len)


def attend_forward(queries, key_rows, value_rows, prefix_len):
    score_scale = (NOPE + ROPE) ** (-0.5)
    scores = dot("qd,kd->qk", queries, key_rows) * score_scale
    scores = jnp.where(visible_mask(0, SEQ, prefix_len), scores, masked_score)
    top_score = jnp.max(scores, axis=1, keepdims=True)
    exp_scores = jnp.exp(scores - top_score)
    row_total = jnp.sum(exp_scores, axis=1, keepdims=True)
    weights = (exp_scores / row_total).astype(bf16)
    result = dot("qk,kd->qd", weights, value_rows)
    return (result, (top_score + jnp.log(row_total))[:, 0])


def attend_backward(queries, key_rows, value_rows, log_total, out_grad, prefix_len):
    score_scale = (NOPE + ROPE) ** (-0.5)
    scores = dot("qd,kd->qk", queries, key_rows) * score_scale
    scores = jnp.where(visible_mask(0, SEQ, prefix_len), scores, masked_score)
    weights = jnp.exp(scores - log_total[:, None])
    value_grad = dot("qk,qd->kd", weights.astype(bf16), out_grad)
    weight_grad = dot("qd,kd->qk", out_grad, value_rows)
    centre = jnp.sum(weights * weight_grad, axis=1, keepdims=True)
    score_grad = (weights * (weight_grad - centre)).astype(bf16)
    query_grad = dot("qk,kd->qd", score_grad, key_rows) * score_scale
    key_grad = dot("qk,qd->kd", score_grad, queries) * score_scale
    return (query_grad, key_grad, value_grad)


def on_device(
    inputs,
    attention_gain,
    query_weight,
    latent_weight,
    latent_gain,
    expand_weight,
    output_weight,
    feedforward_gain,
    router_weight,
    shared_gate,
    shared_up,
    shared_down,
    expert_gate,
    expert_up,
    expert_down,
    routes,
    prefix,
    cotangent,
):
    row = lax.axis_index("row")
    col = lax.axis_index("col")
    prefix_len = prefix[0]
    cos_table, sin_table = rotary_tables(SEQ, ROPE // 2)
    first_gain = attention_gain.astype(f32)
    second_gain = feedforward_gain.astype(f32)
    compact_gain = latent_gain.astype(f32)
    residual_in = inputs.astype(f32)
    rows = inputs.shape[0]
    ff = expert_gate.shape[2]
    low = shared_down.shape[0] // 4

    gains = jnp.stack([attention_gain, feedforward_gain])
    common = jnp.concatenate([latent_weight.T, pad_to(gains, 0, 16)], axis=0)
    input_rows, out_grad, project_all, gates, lows = start_step(
        inputs,
        cotangent,
        common,
        query_weight.T,
        expert_gate.transpose(0, 2, 1),
        shared_gate.T,
        shared_up.T,
        pad_to(router_weight.T, 0, 16),
        shared_down,
    )
    project_weight = project_all[: RANK + 256]
    first_all = project_all[RANK + 256].astype(f32)
    second_all = project_all[RANK + 257].astype(f32)
    out_weight = jnp.concatenate(
        [lax.dynamic_slice_in_dim(output_weight, (col ^ k) * VDIM, VDIM, 0) for k in range(4)],
        axis=0,
    )
    order = col ^ jnp.arange(4, dtype=jnp.int32)

    input_rows = input_rows.astype(f32)
    scale_one = lax.rsqrt(jnp.mean(input_rows * input_rows, axis=1) + norm_eps)
    normed = (input_rows * scale_one[:, None] * first_all[None, :]).astype(bf16)
    projected = dot("td,qd->tq", normed, project_weight)
    content = projected[:, :RANK]
    latent_scale = lax.rsqrt(jnp.mean(content * content, axis=1) + norm_eps)
    compact = (content * latent_scale[:, None] * compact_gain[None, :]).astype(bf16)
    shared_key = rotate(projected[:, RANK + 192 :], cos_table, sin_table).astype(bf16)
    key_value = dot("tr,rk->tk", compact, expand_weight, bf16)
    query_rot = jnp.concatenate(
        [
            projected[:, RANK : RANK + NOPE],
            rotate(projected[:, RANK + NOPE : RANK + 192], cos_table, sin_table),
        ],
        axis=1,
    ).astype(bf16)
    key_rows = jnp.concatenate([key_value[:, :NOPE], shared_key], axis=1)
    value_rows = key_value[:, NOPE:]
    head_result, log_total = attend_forward(query_rot, key_rows, value_rows, prefix_len)
    residual_mid, middle_rows, attended_rows, ups, downs = front_step(
        head_result.astype(bf16), out_weight, inputs, expert_up.transpose(0, 2, 1), expert_down
    )

    experts = jnp.arange(EXPERTS, dtype=jnp.int32)
    named = jnp.any(routes.T[None, :, :] == experts[:, None, None], axis=1).astype(f32)
    mine = (experts[:, None] == 2 * col + jnp.arange(128, dtype=jnp.int32)[None, :]).astype(f32)
    hidden, scale_two, act, delta = expert_step(
        middle_rows, out_grad, gates, ups, downs, lows, second_all[None, :], named, mine
    )
    expert_grad = grads_step(hidden, out_grad, delta, act, ff)
    expert_sum = lax.psum_scatter(expert_grad, "dp", scatter_dimension=0, tiled=True)[0]
    act, delta, expert_grad = lax.optimization_barrier((act, delta, expert_grad))
    combined, hidden_grad = back_step(act, delta, gates, ups, downs, lows)
    shared_grad, router_part = shared_step(hidden, out_grad, delta, act, ff, low)

    my_scale_one = lax.dynamic_slice_in_dim(scale_one, row * rows, rows, 0)[:, None]
    my_scale_two = lax.dynamic_slice_in_dim(scale_two[:, :1], row * rows, rows, 0)
    residual_grad, residual_rows, attended_grad, second_gain_part, shared_sum, output = middle_step(
        hidden_grad,
        combined,
        residual_mid,
        cotangent,
        my_scale_two,
        second_gain[None, :],
        out_weight,
        shared_grad,
    )
    head_grad = dot("th,td->hd", attended_rows, residual_rows, bf16)
    output_weight_grad = head_grad.reshape(4, VDIM, 512)[order].reshape(4 * VDIM, 512)
    query_rot_grad, key_grad, value_grad = attend_backward(
        query_rot, key_rows, value_rows, log_total, attended_grad, prefix_len
    )
    pair_grad = jnp.concatenate([key_grad[:, :NOPE], value_grad], axis=1).astype(bf16)
    expand_part = dot("tk,tr->kr", pair_grad, compact, bf16)
    compact_grad = dot("tk,rk->tr", pair_grad, expand_weight)
    weighted_compact = compact_grad * compact_gain[None, :]
    inner_sum = jnp.sum(weighted_compact * content, axis=1)
    content_grad = (
        latent_scale[:, None] * weighted_compact
        - content * (latent_scale * latent_scale * latent_scale * inner_sum / RANK)[:, None]
    )
    latent_gain_part = jnp.sum(compact_grad * content * latent_scale[:, None], axis=0)
    project_grad = jnp.concatenate(
        [
            content_grad,
            query_rot_grad[:, :NOPE],
            rotate(query_rot_grad[:, NOPE:], cos_table, -sin_table),
            rotate(key_grad[:, NOPE:], cos_table, -sin_table),
        ],
        axis=1,
    ).astype(bf16)
    normed_grad = dot("tq,qd->td", project_grad, project_weight, bf16)
    project_part = dot("tq,td->qd", project_grad, normed, bf16)
    latent_part = jnp.concatenate([project_part[:RANK], project_part[RANK + 192 :]], axis=0)
    extra = jnp.concatenate(
        [
            jnp.tile(latent_gain_part.astype(bf16)[None, :], (1, 4)),
            router_part[:EXPERTS],
            jnp.zeros((7, D), bf16),
        ],
        axis=0,
    )
    tail = jnp.concatenate(
        [
            normed_grad.reshape(4, rows, D),
            latent_part.reshape(4, -1, D),
            jnp.broadcast_to(extra[None], (4, 16, D)),
        ],
        axis=1,
    )
    inputs_grad, sums, narrow, gains, latent_small, shared_all = tail_step(
        tail.reshape(-1, D),
        project_part[RANK : RANK + 192],
        jnp.concatenate([output_weight_grad, expand_part], axis=0),
        residual_grad,
        inputs,
        my_scale_one,
        first_gain[None, :],
        second_gain_part,
        shared_sum,
    )
    output_weight_grad = sums[:512].astype(f32)
    expand_grad = sums[512:768].T.astype(f32)
    query_weight_grad = sums[768:].T.astype(f32)
    latent_weight_grad = narrow.reshape(-1, 512).T.astype(f32)
    latent_gain_grad = latent_small[0, 0].astype(f32)
    router_grad = (
        lax.dynamic_index_in_dim(latent_small, col, 0, False)[1 : 1 + EXPERTS].T.astype(f32)
    )
    first_gain_grad, second_gain_grad = gains[0], gains[1]

    pairs = [
        (dp * 4 + c, (2 * c + dp // 4) * 4 + (c ^ (dp % 4))) for dp in range(8) for c in range(4)
    ]
    expert_sum = lax.ppermute(expert_sum, ("dp", "col"), pairs).astype(f32)
    expert_gate_grad = expert_sum[None, :ff].transpose(0, 2, 1)
    expert_up_grad = expert_sum[None, ff : 2 * ff].transpose(0, 2, 1)
    expert_down_grad = expert_sum[None, 2 * ff :]
    shared_sum = shared_all[order].astype(f32)
    shared_gate_grad = shared_sum[:, :low].reshape(4 * low, 512).T
    shared_up_grad = shared_sum[:, low : 2 * low].reshape(4 * low, 512).T
    shared_down_grad = shared_sum[:, 2 * low :].reshape(4 * low, 512)
    return (
        output,
        inputs_grad,
        first_gain_grad,
        query_weight_grad,
        latent_weight_grad,
        latent_gain_grad,
        expand_grad,
        output_weight_grad,
        second_gain_grad,
        router_grad,
        shared_gate_grad,
        shared_up_grad,
        shared_down_grad,
        expert_gate_grad,
        expert_up_grad,
        expert_down_grad,
    )


def solution(mesh):
    placed = (
        P(("dp", "row"), "col"),
        P("col"),
        P("col", "row"),
        P("col", None),
        P(),
        P(None, ("row", "col")),
        P("row", "col"),
        P("col"),
        P("col", None),
        P("col", "row"),
        P("col", "row"),
        P("row", "col"),
        P(None, "col", "row"),
        P(None, "col", "row"),
        P(None, "row", "col"),
        P("dp", None),
        P("dp"),
        P(("dp", "row"), "col"),
    )
    return jax.shard_map(
        on_device,
        mesh=mesh,
        in_specs=placed,
        out_specs=(
            P(("dp", "row"), "col"),
            P(("dp", "row"), "col"),
            P("col"),
            P("col", "row"),
            P("col", None),
            P(),
            P(None, ("row", "col")),
            P("row", "col"),
            P("col"),
            P("col", None),
            P("col", "row"),
            P("col", "row"),
            P("row", "col"),
            P("dp", "col", "row"),
            P("dp", "col", "row"),
            P("dp", "row", "col"),
        ),
        check_vma=False,
    )
```

```python
import functools
import math

import jax
import jax.numpy as jnp
from jax import lax
from jax.experimental import pallas as pl
from jax.experimental.pallas import tpu as pltpu
from jax.sharding import PartitionSpec as P

D = 2048
NOPE = 128
ROPE = 64
VDIM = 128
RANK = 512
TOPK = 6
EXPERTS = 8
SEQ = 1024

norm_eps = 1e-06
masked_score = -1e30
bf16 = jnp.bfloat16
f32 = jnp.float32
MESH = pl.DeviceIdType.MESH
DMA = pltpu.SemaphoreType.DMA
VMEM = pl.BlockSpec(memory_space=pltpu.VMEM)
HBM = pl.BlockSpec(memory_space=pl.ANY)


def place():
    row = lax.axis_index("row")
    col = lax.axis_index("col")
    sibling = col + 1 - 2 * lax.rem(col, 2)
    across = lax.rem(col + 2, 4)
    return (row, sibling, across, lax.rem(sibling + 2, 4))


def greet(columns, row, others=()):
    barrier = pltpu.get_barrier_semaphore()
    targets = [{"col": column} for column in columns]
    targets += [{"row": lax.rem(row + step, 4)} for step in (1, 2, 3)]
    targets += list(others)
    for target in targets:
        pl.semaphore_signal(barrier, inc=1, device_id=target, device_id_type=MESH)
    pl.semaphore_wait(barrier, len(targets))


def along_z(dp, step):
    return dp // 4 * 4 + lax.rem(lax.rem(dp, 4) + step, 4)


def remote(source, target, sems, at, **device):
    return pltpu.make_async_remote_copy(
        src_ref=source,
        dst_ref=target,
        send_sem=sems[0].at[at],
        recv_sem=sems[1].at[at],
        device_id=device,
        device_id_type=MESH,
    )


def starter(pending):
    def go(*arguments, **device):
        copy = remote(*arguments, **device)
        copy.start()
        pending.append(copy)
        return copy

    return go


def pair(*shape):
    return [DMA(shape), DMA(shape)]


def params(collective):
    return pltpu.CompilerParams(
        collective_id=collective, has_side_effects=True, vmem_limit_bytes=52 << 20
    )


def cost(flops, mebibytes):
    return pl.CostEstimate(flops=flops, bytes_accessed=mebibytes << 20, transcendentals=0)


class Gather:
    def __init__(self, own, full, sems, go, row, sibling, across):
        self.own, self.full, self.go = own, full, go
        self.xs, self.ys, self.cs = sems[0:2], sems[2:4], sems[4:6]
        self.row, self.sibling, self.across = row, sibling, across
        self.arrivals = []

    def block(self, at_row, at_col):
        rows, columns = self.own.shape
        start = pl.multiple_of(at_row * rows, rows)
        return self.full.at[pl.ds(start, rows), pl.ds(at_col * columns, columns)]

    def along(self, source, target, base):
        return [
            self.go(source, target, self.ys, base + k - 1, row=lax.rem(self.row + k, 4))
            for k in (1, 2, 3)
        ]

    def over(self, source, target):
        count = len(self.arrivals)
        self.arrivals.append(self.go(source, target, self.cs, count, col=self.sibling))

    def begin(self):
        row = self.row
        rows, columns = self.own.shape
        self.side = self.go(self.own, self.block(row, 2), self.xs, 0, col=self.across)
        self.first = self.along(self.own, self.block(row, 0), 0)
        self.over(self.own, self.block(row, 1))
        start = pl.multiple_of(row * rows, rows)
        self.full[pl.ds(start, rows), pl.ds(0, columns)] = self.own[...]

    def second(self):
        self.side.wait_recv()
        here = self.block(self.row, 2)
        self.rest = self.along(here, here, 3)
        self.over(here, self.block(self.row, 3))

    def forward(self, group, at_col):
        for k in (1, 3, 2):
            group[k - 1].wait_recv()
            source = lax.rem(self.row + 4 - k, 4)
            self.over(self.block(source, at_col), self.block(source, at_col + 1))

    def forward_first(self):
        self.forward(self.first, 0)

    def forward_rest(self):
        self.forward(self.rest, 2)

    def finish(self):
        for copy in self.arrivals:
            copy.wait_recv()


gather_scratch = pair(1) + pair(6) + pair(8)


class Deal:
    def __init__(self, sems, local_sems, pending, col, peers):
        self.go, self.sems, self.local_sems = starter(pending), sems, local_sems
        self.col, self.peers = col, peers
        self.far = lax.rem(lax.axis_index("dp") + 4, 8)
        self.copies, self.local, self.count = [], [], 0

    def send(self, source, target, flip):
        n = self.count
        self.count += 1
        copy = pltpu.make_async_copy(source(self.col), target(0), self.local_sems.at[n])
        copy.start()
        self.local.append(copy)
        for k, peer in ((2, self.peers[1]), (3, self.peers[2]), (1, self.peers[0])):
            place_at = {"col": peer}
            if flip and k != 1:
                place_at["dp"] = self.far
            self.copies.append(
                self.go(source(peer), target(k), self.sems, (k - 1, n), **place_at)
            )

    def finish(self):
        for copy in self.local:
            copy.wait()
        for copy in self.copies:
            copy.wait_recv()


def deal_scratch(count):
    return pair(3, count) + [DMA((count,))]


def deal_peers(peers):
    far = lax.rem(lax.axis_index("dp") + 4, 8)
    return [{"dp": far, "col": peer} for peer in peers[1:]]


def lanes(array, start, size):
    return lambda k: array.at[pl.ds(start, size), pl.ds(512 * k, 512)]


def rows_at(array, size):
    return lambda column: array.at[pl.ds(pl.multiple_of(column * size, size), size)]


def start_kernel(
    inputs, cotangent, common, query, gate, low_gate, low_up, router, low_down,
    full, out_grad, project, gates, lows, *sems,
):
    row, sibling, across, corner = place()
    col = lax.axis_index("col")
    peers = (sibling, across, corner)
    greet(peers, row, deal_peers(peers))
    pending = []
    go = starter(pending)
    gather = Gather(inputs, full, sems[0:6], go, row, sibling, across)
    beside = Gather(cotangent, out_grad, sems[6:12], go, row, sibling, across)
    deal = Deal(sems[12:14], sems[14], pending, col, peers)
    ff = gate.shape[1]
    low = low_down.shape[0] // 4
    gather.begin()
    deal.send(lambda column: common.at[pl.ds(0, RANK)], lanes(project, 0, RANK), True)
    deal.send(rows_at(query, 192), lanes(project, RANK, 192), False)
    deal.send(lambda column: common.at[pl.ds(RANK, 80)], lanes(project, RANK + 192, 80), False)
    beside.begin()
    gather.second()
    for e in (0, 1):
        deal.send(lambda column, e=e: gate.at[2 * column + e], lanes(gates, e * ff, ff), e == 1)
    beside.second()
    deal.send(rows_at(low_gate, low), lanes(lows, 0, low), True)
    deal.send(rows_at(low_up, low), lanes(lows, low, low), False)
    deal.send(lambda column: router, lanes(lows, 2 * low, 16), True)
    deal.send(rows_at(low_down, low), lanes(lows, 2 * low + 16, low), True)
    gather.forward_first()
    gather.forward_rest()
    beside.forward_first()
    beside.forward_rest()
    gather.finish()
    beside.finish()
    deal.finish()
    for copy in pending:
        copy.wait_send()


def start_step(inputs, cotangent, common, query, gate, low_gate, low_up, router, low_down):
    rows, columns = inputs.shape
    low = low_down.shape[0] // 4
    wide = jax.ShapeDtypeStruct((4 * rows, 4 * columns), bf16)
    return pl.pallas_call(
        start_kernel,
        out_shape=(
            wide,
            wide,
            jax.ShapeDtypeStruct((RANK + 272, 4 * columns), bf16),
            jax.ShapeDtypeStruct((2 * gate.shape[1], 4 * columns), bf16),
            jax.ShapeDtypeStruct((3 * low + 16, 4 * columns), bf16),
        ),
        in_specs=[VMEM] * 2 + [HBM] * 7,
        out_specs=(VMEM, VMEM, HBM, HBM, HBM),
        scratch_shapes=[*gather_scratch, *gather_scratch, *deal_scratch(9)],
        compiler_params=params(0),
        cost_estimate=cost(0, 150),
        name="start_step",
    )(inputs, cotangent, common, query, gate, low_gate, low_up, router, low_down)


def reduce_scratch(rows, columns):
    return [
        pltpu.VMEM((4, 2, rows, columns), bf16),
        pltpu.VMEM((3, 2, rows, columns), bf16),
        pltpu.VMEM((3, 2, rows, columns), bf16),
        pltpu.VMEM((2, rows, columns), f32),
        pltpu.VMEM((2, rows, columns), bf16),
        *pair(1),
        *pair(3, 2),
        *pair(4, 2),
    ]


class Reduction:
    order = (2, 1, 3, 0)

    def __init__(self, part, scratch, row, sibling, across):
        self.part = part
        self.held, self.out_buf, self.in_buf, self.acc, self.side_buf = scratch[:5]
        self.xs, self.ys, self.cs = scratch[5:7], scratch[7:9], scratch[9:11]
        self.row, self.sibling, self.across = row, sibling, across
        self.rows, self.columns = self.acc.shape[1:]

    def rows_of(self, k):
        start = lax.rem(self.row + k, 4) * self.rows
        return pl.ds(pl.multiple_of(start, self.rows), self.rows)

    def pair_copy(self, k, x):
        return remote(
            self.part.at[self.rows_of(k), pl.ds((2 * x + 1) * self.columns, self.columns)],
            self.held.at[k, x],
            self.cs,
            (k, x),
            col=self.sibling,
        )

    def along_copy(self, k, x):
        return remote(
            self.out_buf.at[k - 1, x],
            self.in_buf.at[k - 1, x],
            self.ys,
            (k - 1, x),
            row=lax.rem(self.row + k, 4),
        )

    def side_copy(self):
        return remote(self.side_buf.at[0], self.side_buf.at[1], self.xs, 0, col=self.across)

    def start(self):
        for x in (1, 0):
            for k in self.order:
                self.pair_copy(k, x).start()

    def along_one(self, k, x):
        self.pair_copy(k, x).wait_recv()
        mine = self.part[self.rows_of(k), pl.ds(2 * x * self.columns, self.columns)]
        value = mine.astype(f32) + self.held[k, x].astype(f32)
        if k:
            self.out_buf[k - 1, x] = value.astype(bf16)
            self.along_copy(k, x).start()
        else:
            self.acc[x] = value

    def along(self):
        for x in (1, 0):
            for k in self.order:
                self.along_one(k, x)

    def collect(self, x):
        for k in (1, 3, 2):
            self.along_copy(k, x).wait_recv()
            self.acc[x] += self.in_buf[k - 1, x].astype(f32)

    def over(self):
        self.collect(1)
        self.side_buf[0] = self.acc[1].astype(bf16)
        self.side_copy().start()

    def side(self):
        self.over()
        self.collect(0)

    def total(self):
        self.side_copy().wait_recv()
        return self.acc[0] + self.side_buf[1].astype(f32)

    def finish(self):
        for k in self.order:
            for x in (0, 1):
                self.pair_copy(k, x).wait_send()
                if k:
                    self.along_copy(k, x).wait_send()
        self.side_copy().wait_send()


def product(left, right):
    return jnp.dot(left, right, preferred_element_type=f32).astype(bf16)


def times_rows(left, right):
    return lax.dot_general(left, right, (((1,), (1,)), ((), ())), preferred_element_type=f32)


def over_units(left, right):
    return lax.dot_general(left, right, (((0,), (0,)), ((), ())), preferred_element_type=f32)


def expert_kernel(
    middle, out_grad, gates, ups, downs, lows, gain, named, mine,
    hidden, scale, act, delta, combined,
):
    values = middle[...].astype(f32)
    scales = lax.rsqrt(jnp.mean(values * values, axis=1, keepdims=True) + norm_eps)
    scale[...] = jnp.broadcast_to(scales, scale.shape)
    normal = (values * scales * gain[...]).astype(bf16)
    hidden[...] = normal
    upstream = out_grad[...]
    ff = gates.shape[0] // 2
    low = (lows.shape[0] - 16) // 3
    low_pre = times_rows(lows[pl.ds(0, 2 * low + 16), :], normal)
    logits = low_pre[2 * low : 2 * low + EXPERTS]
    powers = jnp.exp(logits - jnp.max(logits, axis=0, keepdims=True))
    probs = powers / jnp.sum(powers, axis=0, keepdims=True)
    names = named[...]
    probs_part = jnp.zeros_like(probs)
    for e in range(3):
        if e < 2:
            size, at = ff, pl.ds(e * ff, ff)
            gate_pre = times_rows(gates[at, :], normal)
            up_pre = times_rows(ups[at, :], normal)
            act_grad = times_rows(downs[at, :], upstream)
            own = mine[:, e : e + 1]
            weight = jnp.sum(probs * names * own, axis=0, keepdims=True)
            gate_at, up_at, act_at = e * ff, (2 + e) * ff, e * ff
        else:
            size = low
            gate_pre, up_pre = low_pre[:low], low_pre[low : 2 * low]
            act_grad = times_rows(lows[pl.ds(2 * low + 16, low), :], upstream)
            weight = 1.0
            gate_at, up_at, act_at = 4 * ff, 4 * ff + low, 2 * ff
        sig = 1.0 / (1.0 + jnp.exp(-gate_pre))
        silu = gate_pre * sig
        both = silu * up_pre
        act[pl.ds(act_at, size), :] = (weight * both).astype(bf16)
        weighted = weight * act_grad
        delta[pl.ds(gate_at, size), :] = (
            weighted * up_pre * (sig * (1.0 + gate_pre * (1.0 - sig)))
        ).astype(bf16)
        delta[pl.ds(up_at, size), :] = (weighted * silu).astype(bf16)
        if e < 2:
            named_sum = jnp.sum(act_grad * both, axis=0, keepdims=True)
            probs_part = probs_part + named_sum * own * names
    logits_part = probs * (probs_part - jnp.sum(probs * probs_part, axis=0, keepdims=True))
    delta[pl.ds(4 * ff + 2 * low, 16), :] = jnp.concatenate(
        [logits_part, jnp.zeros_like(logits_part)], axis=0
    ).astype(bf16)
    combined[...] = (
        over_units(act[pl.ds(0, 2 * ff), :], downs[...])
        + over_units(act[pl.ds(2 * ff, low), :], lows[pl.ds(2 * low + 16, low), :])
    ).astype(bf16)


def whole(value):
    return pl.BlockSpec(value.shape, lambda i: (0,) * len(value.shape))


def expert_step(middle, out_grad, gates, ups, downs, lows, gain, named, mine):
    tile = 256
    tokens, width = middle.shape
    wide = pl.BlockSpec((tile, width), lambda i: (i, 0))

    def tall(rows):
        return pl.BlockSpec((rows, tile), lambda i: (0, i))

    acts = downs.shape[0] + (lows.shape[0] - 16) // 3
    deltas = gates.shape[0] + ups.shape[0] + 2 * (lows.shape[0] - 16) // 3 + 16
    return pl.pallas_call(
        expert_kernel,
        grid=(tokens // tile,),
        out_shape=(
            jax.ShapeDtypeStruct((tokens, width), bf16),
            jax.ShapeDtypeStruct((tokens, 128), f32),
            jax.ShapeDtypeStruct((acts, tokens), bf16),
            jax.ShapeDtypeStruct((deltas, tokens), bf16),
            jax.ShapeDtypeStruct((tokens, width), bf16),
        ),
        in_specs=[
            wide,
            wide,
            whole(gates),
            whole(ups),
            whole(downs),
            whole(lows),
            whole(gain),
            tall(EXPERTS),
            whole(mine),
        ],
        out_specs=(
            wide,
            pl.BlockSpec((tile, 128), lambda i: (i, 0)),
            tall(acts),
            tall(deltas),
            wide,
        ),
        compiler_params=pltpu.CompilerParams(vmem_limit_bytes=56 << 20),
        cost_estimate=cost(2 * 5 * gates.shape[0] * width * tokens, 30),
        name="expert_step",
    )(middle, out_grad, gates, ups, downs, lows, gain, named, mine)


def back_kernel(delta, gates, ups, lows, hidden_grad):
    ff = gates.shape[0]
    low = lows.shape[0] - 16 - (lows.shape[0] - 16) // 3 + 16
    hidden_grad[...] = (
        over_units(delta[pl.ds(0, ff), :], gates[...])
        + over_units(delta[pl.ds(ff, ff), :], ups[...])
        + over_units(delta[pl.ds(2 * ff, low), :], lows[pl.ds(0, low), :])
    ).astype(bf16)


def back_step(delta, gates, ups, lows):
    tile = 256
    tokens, width = delta.shape[1], gates.shape[1]
    return pl.pallas_call(
        back_kernel,
        grid=(tokens // tile,),
        out_shape=jax.ShapeDtypeStruct((tokens, width), bf16),
        in_specs=[
            pl.BlockSpec((delta.shape[0], tile), lambda i: (0, i)),
            whole(gates),
            whole(ups),
            whole(lows),
        ],
        out_specs=pl.BlockSpec((tile, width), lambda i: (i, 0)),
        compiler_params=pltpu.CompilerParams(vmem_limit_bytes=56 << 20),
        cost_estimate=cost(2 * 3 * gates.shape[0] * width * tokens, 30),
        name="back_step",
    )(delta, gates, ups, lows)


def grads_kernel(
    hidden, out_grad, delta, act, combined, grads, shared, router, total,
    own_shared, chunk_in, ps, pr, *scratch, ff, low,
):
    step = pl.program_id(0)
    row, sibling, across, corner = place()
    dp = lax.axis_index("dp")
    z = lax.rem(dp, 4)
    steps = Reduction(combined, scratch, row, sibling, across)
    piece = shared.shape[1]

    def quarter(at):
        return pl.ds(pl.multiple_of(at * piece, piece), piece)

    def scattered(k):
        return remote(
            own_shared.at[:, quarter(lax.rem(z + k, 4))],
            chunk_in.at[k - 1],
            (ps, pr),
            k - 1,
            dp=along_z(dp, k),
        )

    @pl.when(step == 0)
    def _():
        greet((sibling, across), row, [{"dp": along_z(dp, k)} for k in (1, 2, 3)])
        steps.start()

    for at, blocks in (
        (1, ((2, 1), (1, 1), (3, 1))),
        (2, ((0, 1), (2, 0), (1, 0))),
        (3, ((3, 0), (0, 0))),
    ):

        @pl.when(step == at)
        def _(blocks=blocks):
            for k, x in blocks:
                steps.along_one(k, x)

    @pl.when(step == 8)
    def _():
        steps.over()

    for k in range(4):

        @pl.when(step == k)
        def _(k=k):
            base = 4 * ff
            own_shared[k, pl.ds(0, low), :] = product(delta[pl.ds(base, low), :], hidden[...])
            own_shared[k, pl.ds(low, low), :] = product(
                delta[pl.ds(base + low, low), :], hidden[...]
            )
            router[...] = product(delta[pl.ds(base + 2 * low, 16), :], hidden[...])
            own_shared[k, pl.ds(2 * low, low), :] = product(
                act[pl.ds(2 * ff, low), :], out_grad[...]
            )
            spare = 4 * piece - 3 * low
            own_shared[k, pl.ds(3 * low, spare), :] = jnp.zeros((spare, 512), bf16)

    @pl.when(step == 3)
    def _():
        for k in (1, 2, 3):
            scattered(k).start()

    for e in (0, 1):

        @pl.when(step // 4 == e + 1)
        def _(e=e):
            at = e * ff
            grads[0, pl.ds(0, ff), :] = product(delta[pl.ds(at, ff), :], hidden[...])
            grads[0, pl.ds(ff, ff), :] = product(delta[pl.ds(2 * ff + at, ff), :], hidden[...])
            grads[0, pl.ds(2 * ff, ff), :] = product(act[pl.ds(at, ff), :], out_grad[...])

    @pl.when(step == 11)
    def _():
        steps.collect(0)
        total[...] = steps.total()
        summed = own_shared[:, quarter(z), :].astype(f32)
        for k in (1, 2, 3):
            scattered(k).wait_recv()
            summed += chunk_in[k - 1].astype(f32)
        shared[...] = summed.astype(bf16)
        for k in (1, 2, 3):
            scattered(k).wait_send()
        steps.finish()


def grads_step(hidden, out_grad, delta, act, combined, ff, low):
    tokens = hidden.shape[0]
    piece = -(-3 * low // 64) * 16
    wide = pl.BlockSpec((tokens, 512), lambda i: (0, i % 4))
    return pl.pallas_call(
        functools.partial(grads_kernel, ff=ff, low=low),
        grid=(12,),
        out_shape=(
            jax.ShapeDtypeStruct((8, 3 * ff, 512), bf16),
            jax.ShapeDtypeStruct((4, piece, 512), bf16),
            jax.ShapeDtypeStruct((16, D), bf16),
            jax.ShapeDtypeStruct((tokens // 4, 512), f32),
        ),
        in_specs=[wide, wide, whole(delta), whole(act), whole(combined)],
        out_specs=(
            pl.BlockSpec((1, 3 * ff, 512), lambda i: (jnp.maximum(i - 4, 0), 0, 0)),
            pl.BlockSpec((4, piece, 512), lambda i: (0, 0, 0)),
            pl.BlockSpec((16, 512), lambda i: (0, jnp.minimum(i, 3))),
            pl.BlockSpec((tokens // 4, 512), lambda i: (0, 0)),
        ),
        scratch_shapes=[
            pltpu.VMEM((4, 4 * piece, 512), bf16),
            pltpu.VMEM((3, 4, piece, 512), bf16),
            *pair(3),
            *reduce_scratch(tokens // 4, 512),
        ],
        compiler_params=params(1),
        cost_estimate=cost(2 * 8 * 4 * ff * 512 * tokens, 60),
        name="grads_step",
    )(hidden, out_grad, delta, act, combined)


class ColumnSum:
    def __init__(self, value, buf, sems, go, peers):
        self.buf = buf
        buf[0] = jnp.broadcast_to(value, (value.shape[0], 128)).T[:8]
        self.sent = [
            go(buf.at[0], buf.at[k + 1], sems, k, col=peer) for k, peer in enumerate(peers)
        ]

    def total(self):
        for copy in self.sent:
            copy.wait_recv()
        buf = self.buf
        total = (buf[0] + buf[1]) + (buf[2] + buf[3])
        return jnp.broadcast_to(total[:1], (128, total.shape[1])).T[:, :1]


def middle_kernel(
    part, middle, cotangent, scale, gain, weight, shared,
    residual_grad, residual_rows, attended_grad, gain_part, shared_all,
    sum_buf, out_buf, in_buf, acc, chunk_in, both, ss, sr, rs, rr, hs, hr, ps, pr, *scratch,
):
    row, sibling, across, corner = place()
    dp = lax.axis_index("dp")
    z = lax.rem(dp, 4)
    far = lax.rem(dp + 4, 8)
    peers = (sibling, across, corner)
    greet(peers, row, [{"dp": along_z(dp, k)} for k in (1, 2, 3)] + [{"dp": far}])
    pending = []
    go = starter(pending)
    steps = Reduction(part, scratch, row, sibling, across)
    rows, columns = middle.shape
    head = attended_grad.shape[1]
    steps.start()
    halves = go(shared, chunk_in, (ps, pr), 0, dp=far)
    steps.along()
    steps.over()
    halves.wait_recv()
    both[...] = (shared[...].astype(f32) + chunk_in[...].astype(f32)).astype(bf16)
    shared_all[z, 0] = both[0]
    home = [
        go(both.at[j + 1], shared_all.at[z, j + 1], (ps, pr), 1 + j, col=peer)
        for j, peer in enumerate(peers)
    ]
    steps.collect(0)
    upstream = steps.total()
    weighted = upstream * gain[...]
    values = middle[...]
    scales = scale[...]
    inner = ColumnSum(
        jnp.sum(weighted * values, axis=1, keepdims=True), sum_buf, (ss, sr), go, peers
    )
    gain_part[...] = jnp.sum(upstream * values * scales, axis=0, keepdims=True)
    for copy in home:
        copy.wait_recv()
    spread = [
        go(shared_all.at[z], shared_all.at[z], (ps, pr), 3 + k, dp=along_z(dp, k))
        for k in (1, 2, 3)
    ]
    base = cotangent[...].astype(f32) + scales * weighted
    grad = base - values * (scales * scales * scales * inner.total() / D)
    residual_grad[...] = grad

    def block(at_row):
        return pl.ds(pl.multiple_of(at_row * rows, rows), rows)

    residual_rows[block(row), :] = grad.astype(bf16)
    sent = [
        go(
            residual_rows.at[block(row)],
            residual_rows.at[block(row)],
            (rs, rr),
            k - 1,
            row=lax.rem(row + k, 4),
        )
        for k in (1, 2, 3)
    ]
    got = []
    for k in (0, 1, 3, 2):
        source = lax.rem(row + 4 - k, 4)
        if k:
            sent[k - 1].wait_recv()
        result = times_rows(residual_rows[block(source), :], weight[...])
        acc[block(source), :] = result[:, :head]
        for j, peer in enumerate(peers):
            out_buf[j, block(source), :] = result[:, (j + 1) * head : (j + 2) * head].astype(bf16)
            got.append(
                go(
                    out_buf.at[j, block(source)],
                    in_buf.at[j, block(source)],
                    (hs, hr),
                    (j, k),
                    col=peer,
                )
            )
    for copy in got:
        copy.wait_recv()
    attended_grad[...] = (
        acc[...] + in_buf[0].astype(f32) + in_buf[1].astype(f32) + in_buf[2].astype(f32)
    ).astype(bf16)
    for copy in spread:
        copy.wait_recv()
    for copy in pending:
        copy.wait_send()
    steps.finish()


def middle_step(part, middle, cotangent, scale, gain, weight, shared):
    rows, columns = middle.shape
    piece = shared.shape[1]
    return pl.pallas_call(
        middle_kernel,
        out_shape=(
            jax.ShapeDtypeStruct((rows, columns), f32),
            jax.ShapeDtypeStruct((4 * rows, columns), bf16),
            jax.ShapeDtypeStruct((4 * rows, VDIM), bf16),
            jax.ShapeDtypeStruct((1, columns), f32),
            jax.ShapeDtypeStruct((4, 4, piece, columns), bf16),
        ),
        in_specs=[VMEM] * 7,
        out_specs=(VMEM,) * 5,
        scratch_shapes=[
            pltpu.VMEM((4, 8, rows), f32),
            pltpu.VMEM((3, 4 * rows, VDIM), bf16),
            pltpu.VMEM((3, 4 * rows, VDIM), bf16),
            pltpu.VMEM((4 * rows, VDIM), f32),
            pltpu.VMEM((4, piece, columns), bf16),
            pltpu.VMEM((4, piece, columns), bf16),
            *pair(3),
            *pair(3),
            *pair(3, 4),
            *pair(7),
            *reduce_scratch(rows, columns),
        ],
        compiler_params=params(3),
        cost_estimate=cost(1 << 29, 200),
        name="middle_step",
    )(part, middle, cotangent, scale, gain, weight, shared)


def tail_kernel(
    part, narrow_part, query, ready, residual_grad, inputs, scale, gain, gain_part,
    inputs_grad, sums, narrow, gains, latent_gain,
    chunk_in, all_parts, narrow_all, lat_buf, lat_half, sum_buf,
    qs, qr, ps, pr, as_, ar, ls, lr, ns, nr, ss, sr, gs, gr, *scratch,
):
    row, sibling, across, corner = place()
    col = lax.axis_index("col")
    dp = lax.axis_index("dp")
    z = lax.rem(dp, 4)
    far = lax.rem(dp + 4, 8)
    peers = (sibling, across, corner)
    greet(peers, row, [{"dp": along_z(dp, k)} for k in (1, 2, 3)] + [{"dp": far}])
    pending = []
    go = starter(pending)
    count = len(scratch) // 2
    steps = Reduction(part, scratch[:count], row, sibling, across)
    before = Reduction(narrow_part, scratch[count:], row, sibling, across)
    rows, columns = inputs.shape
    piece = query.shape[0]
    lat = narrow_all.shape[1]
    keep = lat - 32

    def head(at):
        return pl.ds(pl.multiple_of(at * piece, piece), piece)

    def chunk(at):
        return pl.ds(pl.multiple_of(at * 2 * piece, 2 * piece), 2 * piece)

    before.start()
    dealt = [
        go(
            query.at[:, pl.ds((j + 1) * columns, columns)],
            all_parts.at[head(4 + col)],
            (qs, qr),
            j,
            col=peer,
        )
        for j, peer in enumerate(peers)
    ]
    steps.start()
    all_parts[pl.ds(0, 4 * piece), :] = ready[...]
    all_parts[head(4 + col), :] = query[:, pl.ds(0, columns)]
    before.along()
    for copy in dealt:
        copy.wait_recv()
    scattered = [
        go(
            all_parts.at[chunk(lax.rem(z + k, 4))],
            chunk_in.at[k - 1],
            (ps, pr),
            k - 1,
            dp=along_z(dp, k),
        )
        for k in (1, 2, 3)
    ]
    steps.along()
    before.side()
    lat_buf[z] = jnp.concatenate(
        [before.total(), gain_part[...], jnp.zeros((15, columns), f32)], axis=0
    ).astype(bf16)
    along = [
        go(lat_buf.at[z], lat_buf.at[z], (ls, lr), k - 1, dp=along_z(dp, k)) for k in (1, 2, 3)
    ]
    total = all_parts[chunk(z), :].astype(f32)
    for k in (1, 2, 3):
        scattered[k - 1].wait_recv()
        total += chunk_in[k - 1].astype(f32)
    chunk_in[3] = total.astype(bf16)
    halves = go(chunk_in.at[3], chunk_in.at[4], (ps, pr), 3, dp=far)
    steps.over()
    for copy in along:
        copy.wait_recv()
    lat_half[0] = (
        (lat_buf[0].astype(f32) + lat_buf[1].astype(f32))
        + (lat_buf[2].astype(f32) + lat_buf[3].astype(f32))
    ).astype(bf16)
    other = go(lat_half.at[0], lat_half.at[1], (ls, lr), 3, dp=far)
    steps.collect(0)
    halves.wait_recv()
    sums[chunk(z), :] = (chunk_in[3].astype(f32) + chunk_in[4].astype(f32)).astype(bf16)
    shared = [
        go(sums.at[chunk(z)], sums.at[chunk(z)], (as_, ar), k - 1, dp=along_z(dp, k))
        for k in (1, 2, 3)
    ]
    upstream = steps.total()
    weighted = upstream * gain[...]
    values = inputs[...].astype(f32)
    scales = scale[...]
    inner = ColumnSum(
        jnp.sum(weighted * values, axis=1, keepdims=True), sum_buf, (ss, sr), go, peers
    )
    other.wait_recv()
    narrow_all[row] = (lat_half[0].astype(f32) + lat_half[1].astype(f32)).astype(bf16)
    spread = [
        go(narrow_all.at[row], narrow_all.at[row], (ns, nr), k - 1, row=lax.rem(row + k, 4))
        for k in (1, 2, 3)
    ]
    inputs_grad[...] = (
        residual_grad[...]
        + scales * weighted
        - values * (scales * scales * scales * inner.total() / D)
    ).astype(bf16)
    for copy in spread:
        copy.wait_recv()
    narrow[...] = narrow_all[:, :keep, :]
    latent_gain[col] = narrow_all[0, pl.ds(keep, 16), :]
    last = [
        go(latent_gain.at[col], latent_gain.at[col], (gs, gr), j, col=peer)
        for j, peer in enumerate(peers)
    ]
    edge = pl.ds(keep + 16, 16)
    gains[...] = (
        narrow_all[0, edge, :].astype(f32)
        + narrow_all[1, edge, :].astype(f32)
        + narrow_all[2, edge, :].astype(f32)
        + narrow_all[3, edge, :].astype(f32)
    )
    for copy in last + shared:
        copy.wait_recv()
    for copy in pending:
        copy.wait_send()
    steps.finish()
    before.finish()


def tail_step(
    part, narrow_part, query, ready, residual_grad, inputs, scale, gain, gain_part
):
    rows, columns = inputs.shape
    piece = query.shape[0]
    narrow_rows = narrow_part.shape[0] // 4
    lat = narrow_rows + 16
    return pl.pallas_call(
        tail_kernel,
        out_shape=(
            jax.ShapeDtypeStruct((rows, columns), bf16),
            jax.ShapeDtypeStruct((8 * piece, columns), bf16),
            jax.ShapeDtypeStruct((4, lat - 32, columns), bf16),
            jax.ShapeDtypeStruct((16, columns), f32),
            jax.ShapeDtypeStruct((4, 16, columns), bf16),
        ),
        in_specs=[VMEM] * 9,
        out_specs=(VMEM,) * 5,
        scratch_shapes=[
            pltpu.VMEM((5, 2 * piece, columns), bf16),
            pltpu.VMEM((8 * piece, columns), bf16),
            pltpu.VMEM((4, lat, columns), bf16),
            pltpu.VMEM((4, lat, columns), bf16),
            pltpu.VMEM((2, lat, columns), bf16),
            pltpu.VMEM((4, 8, rows), f32),
            *pair(3),
            *pair(4),
            *pair(3),
            *pair(4),
            *pair(3),
            *pair(3),
            *pair(3),
            *reduce_scratch(rows, columns),
            *reduce_scratch(narrow_rows, columns),
        ],
        compiler_params=params(4),
        cost_estimate=cost(1 << 20, 200),
        name="tail_step",
    )(part, narrow_part, query, ready, residual_grad, inputs, scale, gain, gain_part)


def front_kernel(
    attended, weight, inputs, up, down, middle, full, attended_rows, ups, downs,
    own, out_buf, in_buf, acc, as_, ar, ps, pr, *sems,
):
    row, sibling, across, corner = place()
    peers = (sibling, across, corner)
    greet(peers, row, deal_peers(peers))
    pending = []
    go = starter(pending)
    rows, columns = inputs.shape
    head = attended.shape[1]
    order = (2, 1, 3, 0)

    def block(k):
        return pl.ds(pl.multiple_of(lax.rem(row + k, 4) * rows, rows), rows)

    def slot(k):
        return pl.ds(k * head, head)

    got = {}
    for k in order:
        got[2, k] = go(
            attended.at[block(k)], attended_rows.at[block(k), slot(2)], (as_, ar), (1, k), col=across
        )
    for k in order:
        got[1, k] = go(
            attended.at[block(k)], attended_rows.at[block(k), slot(1)], (as_, ar), (0, k), col=sibling
        )
    attended_rows[:, slot(0)] = attended[...]
    deal = Deal(sems[6:8], sems[8], pending, lax.axis_index("col"), peers)
    ff = up.shape[1]
    for k in order:
        got[2, k].wait_recv()
        view = attended_rows.at[block(k), slot(2)]
        got[3, k] = go(
            view, attended_rows.at[block(k), slot(3)], (as_, ar), (2, k), col=sibling
        )
    for e in (0, 1):
        deal.send(lambda column, e=e: up.at[2 * column + e], lanes(ups, e * ff, ff), e == 1)
        deal.send(lambda column, e=e: down.at[2 * column + e], lanes(downs, e * ff, ff), e == 1)
    sent = {}
    for k in order:
        got[1, k].wait_recv()
        got[3, k].wait_recv()
        product = jnp.dot(attended_rows[block(k), :], weight[...], preferred_element_type=f32)
        if k:
            out_buf[k - 1] = product.astype(bf16)
            sent[k] = go(
                out_buf.at[k - 1], in_buf.at[k - 1], (ps, pr), k - 1, row=lax.rem(row + k, 4)
            )
        else:
            acc[...] = product + inputs[...].astype(f32)
    total = acc[...]
    for k in (1, 3, 2):
        sent[k].wait_recv()
        total += in_buf[k - 1].astype(f32)
    middle[...] = total
    own[...] = total.astype(bf16)
    gather = Gather(own, full, sems[:6], go, row, sibling, across)
    gather.begin()
    gather.second()
    gather.forward_first()
    gather.forward_rest()
    gather.finish()
    deal.finish()
    for copy in pending:
        copy.wait_send()


def front_step(attended, weight, inputs, up, down):
    rows, columns = inputs.shape
    dealt = jax.ShapeDtypeStruct((2 * up.shape[1], 4 * columns), bf16)
    return pl.pallas_call(
        front_kernel,
        out_shape=(
            jax.ShapeDtypeStruct((rows, columns), f32),
            jax.ShapeDtypeStruct((4 * rows, 4 * columns), bf16),
            jax.ShapeDtypeStruct((4 * rows, columns), bf16),
            dealt,
            dealt,
        ),
        in_specs=[VMEM] * 3 + [HBM] * 2,
        out_specs=(VMEM,) * 3 + (HBM,) * 2,
        scratch_shapes=[
            pltpu.VMEM((rows, columns), bf16),
            pltpu.VMEM((3, rows, columns), bf16),
            pltpu.VMEM((3, rows, columns), bf16),
            pltpu.VMEM((rows, columns), f32),
            *pair(3, 4),
            *pair(3),
            *gather_scratch,
            *deal_scratch(4),
        ],
        compiler_params=params(5),
        cost_estimate=cost(1 << 29, 150),
        name="front_step",
    )(attended, weight, inputs, up, down)


def dot(spec, left, right, kind=f32):
    return jnp.einsum(spec, left, right, preferred_element_type=f32).astype(kind)


def rotary_tables(length, half_width):
    position = jnp.arange(length, dtype=f32)[:, None]
    frequency = jnp.exp(jnp.arange(half_width, dtype=f32) * (-math.log(10000.0) / half_width))
    angles = position * frequency[None, :]
    return (jnp.cos(angles), jnp.sin(angles))


def rotate(values, cos_table, sin_table):
    half_width = cos_table.shape[-1]
    first_half = values[..., :half_width]
    second_half = values[..., half_width:]
    return jnp.concatenate(
        [
            first_half * cos_table - second_half * sin_table,
            second_half * cos_table + first_half * sin_table,
        ],
        axis=-1,
    )


def pad_to(values, axis, size):
    widths = [(0, 0)] * values.ndim
    widths[axis] = (0, size - values.shape[axis])
    return jnp.pad(values, widths)


def visible_mask(offset, block_rows, prefix_len):
    query_pos = offset + jnp.arange(block_rows, dtype=jnp.int32)
    key_pos = jnp.arange(SEQ, dtype=jnp.int32)
    return (key_pos[None, :] <= query_pos[:, None]) | (key_pos[None, :] < prefix_len)


def attend_forward(queries, key_rows, value_rows, prefix_len):
    score_scale = (NOPE + ROPE) ** (-0.5)
    scores = dot("qd,kd->qk", queries, key_rows) * score_scale
    scores = jnp.where(visible_mask(0, SEQ, prefix_len), scores, masked_score)
    top_score = jnp.max(scores, axis=1, keepdims=True)
    exp_scores = jnp.exp(scores - top_score)
    row_total = jnp.sum(exp_scores, axis=1, keepdims=True)
    weights = (exp_scores / row_total).astype(bf16)
    result = dot("qk,kd->qd", weights, value_rows)
    return (result, (top_score + jnp.log(row_total))[:, 0])


def attend_backward(queries, key_rows, value_rows, log_total, out_grad, prefix_len):
    score_scale = (NOPE + ROPE) ** (-0.5)
    scores = dot("qd,kd->qk", queries, key_rows) * score_scale
    scores = jnp.where(visible_mask(0, SEQ, prefix_len), scores, masked_score)
    weights = jnp.exp(scores - log_total[:, None])
    value_grad = dot("qk,qd->kd", weights.astype(bf16), out_grad)
    weight_grad = dot("qd,kd->qk", out_grad, value_rows)
    centre = jnp.sum(weights * weight_grad, axis=1, keepdims=True)
    score_grad = (weights * (weight_grad - centre)).astype(bf16)
    query_grad = dot("qk,kd->qd", score_grad, key_rows) * score_scale
    key_grad = dot("qk,qd->kd", score_grad, queries) * score_scale
    return (query_grad, key_grad, value_grad)


def on_device(
    inputs,
    attention_gain,
    query_weight,
    latent_weight,
    latent_gain,
    expand_weight,
    output_weight,
    feedforward_gain,
    router_weight,
    shared_gate,
    shared_up,
    shared_down,
    expert_gate,
    expert_up,
    expert_down,
    routes,
    prefix,
    cotangent,
):
    row = lax.axis_index("row")
    col = lax.axis_index("col")
    prefix_len = prefix[0]
    cos_table, sin_table = rotary_tables(SEQ, ROPE // 2)
    first_gain = attention_gain.astype(f32)
    second_gain = feedforward_gain.astype(f32)
    compact_gain = latent_gain.astype(f32)
    residual_in = inputs.astype(f32)
    rows = inputs.shape[0]
    ff = expert_gate.shape[2]
    low = shared_down.shape[0] // 4

    gains = jnp.stack([attention_gain, feedforward_gain])
    common = jnp.concatenate([latent_weight.T, pad_to(gains, 0, 16)], axis=0)
    input_rows, out_grad, project_all, gates, lows = start_step(
        inputs,
        cotangent,
        common,
        query_weight.T,
        expert_gate.transpose(0, 2, 1),
        shared_gate.T,
        shared_up.T,
        pad_to(router_weight.T, 0, 16),
        shared_down,
    )
    project_weight = project_all[: RANK + 256]
    first_all = project_all[RANK + 256].astype(f32)
    second_all = project_all[RANK + 257].astype(f32)
    out_weight = jnp.concatenate(
        [lax.dynamic_slice_in_dim(output_weight, (col ^ k) * VDIM, VDIM, 0) for k in range(4)],
        axis=0,
    )
    order = col ^ jnp.arange(4, dtype=jnp.int32)

    input_rows = input_rows.astype(f32)
    scale_one = lax.rsqrt(jnp.mean(input_rows * input_rows, axis=1) + norm_eps)
    normed = (input_rows * scale_one[:, None] * first_all[None, :]).astype(bf16)
    projected = dot("td,qd->tq", normed, project_weight)
    content = projected[:, :RANK]
    latent_scale = lax.rsqrt(jnp.mean(content * content, axis=1) + norm_eps)
    compact = (content * latent_scale[:, None] * compact_gain[None, :]).astype(bf16)
    shared_key = rotate(projected[:, RANK + 192 :], cos_table, sin_table).astype(bf16)
    key_value = dot("tr,rk->tk", compact, expand_weight, bf16)
    query_rot = jnp.concatenate(
        [
            projected[:, RANK : RANK + NOPE],
            rotate(projected[:, RANK + NOPE : RANK + 192], cos_table, sin_table),
        ],
        axis=1,
    ).astype(bf16)
    key_rows = jnp.concatenate([key_value[:, :NOPE], shared_key], axis=1)
    value_rows = key_value[:, NOPE:]
    head_result, log_total = attend_forward(query_rot, key_rows, value_rows, prefix_len)
    residual_mid, middle_rows, attended_rows, ups, downs = front_step(
        head_result.astype(bf16), out_weight, inputs, expert_up.transpose(0, 2, 1), expert_down
    )

    experts = jnp.arange(EXPERTS, dtype=jnp.int32)
    named = jnp.any(routes.T[None, :, :] == experts[:, None, None], axis=1).astype(f32)
    mine = (experts[:, None] == 2 * col + jnp.arange(128, dtype=jnp.int32)[None, :]).astype(f32)
    hidden, scale_two, act, delta, combined = expert_step(
        middle_rows, out_grad, gates, ups, downs, lows, second_all[None, :], named, mine
    )
    expert_grad, shared_grad, router_part, combined_sum = grads_step(
        hidden, out_grad, delta, act, combined, ff, low
    )
    output = (residual_mid + combined_sum).astype(bf16)
    expert_sum = lax.psum_scatter(expert_grad, "dp", scatter_dimension=0, tiled=True)[0]
    delta, expert_grad = lax.optimization_barrier((delta, expert_grad))
    hidden_grad = back_step(delta, gates, ups, lows)

    my_scale_one = lax.dynamic_slice_in_dim(scale_one, row * rows, rows, 0)[:, None]
    my_scale_two = lax.dynamic_slice_in_dim(scale_two[:, :1], row * rows, rows, 0)
    residual_grad, residual_rows, attended_grad, second_gain_part, shared_all = middle_step(
        hidden_grad,
        residual_mid,
        cotangent,
        my_scale_two,
        second_gain[None, :],
        out_weight,
        shared_grad,
    )
    head_grad = dot("th,td->hd", attended_rows, residual_rows, bf16)
    output_weight_grad = head_grad.reshape(4, VDIM, 512)[order].reshape(4 * VDIM, 512)
    query_rot_grad, key_grad, value_grad = attend_backward(
        query_rot, key_rows, value_rows, log_total, attended_grad, prefix_len
    )
    pair_grad = jnp.concatenate([key_grad[:, :NOPE], value_grad], axis=1).astype(bf16)
    expand_part = dot("tk,tr->kr", pair_grad, compact, bf16)
    compact_grad = dot("tk,rk->tr", pair_grad, expand_weight)
    weighted_compact = compact_grad * compact_gain[None, :]
    inner_sum = jnp.sum(weighted_compact * content, axis=1)
    content_grad = (
        latent_scale[:, None] * weighted_compact
        - content * (latent_scale * latent_scale * latent_scale * inner_sum / RANK)[:, None]
    )
    latent_gain_part = jnp.sum(compact_grad * content * latent_scale[:, None], axis=0)
    project_grad = jnp.concatenate(
        [
            content_grad,
            query_rot_grad[:, :NOPE],
            rotate(query_rot_grad[:, NOPE:], cos_table, -sin_table),
            rotate(key_grad[:, NOPE:], cos_table, -sin_table),
        ],
        axis=1,
    ).astype(bf16)
    normed_grad = dot("tq,qd->td", project_grad, project_weight, bf16)
    project_part = dot("tq,td->qd", project_grad, normed, bf16)
    latent_part = jnp.concatenate([project_part[:RANK], project_part[RANK + 192 :]], axis=0)
    first_part = jnp.sum(
        normed_grad.astype(f32) * (input_rows * scale_one[:, None]), axis=0, keepdims=True
    )
    extra = jnp.concatenate(
        [
            jnp.tile(latent_gain_part[None, :], (1, 4)).astype(bf16),
            first_part.astype(bf16),
            router_part[:EXPERTS],
            jnp.zeros((6, D), bf16),
        ],
        axis=0,
    )
    narrow_part = jnp.concatenate(
        [latent_part.reshape(4, -1, D), jnp.broadcast_to(extra[None], (4, 16, D))], axis=1
    )
    narrow_part, expert_sum = lax.optimization_barrier((narrow_part, expert_sum))
    pairs = [
        (dp * 4 + c, (2 * c + dp // 4) * 4 + (c ^ (dp % 4))) for dp in range(8) for c in range(4)
    ]
    expert_sum = lax.ppermute(expert_sum, ("dp", "col"), pairs)
    inputs_grad, sums, narrow, gains, latent_small = tail_step(
        normed_grad,
        narrow_part.reshape(-1, D),
        project_part[RANK : RANK + 192],
        jnp.concatenate([output_weight_grad, expand_part], axis=0),
        residual_grad,
        inputs,
        my_scale_one,
        first_gain[None, :],
        second_gain_part,
    )
    output_weight_grad = sums[:512].astype(f32)
    expand_grad = sums[512:768].T.astype(f32)
    query_weight_grad = sums[768:].T.astype(f32)
    latent_weight_grad = narrow.reshape(-1, 512).T.astype(f32)
    latent_gain_grad = latent_small[0, 0].astype(f32)
    own_small = lax.dynamic_index_in_dim(latent_small, col, 0, False).astype(f32)
    first_gain_grad = own_small[1]
    router_grad = own_small[2 : 2 + EXPERTS].T
    second_gain_grad = gains[0]

    expert_sum = expert_sum.astype(f32)
    expert_gate_grad = expert_sum[None, :ff].transpose(0, 2, 1)
    expert_up_grad = expert_sum[None, ff : 2 * ff].transpose(0, 2, 1)
    expert_down_grad = expert_sum[None, 2 * ff :]
    shared_sum = shared_all.transpose(1, 0, 2, 3).reshape(4, -1, 512)[order].astype(f32)
    shared_gate_grad = shared_sum[:, :low].reshape(4 * low, 512).T
    shared_up_grad = shared_sum[:, low : 2 * low].reshape(4 * low, 512).T
    shared_down_grad = shared_sum[:, 2 * low : 3 * low].reshape(4 * low, 512)
    return (
        output,
        inputs_grad,
        first_gain_grad,
        query_weight_grad,
        latent_weight_grad,
        latent_gain_grad,
        expand_grad,
        output_weight_grad,
        second_gain_grad,
        router_grad,
        shared_gate_grad,
        shared_up_grad,
        shared_down_grad,
        expert_gate_grad,
        expert_up_grad,
        expert_down_grad,
    )


def solution(mesh):
    placed = (
        P(("dp", "row"), "col"),
        P("col"),
        P("col", "row"),
        P("col", None),
        P(),
        P(None, ("row", "col")),
        P("row", "col"),
        P("col"),
        P("col", None),
        P("col", "row"),
        P("col", "row"),
        P("row", "col"),
        P(None, "col", "row"),
        P(None, "col", "row"),
        P(None, "row", "col"),
        P("dp", None),
        P("dp"),
        P(("dp", "row"), "col"),
    )
    return jax.shard_map(
        on_device,
        mesh=mesh,
        in_specs=placed,
        out_specs=(
            P(("dp", "row"), "col"),
            P(("dp", "row"), "col"),
            P("col"),
            P("col", "row"),
            P("col", None),
            P(),
            P(None, ("row", "col")),
            P("row", "col"),
            P("col"),
            P("col", None),
            P("col", "row"),
            P("col", "row"),
            P("row", "col"),
            P("dp", "col", "row"),
            P("dp", "col", "row"),
            P("dp", "row", "col"),
        ),
        check_vma=False,
    )
```

```python
import functools
import math

import jax
import jax.numpy as jnp
from jax import lax
from jax.experimental import pallas as pl
from jax.experimental.pallas import tpu as pltpu
from jax.sharding import PartitionSpec as P

D = 2048
NOPE = 128
ROPE = 64
VDIM = 128
RANK = 512
TOPK = 6
EXPERTS = 8
SEQ = 1024

norm_eps = 1e-06
masked_score = -1e30
bf16 = jnp.bfloat16
f32 = jnp.float32
MESH = pl.DeviceIdType.MESH
DMA = pltpu.SemaphoreType.DMA
VMEM = pl.BlockSpec(memory_space=pltpu.VMEM)
HBM = pl.BlockSpec(memory_space=pl.ANY)


def place():
    row = lax.axis_index("row")
    col = lax.axis_index("col")
    sibling = col + 1 - 2 * lax.rem(col, 2)
    across = lax.rem(col + 2, 4)
    return (row, sibling, across, lax.rem(sibling + 2, 4))


def greet(columns, row, others=()):
    barrier = pltpu.get_barrier_semaphore()
    targets = [{"col": column} for column in columns]
    targets += [{"row": lax.rem(row + step, 4)} for step in (1, 2, 3)]
    targets += list(others)
    for target in targets:
        pl.semaphore_signal(barrier, inc=1, device_id=target, device_id_type=MESH)
    pl.semaphore_wait(barrier, len(targets))


def along_z(dp, step):
    return dp // 4 * 4 + lax.rem(lax.rem(dp, 4) + step, 4)


def remote(source, target, sems, at, **device):
    return pltpu.make_async_remote_copy(
        src_ref=source,
        dst_ref=target,
        send_sem=sems[0].at[at],
        recv_sem=sems[1].at[at],
        device_id=device,
        device_id_type=MESH,
    )


def starter(pending):
    def go(*arguments, **device):
        copy = remote(*arguments, **device)
        copy.start()
        pending.append(copy)
        return copy

    return go


def pair(*shape):
    return [DMA(shape), DMA(shape)]


def params(collective):
    return pltpu.CompilerParams(
        collective_id=collective, has_side_effects=True, vmem_limit_bytes=52 << 20
    )


def cost(flops, mebibytes):
    return pl.CostEstimate(flops=flops, bytes_accessed=mebibytes << 20, transcendentals=0)


class Gather:
    def __init__(self, own, full, sems, go, row, sibling, across):
        self.own, self.full, self.go = own, full, go
        self.xs, self.ys, self.cs = sems[0:2], sems[2:4], sems[4:6]
        self.row, self.sibling, self.across = row, sibling, across
        self.arrivals, self.halves = [], []

    def block(self, at_row, at_col):
        rows, columns = self.own.shape
        start = pl.multiple_of(at_row * rows, rows)
        return self.full.at[pl.ds(start, rows), pl.ds(at_col * columns, columns)]

    def along(self, source, target, base):
        return [
            self.go(source, target, self.ys, base + n, row=lax.rem(self.row + k, 4))
            for n, k in enumerate((1, 3))
        ]

    def over(self, source, target):
        count = len(self.arrivals)
        self.arrivals.append(self.go(source, target, self.cs, count, col=self.sibling))

    def begin(self):
        row = self.row
        rows, columns = self.own.shape
        self.side = self.go(self.own, self.block(row, 2), self.xs, 0, col=self.across)
        self.first = self.along(self.own, self.block(row, 0), 0)
        self.over(self.own, self.block(row, 1))
        start = pl.multiple_of(row * rows, rows)
        self.full[pl.ds(start, rows), pl.ds(0, columns)] = self.own[...]

    def second(self):
        self.side.wait_recv()
        here = self.block(self.row, 2)
        self.rest = self.along(here, here, 2)
        self.over(here, self.block(self.row, 3))

    def forward(self, group, at_col, base):
        rows, columns = self.own.shape
        for n, k in enumerate((1, 3)):
            group[n].wait_recv()
            source = lax.rem(self.row + 4 - k, 4)
            start = pl.multiple_of(source * rows + n * (rows // 2), rows // 2)
            half = self.full.at[pl.ds(start, rows // 2), pl.ds(at_col * columns, columns)]
            self.halves.append(
                self.go(half, half, self.ys, base + n, row=lax.rem(self.row + k, 4))
            )
            self.over(self.block(source, at_col), self.block(source, at_col + 1))

    def forward_first(self):
        self.forward(self.first, 0, 4)

    def forward_rest(self):
        self.forward(self.rest, 2, 6)

    def finish(self):
        facing = lax.rem(self.row + 2, 4)
        for n, at_col in enumerate((0, 2)):
            for copy in self.halves[2 * n : 2 * n + 2]:
                copy.wait_recv()
            self.over(self.block(facing, at_col), self.block(facing, at_col + 1))
        for copy in self.arrivals:
            copy.wait_recv()


gather_scratch = pair(1) + pair(8) + pair(8)


class Deal:
    def __init__(self, sems, local_sems, pending, col, peers):
        self.go, self.sems, self.local_sems = starter(pending), sems, local_sems
        self.col, self.peers = col, peers
        self.far = lax.rem(lax.axis_index("dp") + 4, 8)
        self.copies, self.local, self.count = [], [], 0

    def send(self, source, target, flip):
        n = self.count
        self.count += 1
        copy = pltpu.make_async_copy(source(self.col), target(0), self.local_sems.at[n])
        copy.start()
        self.local.append(copy)
        for k, peer in ((2, self.peers[1]), (3, self.peers[2]), (1, self.peers[0])):
            place_at = {"col": peer}
            if flip and k != 1:
                place_at["dp"] = self.far
            self.copies.append(
                self.go(source(peer), target(k), self.sems, (k - 1, n), **place_at)
            )

    def finish(self):
        for copy in self.local:
            copy.wait()
        for copy in self.copies:
            copy.wait_recv()


def deal_scratch(count):
    return pair(3, count) + [DMA((count,))]


def deal_peers(peers):
    far = lax.rem(lax.axis_index("dp") + 4, 8)
    return [{"dp": far, "col": peer} for peer in peers[1:]]


def lanes(array, start, size):
    return lambda k: array.at[pl.ds(start, size), pl.ds(512 * k, 512)]


def rows_at(array, size):
    return lambda column: array.at[pl.ds(pl.multiple_of(column * size, size), size)]


def start_kernel(
    inputs, common, query, gate, full, project, gates, *sems,
):
    row, sibling, across, corner = place()
    col = lax.axis_index("col")
    peers = (sibling, across, corner)
    greet(peers, row, deal_peers(peers))
    pending = []
    go = starter(pending)
    gather = Gather(inputs, full, sems[0:6], go, row, sibling, across)
    deal = Deal(sems[6:8], sems[8], pending, col, peers)
    ff = gate.shape[1]
    gather.begin()
    deal.send(lambda column: common.at[pl.ds(0, RANK)], lanes(project, 0, RANK), True)
    deal.send(rows_at(query, 192), lanes(project, RANK, 192), False)
    deal.send(lambda column: common.at[pl.ds(RANK, 80)], lanes(project, RANK + 192, 80), False)
    gather.second()
    for e in (0, 1):
        deal.send(lambda column, e=e: gate.at[2 * column + e], lanes(gates, e * ff, ff), e == 1)
    gather.forward_first()
    gather.forward_rest()
    gather.finish()
    deal.finish()
    for copy in pending:
        copy.wait_send()


def start_step(inputs, common, query, gate):
    rows, columns = inputs.shape
    return pl.pallas_call(
        start_kernel,
        out_shape=(
            jax.ShapeDtypeStruct((4 * rows, 4 * columns), bf16),
            jax.ShapeDtypeStruct((RANK + 272, 4 * columns), bf16),
            jax.ShapeDtypeStruct((2 * gate.shape[1], 4 * columns), bf16),
        ),
        in_specs=[VMEM] + [HBM] * 3,
        out_specs=(VMEM, HBM, HBM),
        scratch_shapes=[*gather_scratch, *deal_scratch(5)],
        compiler_params=params(0),
        cost_estimate=cost(0, 150),
        name="start_step",
    )(inputs, common, query, gate)


def reduce_scratch(rows, columns):
    return [
        pltpu.VMEM((4, 2, rows, columns), bf16),
        pltpu.VMEM((3, 2, rows, columns), bf16),
        pltpu.VMEM((3, 2, rows, columns), bf16),
        pltpu.VMEM((2, rows, columns), f32),
        pltpu.VMEM((2, rows, columns), bf16),
        *pair(1),
        *pair(3, 2),
        *pair(4, 2),
    ]


class Reduction:
    order = (2, 1, 3, 0)

    def __init__(self, part, scratch, row, sibling, across):
        self.part = part
        self.held, self.out_buf, self.in_buf, self.acc, self.side_buf = scratch[:5]
        self.xs, self.ys, self.cs = scratch[5:7], scratch[7:9], scratch[9:11]
        self.row, self.sibling, self.across = row, sibling, across
        self.rows, self.columns = self.acc.shape[1:]

    def rows_of(self, k):
        start = lax.rem(self.row + k, 4) * self.rows
        return pl.ds(pl.multiple_of(start, self.rows), self.rows)

    def pair_copy(self, k, x):
        return remote(
            self.part.at[self.rows_of(k), pl.ds((2 * x + 1) * self.columns, self.columns)],
            self.held.at[k, x],
            self.cs,
            (k, x),
            col=self.sibling,
        )

    def along_copy(self, k, x):
        return remote(
            self.out_buf.at[k - 1, x],
            self.in_buf.at[k - 1, x],
            self.ys,
            (k - 1, x),
            row=lax.rem(self.row + k, 4),
        )

    def side_copy(self):
        return remote(self.side_buf.at[0], self.side_buf.at[1], self.xs, 0, col=self.across)

    def start(self):
        for x in (1, 0):
            for k in self.order:
                self.pair_copy(k, x).start()

    def along_one(self, k, x):
        self.pair_copy(k, x).wait_recv()
        mine = self.part[self.rows_of(k), pl.ds(2 * x * self.columns, self.columns)]
        value = mine.astype(f32) + self.held[k, x].astype(f32)
        if k:
            self.out_buf[k - 1, x] = value.astype(bf16)
            self.along_copy(k, x).start()
        else:
            self.acc[x] = value

    def along(self):
        for x in (1, 0):
            for k in self.order:
                self.along_one(k, x)

    def collect(self, x):
        for k in (1, 3, 2):
            self.along_copy(k, x).wait_recv()
            self.acc[x] += self.in_buf[k - 1, x].astype(f32)

    def over(self):
        self.collect(1)
        self.side_buf[0] = self.acc[1].astype(bf16)
        self.side_copy().start()

    def side(self):
        self.over()
        self.collect(0)

    def total(self):
        self.side_copy().wait_recv()
        return self.acc[0] + self.side_buf[1].astype(f32)

    def finish(self):
        for k in self.order:
            for x in (0, 1):
                self.pair_copy(k, x).wait_send()
                if k:
                    self.along_copy(k, x).wait_send()
        self.side_copy().wait_send()


def product(left, right):
    return jnp.dot(left, right, preferred_element_type=f32).astype(bf16)


def times_rows(left, right):
    return lax.dot_general(left, right, (((1,), (1,)), ((), ())), preferred_element_type=f32)


def over_units(left, right):
    return lax.dot_general(left, right, (((0,), (0,)), ((), ())), preferred_element_type=f32)


def expert_kernel(
    middle, out_grad, gates, ups, downs, lows, gain, named, mine,
    hidden, scale, act, delta, combined,
):
    values = middle[...].astype(f32)
    scales = lax.rsqrt(jnp.mean(values * values, axis=1, keepdims=True) + norm_eps)
    scale[...] = jnp.broadcast_to(scales, scale.shape)
    normal = (values * scales * gain[...]).astype(bf16)
    hidden[...] = normal
    upstream = out_grad[...]
    ff = gates.shape[0] // 2
    low = (lows.shape[0] - 16) // 3
    low_pre = times_rows(lows[pl.ds(0, 2 * low + 16), :], normal)
    logits = low_pre[2 * low : 2 * low + EXPERTS]
    powers = jnp.exp(logits - jnp.max(logits, axis=0, keepdims=True))
    probs = powers / jnp.sum(powers, axis=0, keepdims=True)
    names = named[...]
    probs_part = jnp.zeros_like(probs)
    for e in range(3):
        if e < 2:
            size, at = ff, pl.ds(e * ff, ff)
            gate_pre = times_rows(gates[at, :], normal)
            up_pre = times_rows(ups[at, :], normal)
            act_grad = times_rows(downs[at, :], upstream)
            own = mine[:, e : e + 1]
            weight = jnp.sum(probs * names * own, axis=0, keepdims=True)
            gate_at, up_at, act_at = e * ff, (2 + e) * ff, e * ff
        else:
            size = low
            gate_pre, up_pre = low_pre[:low], low_pre[low : 2 * low]
            act_grad = times_rows(lows[pl.ds(2 * low + 16, low), :], upstream)
            weight = 1.0
            gate_at, up_at, act_at = 4 * ff, 4 * ff + low, 2 * ff
        sig = 1.0 / (1.0 + jnp.exp(-gate_pre))
        silu = gate_pre * sig
        both = silu * up_pre
        act[pl.ds(act_at, size), :] = (weight * both).astype(bf16)
        weighted = weight * act_grad
        delta[pl.ds(gate_at, size), :] = (
            weighted * up_pre * (sig * (1.0 + gate_pre * (1.0 - sig)))
        ).astype(bf16)
        delta[pl.ds(up_at, size), :] = (weighted * silu).astype(bf16)
        if e < 2:
            named_sum = jnp.sum(act_grad * both, axis=0, keepdims=True)
            probs_part = probs_part + named_sum * own * names
    logits_part = probs * (probs_part - jnp.sum(probs * probs_part, axis=0, keepdims=True))
    delta[pl.ds(4 * ff + 2 * low, 16), :] = jnp.concatenate(
        [logits_part, jnp.zeros_like(logits_part)], axis=0
    ).astype(bf16)
    combined[...] = (
        over_units(act[pl.ds(0, 2 * ff), :], downs[...])
        + over_units(act[pl.ds(2 * ff, low), :], lows[pl.ds(2 * low + 16, low), :])
    ).astype(bf16)


def whole(value):
    return pl.BlockSpec(value.shape, lambda i: (0,) * len(value.shape))


def once(value):
    return pl.BlockSpec(
        value.shape, lambda i: (0,) * len(value.shape), pipeline_mode=pl.Buffered(1)
    )


def expert_step(middle, out_grad, gates, ups, downs, lows, gain, named, mine):
    tile = 256
    tokens, width = middle.shape
    wide = pl.BlockSpec((tile, width), lambda i: (i, 0))

    def tall(rows):
        return pl.BlockSpec((rows, tile), lambda i: (0, i))

    acts = downs.shape[0] + (lows.shape[0] - 16) // 3
    deltas = gates.shape[0] + ups.shape[0] + 2 * (lows.shape[0] - 16) // 3 + 16
    return pl.pallas_call(
        expert_kernel,
        grid=(tokens // tile,),
        out_shape=(
            jax.ShapeDtypeStruct((tokens, width), bf16),
            jax.ShapeDtypeStruct((tokens, 128), f32),
            jax.ShapeDtypeStruct((acts, tokens), bf16),
            jax.ShapeDtypeStruct((deltas, tokens), bf16),
            jax.ShapeDtypeStruct((tokens, width), bf16),
        ),
        in_specs=[
            wide,
            wide,
            whole(gates),
            whole(ups),
            whole(downs),
            whole(lows),
            whole(gain),
            tall(EXPERTS),
            whole(mine),
        ],
        out_specs=(
            wide,
            pl.BlockSpec((tile, 128), lambda i: (i, 0)),
            tall(acts),
            tall(deltas),
            wide,
        ),
        compiler_params=pltpu.CompilerParams(vmem_limit_bytes=56 << 20),
        cost_estimate=cost(2 * 5 * gates.shape[0] * width * tokens, 30),
        name="expert_step",
    )(middle, out_grad, gates, ups, downs, lows, gain, named, mine)


def grads_kernel(
    hidden, out_grad, delta, act, combined, gates, ups, lows,
    grads, shared, router, total, hidden_grad,
    own_shared, chunk_in, ps, pr, *scratch, ff, low,
):
    step = pl.program_id(0)
    row, sibling, across, corner = place()
    dp = lax.axis_index("dp")
    z = lax.rem(dp, 4)
    steps = Reduction(combined, scratch, row, sibling, across)
    piece = shared.shape[1]

    def quarter(at):
        return pl.ds(pl.multiple_of(at * piece, piece), piece)

    def scattered(k):
        return remote(
            own_shared.at[:, quarter(lax.rem(z + k, 4))],
            chunk_in.at[k - 1],
            (ps, pr),
            k - 1,
            dp=along_z(dp, k),
        )

    @pl.when(step == 0)
    def _():
        greet((sibling, across), row, [{"dp": along_z(dp, k)} for k in (1, 2, 3)])
        steps.start()

    for at, blocks in (
        (1, ((2, 1), (1, 1), (3, 1))),
        (2, ((0, 1), (2, 0), (1, 0))),
        (3, ((3, 0), (0, 0))),
    ):

        @pl.when(step == at)
        def _(blocks=blocks):
            for k, x in blocks:
                steps.along_one(k, x)

    @pl.when(step == 8)
    def _():
        steps.over()

    for k in range(4):

        @pl.when(step == k)
        def _(k=k):
            base = 4 * ff
            own_shared[k, pl.ds(0, low), :] = product(delta[pl.ds(base, low), :], hidden[...])
            own_shared[k, pl.ds(low, low), :] = product(
                delta[pl.ds(base + low, low), :], hidden[...]
            )
            router[...] = product(delta[pl.ds(base + 2 * low, 16), :], hidden[...])
            own_shared[k, pl.ds(2 * low, low), :] = product(
                act[pl.ds(2 * ff, low), :], out_grad[...]
            )
            spare = 4 * piece - 3 * low
            own_shared[k, pl.ds(3 * low, spare), :] = jnp.zeros((spare, 512), bf16)

    @pl.when(step == 3)
    def _():
        for k in (1, 2, 3):
            scattered(k).start()

    for e in (0, 1):

        @pl.when(step // 4 == e + 1)
        def _(e=e):
            at = e * ff
            grads[0, pl.ds(0, ff), :] = product(delta[pl.ds(at, ff), :], hidden[...])
            grads[0, pl.ds(ff, ff), :] = product(delta[pl.ds(2 * ff + at, ff), :], hidden[...])
            grads[0, pl.ds(2 * ff, ff), :] = product(act[pl.ds(at, ff), :], out_grad[...])

    @pl.when(step >= 12)
    def _():
        at = pl.ds(pl.multiple_of((step - 12) * 256, 256), 256)
        hidden_grad[...] = (
            over_units(delta[pl.ds(0, 2 * ff), at], gates[...])
            + over_units(delta[pl.ds(2 * ff, 2 * ff), at], ups[...])
            + over_units(delta[pl.ds(4 * ff, 2 * low + 16), at], lows[pl.ds(0, 2 * low + 16), :])
        ).astype(bf16)

    @pl.when(step == 15)
    def _():
        steps.collect(0)
        total[...] = steps.total()
        summed = own_shared[:, quarter(z), :].astype(f32)
        for k in (1, 2, 3):
            scattered(k).wait_recv()
            summed += chunk_in[k - 1].astype(f32)
        shared[...] = summed.astype(bf16)
        for k in (1, 2, 3):
            scattered(k).wait_send()
        steps.finish()


def grads_step(hidden, out_grad, delta, act, combined, gates, ups, lows):
    tokens = hidden.shape[0]
    ff, low = gates.shape[0] // 2, (lows.shape[0] - 16) // 3
    piece = -(-3 * low // 64) * 16
    wide = pl.BlockSpec((tokens, 512), lambda i: (0, i % 4))
    return pl.pallas_call(
        functools.partial(grads_kernel, ff=ff, low=low),
        grid=(16,),
        out_shape=(
            jax.ShapeDtypeStruct((8, 3 * ff, 512), bf16),
            jax.ShapeDtypeStruct((4, piece, 512), bf16),
            jax.ShapeDtypeStruct((16, D), bf16),
            jax.ShapeDtypeStruct((tokens // 4, 512), f32),
            jax.ShapeDtypeStruct((tokens, D), bf16),
        ),
        in_specs=[wide, wide] + [once(v) for v in (delta, act, combined, gates, ups, lows)],
        out_specs=(
            pl.BlockSpec((1, 3 * ff, 512), lambda i: (jnp.clip(i - 4, 0, 7), 0, 0)),
            pl.BlockSpec((4, piece, 512), lambda i: (0, 0, 0)),
            pl.BlockSpec((16, 512), lambda i: (0, jnp.minimum(i, 3))),
            pl.BlockSpec((tokens // 4, 512), lambda i: (0, 0)),
            pl.BlockSpec((256, D), lambda i: (jnp.maximum(i - 12, 0), 0)),
        ),
        scratch_shapes=[
            pltpu.VMEM((4, 4 * piece, 512), bf16),
            pltpu.VMEM((3, 4, piece, 512), bf16),
            *pair(3),
            *reduce_scratch(tokens // 4, 512),
        ],
        compiler_params=params(1),
        cost_estimate=cost(2 * 8 * 4 * ff * 512 * tokens, 60),
        name="grads_step",
    )(hidden, out_grad, delta, act, combined, gates, ups, lows)


class ColumnSum:
    def __init__(self, value, buf, sems, go, peers):
        self.buf = buf
        buf[0] = jnp.broadcast_to(value, (value.shape[0], 128)).T[:8]
        self.sent = [
            go(buf.at[0], buf.at[k + 1], sems, k, col=peer) for k, peer in enumerate(peers)
        ]

    def total(self):
        for copy in self.sent:
            copy.wait_recv()
        buf = self.buf
        total = (buf[0] + buf[1]) + (buf[2] + buf[3])
        return jnp.broadcast_to(total[:1], (128, total.shape[1])).T[:, :1]


def middle_kernel(
    part, middle, cotangent, scale, gain, weight, shared,
    residual_grad, residual_rows, attended_grad, gain_part, shared_all,
    sum_buf, out_buf, in_buf, acc, chunk_in, both, ss, sr, rs, rr, hs, hr, ps, pr, *scratch,
):
    row, sibling, across, corner = place()
    dp = lax.axis_index("dp")
    z = lax.rem(dp, 4)
    col = lax.axis_index("col")
    piece = shared.shape[1]
    quarter = pl.ds(pl.multiple_of(z * piece, piece), piece)
    far = lax.rem(dp + 4, 8)
    peers = (sibling, across, corner)
    greet(peers, row, [{"dp": along_z(dp, k)} for k in (1, 2, 3)] + [{"dp": far}])
    pending = []
    go = starter(pending)
    steps = Reduction(part, scratch, row, sibling, across)
    rows, columns = middle.shape
    head = attended_grad.shape[1]
    steps.start()
    halves = go(shared, chunk_in, (ps, pr), 0, dp=far)
    steps.along()
    steps.over()
    halves.wait_recv()
    both[...] = (shared[...].astype(f32) + chunk_in[...].astype(f32)).astype(bf16)
    shared_all[col, quarter, :] = both[0]
    home = [
        go(both.at[j + 1], shared_all.at[col, quarter], (ps, pr), 1 + j, col=peer)
        for j, peer in enumerate(peers)
    ]
    steps.collect(0)
    upstream = steps.total()
    weighted = upstream * gain[...]
    values = middle[...]
    scales = scale[...]
    inner = ColumnSum(
        jnp.sum(weighted * values, axis=1, keepdims=True), sum_buf, (ss, sr), go, peers
    )
    gain_part[...] = jnp.sum(upstream * values * scales, axis=0, keepdims=True)
    for copy in home:
        copy.wait_recv()
    spread = [
        go(
            shared_all.at[:, quarter],
            shared_all.at[:, quarter],
            (ps, pr),
            3 + k,
            dp=along_z(dp, k),
        )
        for k in (1, 2, 3)
    ]
    base = cotangent[...].astype(f32) + scales * weighted
    grad = base - values * (scales * scales * scales * inner.total() / D)
    residual_grad[...] = grad

    def block(at_row):
        return pl.ds(pl.multiple_of(at_row * rows, rows), rows)

    residual_rows[block(row), :] = grad.astype(bf16)
    sent = [
        go(
            residual_rows.at[block(row)],
            residual_rows.at[block(row)],
            (rs, rr),
            k - 1,
            row=lax.rem(row + k, 4),
        )
        for k in (1, 2, 3)
    ]
    got = []
    for k in (0, 1, 3, 2):
        source = lax.rem(row + 4 - k, 4)
        if k:
            sent[k - 1].wait_recv()
        result = times_rows(residual_rows[block(source), :], weight[...])
        acc[block(source), :] = result[:, :head]
        for j, peer in enumerate(peers):
            out_buf[j, block(source), :] = result[:, (j + 1) * head : (j + 2) * head].astype(bf16)
            got.append(
                go(
                    out_buf.at[j, block(source)],
                    in_buf.at[j, block(source)],
                    (hs, hr),
                    (j, k),
                    col=peer,
                )
            )
    for copy in got:
        copy.wait_recv()
    attended_grad[...] = (
        acc[...] + in_buf[0].astype(f32) + in_buf[1].astype(f32) + in_buf[2].astype(f32)
    ).astype(bf16)
    for copy in spread:
        copy.wait_recv()
    for copy in pending:
        copy.wait_send()
    steps.finish()


def middle_step(part, middle, cotangent, scale, gain, weight, shared):
    rows, columns = middle.shape
    piece = shared.shape[1]
    return pl.pallas_call(
        middle_kernel,
        out_shape=(
            jax.ShapeDtypeStruct((rows, columns), f32),
            jax.ShapeDtypeStruct((4 * rows, columns), bf16),
            jax.ShapeDtypeStruct((4 * rows, VDIM), bf16),
            jax.ShapeDtypeStruct((1, columns), f32),
            jax.ShapeDtypeStruct((4, 4 * piece, columns), bf16),
        ),
        in_specs=[VMEM] * 7,
        out_specs=(VMEM,) * 5,
        scratch_shapes=[
            pltpu.VMEM((4, 8, rows), f32),
            pltpu.VMEM((3, 4 * rows, VDIM), bf16),
            pltpu.VMEM((3, 4 * rows, VDIM), bf16),
            pltpu.VMEM((4 * rows, VDIM), f32),
            pltpu.VMEM((4, piece, columns), bf16),
            pltpu.VMEM((4, piece, columns), bf16),
            *pair(3),
            *pair(3),
            *pair(3, 4),
            *pair(7),
            *reduce_scratch(rows, columns),
        ],
        compiler_params=params(3),
        cost_estimate=cost(1 << 29, 200),
        name="middle_step",
    )(part, middle, cotangent, scale, gain, weight, shared)


def tail_kernel(
    part, narrow_part, query, ready, residual_grad, inputs, scale, gain, gain_part,
    inputs_grad, sums, narrow, gains, latent_gain,
    chunk_in, all_parts, narrow_all, lat_buf, lat_half, sum_buf,
    qs, qr, ps, pr, as_, ar, ls, lr, ns, nr, ss, sr, gs, gr, *scratch,
):
    row, sibling, across, corner = place()
    col = lax.axis_index("col")
    dp = lax.axis_index("dp")
    z = lax.rem(dp, 4)
    far = lax.rem(dp + 4, 8)
    peers = (sibling, across, corner)
    greet(peers, row, [{"dp": along_z(dp, k)} for k in (1, 2, 3)] + [{"dp": far}])
    pending = []
    go = starter(pending)
    count = len(scratch) // 2
    steps = Reduction(part, scratch[:count], row, sibling, across)
    before = Reduction(narrow_part, scratch[count:], row, sibling, across)
    rows, columns = inputs.shape
    piece = query.shape[0]
    lat = narrow_all.shape[1]
    keep = lat - 32

    def head(at):
        return pl.ds(pl.multiple_of(at * piece, piece), piece)

    def chunk(at):
        return pl.ds(pl.multiple_of(at * 2 * piece, 2 * piece), 2 * piece)

    before.start()
    dealt = [
        go(
            query.at[:, pl.ds((j + 1) * columns, columns)],
            all_parts.at[head(4 + col)],
            (qs, qr),
            j,
            col=peer,
        )
        for j, peer in enumerate(peers)
    ]
    steps.start()
    all_parts[pl.ds(0, 4 * piece), :] = ready[...]
    all_parts[head(4 + col), :] = query[:, pl.ds(0, columns)]
    before.along()
    for copy in dealt:
        copy.wait_recv()
    scattered = [
        go(
            all_parts.at[chunk(lax.rem(z + k, 4))],
            chunk_in.at[k - 1],
            (ps, pr),
            k - 1,
            dp=along_z(dp, k),
        )
        for k in (1, 2, 3)
    ]
    steps.along()
    before.side()
    lat_buf[z] = jnp.concatenate(
        [before.total(), gain_part[...], jnp.zeros((15, columns), f32)], axis=0
    ).astype(bf16)
    along = [
        go(lat_buf.at[z], lat_buf.at[z], (ls, lr), k - 1, dp=along_z(dp, k)) for k in (1, 2, 3)
    ]
    total = all_parts[chunk(z), :].astype(f32)
    for k in (1, 2, 3):
        scattered[k - 1].wait_recv()
        total += chunk_in[k - 1].astype(f32)
    chunk_in[3] = total.astype(bf16)
    halves = go(chunk_in.at[3], chunk_in.at[4], (ps, pr), 3, dp=far)
    steps.over()
    for copy in along:
        copy.wait_recv()
    lat_half[0] = (
        (lat_buf[0].astype(f32) + lat_buf[1].astype(f32))
        + (lat_buf[2].astype(f32) + lat_buf[3].astype(f32))
    ).astype(bf16)
    other = go(lat_half.at[0], lat_half.at[1], (ls, lr), 3, dp=far)
    steps.collect(0)
    halves.wait_recv()
    sums[chunk(z), :] = (chunk_in[3].astype(f32) + chunk_in[4].astype(f32)).astype(bf16)
    shared = [
        go(sums.at[chunk(z)], sums.at[chunk(z)], (as_, ar), k - 1, dp=along_z(dp, k))
        for k in (1, 2, 3)
    ]
    upstream = steps.total()
    weighted = upstream * gain[...]
    values = inputs[...].astype(f32)
    scales = scale[...]
    inner = ColumnSum(
        jnp.sum(weighted * values, axis=1, keepdims=True), sum_buf, (ss, sr), go, peers
    )
    other.wait_recv()
    narrow_all[row] = (lat_half[0].astype(f32) + lat_half[1].astype(f32)).astype(bf16)
    spread = [
        go(narrow_all.at[row], narrow_all.at[row], (ns, nr), k - 1, row=lax.rem(row + k, 4))
        for k in (1, 2, 3)
    ]
    inputs_grad[...] = (
        residual_grad[...]
        + scales * weighted
        - values * (scales * scales * scales * inner.total() / D)
    ).astype(bf16)
    for copy in spread:
        copy.wait_recv()
    narrow[...] = narrow_all[:, :keep, :]
    latent_gain[col] = narrow_all[0, pl.ds(keep, 16), :]
    last = [
        go(latent_gain.at[col], latent_gain.at[col], (gs, gr), j, col=peer)
        for j, peer in enumerate(peers)
    ]
    edge = pl.ds(keep + 16, 16)
    gains[...] = (
        narrow_all[0, edge, :].astype(f32)
        + narrow_all[1, edge, :].astype(f32)
        + narrow_all[2, edge, :].astype(f32)
        + narrow_all[3, edge, :].astype(f32)
    )
    for copy in last + shared:
        copy.wait_recv()
    for copy in pending:
        copy.wait_send()
    steps.finish()
    before.finish()


def tail_step(
    part, narrow_part, query, ready, residual_grad, inputs, scale, gain, gain_part
):
    rows, columns = inputs.shape
    piece = query.shape[0]
    narrow_rows = narrow_part.shape[0] // 4
    lat = narrow_rows + 16
    return pl.pallas_call(
        tail_kernel,
        out_shape=(
            jax.ShapeDtypeStruct((rows, columns), bf16),
            jax.ShapeDtypeStruct((8 * piece, columns), bf16),
            jax.ShapeDtypeStruct((4, lat - 32, columns), bf16),
            jax.ShapeDtypeStruct((16, columns), f32),
            jax.ShapeDtypeStruct((4, 16, columns), bf16),
        ),
        in_specs=[VMEM] * 9,
        out_specs=(VMEM,) * 5,
        scratch_shapes=[
            pltpu.VMEM((5, 2 * piece, columns), bf16),
            pltpu.VMEM((8 * piece, columns), bf16),
            pltpu.VMEM((4, lat, columns), bf16),
            pltpu.VMEM((4, lat, columns), bf16),
            pltpu.VMEM((2, lat, columns), bf16),
            pltpu.VMEM((4, 8, rows), f32),
            *pair(3),
            *pair(4),
            *pair(3),
            *pair(4),
            *pair(3),
            *pair(3),
            *pair(3),
            *reduce_scratch(rows, columns),
            *reduce_scratch(narrow_rows, columns),
        ],
        compiler_params=params(4),
        cost_estimate=cost(1 << 20, 200),
        name="tail_step",
    )(part, narrow_part, query, ready, residual_grad, inputs, scale, gain, gain_part)


score_scale = (NOPE + ROPE) ** (-0.5)


def swap_halves(values):
    lane = lax.broadcasted_iota(jnp.int32, values.shape, 1)
    return jnp.where(
        lax.rem(lane, 64) < 32, pltpu.roll(values, 96, 1), pltpu.roll(values, 32, 1)
    )


def masked_scores(queries, keys, early, start):
    scores = times_rows(queries, keys) * score_scale
    query_pos = start + lax.broadcasted_iota(jnp.int32, scores.shape, 0)
    key_pos = lax.broadcasted_iota(jnp.int32, scores.shape, 1)
    return jnp.where((key_pos <= query_pos) | (early > 0.0), scores, masked_score)


def front_kernel(
    input_rows, project, expand, weight, inputs, cotangent, cosine, sine, early, gain,
    up, down, low_gate, low_up, router, low_down,
    middle, full, attended_rows, out_grad, normed, scale, content, latent_scale, compact,
    queries, keys, values, log_total, ups, downs, lows,
    attended, own, out_buf, in_buf, acc, as_, ar, ps, pr, *sems,
):
    row, sibling, across, corner = place()
    peers = (sibling, across, corner)
    greet(peers, row, deal_peers(peers))
    pending = []
    go = starter(pending)
    rows, columns = inputs.shape
    head = attended.shape[1]
    order = (2, 1, 3, 0)
    beside = Gather(cotangent, out_grad, sems[6:12], go, row, sibling, across)
    deal = Deal(sems[12:14], sems[14], pending, lax.axis_index("col"), peers)
    ff = up.shape[1]
    low = low_down.shape[0] // 4
    beside.begin()
    for e in (0, 1):
        deal.send(lambda column, e=e: up.at[2 * column + e], lanes(ups, e * ff, ff), e == 1)

    first_gain = project[pl.ds(RANK + 256, 16), :].astype(f32)[:1]
    for i in range(4):
        at = pl.ds(i * rows, rows)
        wide = input_rows[at, :].astype(f32)
        scales = lax.rsqrt(jnp.mean(wide * wide, axis=1, keepdims=True) + norm_eps)
        scale[at, :] = scales
        normal = (wide * scales * first_gain).astype(bf16)
        normed[at, :] = normal
        projected = times_rows(normal, project[pl.ds(0, RANK + 256), :])
        inner = projected[:, :RANK]
        inner_scale = lax.rsqrt(jnp.mean(inner * inner, axis=1, keepdims=True) + norm_eps)
        content[at, :] = inner
        latent_scale[at, :] = inner_scale
        narrow = (inner * inner_scale * gain[...]).astype(bf16)
        compact[at, :] = narrow
        pair_rows = jnp.dot(narrow, expand[...], preferred_element_type=f32)
        both = projected[:, RANK + NOPE :]
        both = both * cosine[at, :] + swap_halves(both) * sine[at, :]
        lane = lax.broadcasted_iota(jnp.int32, both.shape, 1)
        queries[at, pl.ds(0, NOPE)] = projected[:, RANK : RANK + NOPE].astype(bf16)
        queries[at, pl.ds(NOPE, 128)] = jnp.where(lane < ROPE, both, 0.0).astype(bf16)
        keys[at, pl.ds(0, NOPE)] = pair_rows[:, :NOPE].astype(bf16)
        keys[at, pl.ds(NOPE, 128)] = jnp.where(
            lane < ROPE, pltpu.roll(both, 64, 1), 0.0
        ).astype(bf16)
        values[at, :] = pair_rows[:, NOPE:].astype(bf16)
    beside.second()
    deal.send(rows_at(low_gate, low), lanes(lows, 0, low), True)
    deal.send(rows_at(low_up, low), lanes(lows, low, low), False)
    deal.send(lambda column: router, lanes(lows, 2 * low, 16), True)
    deal.send(rows_at(low_down, low), lanes(lows, 2 * low + 16, low), True)

    def start_of(k):
        return pl.multiple_of(lax.rem(row + k, 4) * rows, rows)

    def block(k):
        return pl.ds(start_of(k), rows)

    def slot(k):
        return pl.ds(k * head, head)

    got = {}
    for k in order:
        scores = masked_scores(queries[block(k), :], keys[...], early[...], start_of(k))
        top = jnp.max(scores, axis=1, keepdims=True)
        powers = jnp.exp(scores - top)
        power_sum = jnp.sum(powers, axis=1, keepdims=True)
        log_total[block(k), :] = top + jnp.log(power_sum)
        probs = (powers / power_sum).astype(bf16)
        attended[block(k), :] = jnp.dot(
            probs, values[...], preferred_element_type=f32
        ).astype(bf16)
        for j, peer in ((2, across), (1, sibling)):
            got[j, k] = go(
                attended.at[block(k)],
                attended_rows.at[block(k), slot(j)],
                (as_, ar),
                (j - 1, k),
                col=peer,
            )
        attended_rows[block(k), slot(0)] = attended[block(k), :]
    beside.forward_first()
    for k in order:
        got[2, k].wait_recv()
        view = attended_rows.at[block(k), slot(2)]
        got[3, k] = go(view, attended_rows.at[block(k), slot(3)], (as_, ar), (2, k), col=sibling)
    for e in (0, 1):
        deal.send(lambda column, e=e: down.at[2 * column + e], lanes(downs, e * ff, ff), e == 1)
    sent = {}
    for k in order:
        got[1, k].wait_recv()
        got[3, k].wait_recv()
        result = jnp.dot(attended_rows[block(k), :], weight[...], preferred_element_type=f32)
        if k:
            out_buf[k - 1] = result.astype(bf16)
            sent[k] = go(
                out_buf.at[k - 1], in_buf.at[k - 1], (ps, pr), k - 1, row=lax.rem(row + k, 4)
            )
        else:
            acc[...] = result + inputs[...].astype(f32)
    total = acc[...]
    for k in (1, 3, 2):
        sent[k].wait_recv()
        total += in_buf[k - 1].astype(f32)
    middle[...] = total
    own[...] = total.astype(bf16)
    gather = Gather(own, full, sems[:6], go, row, sibling, across)
    gather.begin()
    beside.forward_rest()
    gather.second()
    gather.forward_first()
    gather.forward_rest()
    beside.finish()
    gather.finish()
    deal.finish()
    for copy in pending:
        copy.wait_send()


def front_step(
    input_rows, project, expand, weight, inputs, cotangent, cosine, sine, early, gain,
    up, down, low_gate, low_up, router, low_down,
):
    rows, columns = inputs.shape
    tokens, width = input_rows.shape
    low = low_down.shape[0] // 4

    def array(*shape, kind=bf16):
        return jax.ShapeDtypeStruct(shape, kind)

    return pl.pallas_call(
        front_kernel,
        out_shape=(
            array(rows, columns, kind=f32),
            array(tokens, width),
            array(tokens, columns),
            array(tokens, width),
            array(tokens, width),
            array(tokens, 1, kind=f32),
            array(tokens, RANK, kind=f32),
            array(tokens, 1, kind=f32),
            array(tokens, RANK),
            array(tokens, 256),
            array(tokens, 256),
            array(tokens, VDIM),
            array(tokens, 1, kind=f32),
            array(2 * up.shape[1], width),
            array(2 * up.shape[1], width),
            array(3 * low + 16, width),
        ),
        in_specs=[VMEM] * 10 + [HBM] * 6,
        out_specs=(VMEM,) * 13 + (HBM,) * 3,
        scratch_shapes=[
            pltpu.VMEM((tokens, VDIM), bf16),
            pltpu.VMEM((rows, columns), bf16),
            pltpu.VMEM((3, rows, columns), bf16),
            pltpu.VMEM((3, rows, columns), bf16),
            pltpu.VMEM((rows, columns), f32),
            *pair(3, 4),
            *pair(3),
            *gather_scratch,
            *gather_scratch,
            *deal_scratch(8),
        ],
        compiler_params=params(5),
        cost_estimate=cost(1 << 33, 150),
        name="front_step",
    )(
        input_rows, project, expand, weight, inputs, cotangent, cosine, sine, early, gain,
        up, down, low_gate, low_up, router, low_down,
    )


def attend_back_kernel(
    queries, keys, values, log_total, attended_grad, early, compact, content, latent_scale, gain,
    expand, cosine, sine, project, normed, input_rows, scale, attended_rows, residual_rows, router,
    normed_grad, narrow, query_part, ready,
    query_grad, key_grad, value_grad, pair_grad, project_grad, first_sum, gain_sum,
):
    tile = 256
    col = lax.axis_index("col")
    tokens = queries.shape[0]
    key_grad[...] = jnp.zeros_like(key_grad)
    value_grad[...] = jnp.zeros_like(value_grad)
    first_sum[...] = jnp.zeros_like(first_sum)
    gain_sum[...] = jnp.zeros_like(gain_sum)
    for i in range(tokens // tile):
        at = pl.ds(i * tile, tile)
        query = queries[at, :]
        upstream = attended_grad[at, :]
        scores = masked_scores(query, keys[...], early[...], i * tile)
        probs = jnp.exp(scores - log_total[at, :])
        value_grad[...] += over_units(probs.astype(bf16), upstream)
        weight_grad = times_rows(upstream, values[...])
        centre = jnp.sum(probs * weight_grad, axis=1, keepdims=True)
        score_grad = (probs * (weight_grad - centre)).astype(bf16)
        query_grad[at, :] = (
            jnp.dot(score_grad, keys[...], preferred_element_type=f32) * score_scale
        )
        key_grad[...] += over_units(score_grad, query)
    for i in range(tokens // tile):
        at = pl.ds(i * tile, tile)
        keys_back = key_grad[at, :] * score_scale
        query_back = query_grad[at, :]
        pair_rows = jnp.concatenate([keys_back[:, :NOPE], value_grad[at, :]], axis=1).astype(bf16)
        pair_grad[at, :] = pair_rows
        compact_grad = times_rows(pair_rows, expand[...])
        inner = content[at, :]
        scales = latent_scale[at, :]
        weighted = compact_grad * gain[...]
        inner_sum = jnp.sum(weighted * inner, axis=1, keepdims=True)
        content_grad = scales * weighted - inner * (scales * scales * scales * inner_sum / RANK)
        gain_sum[...] += jnp.sum(compact_grad * inner * scales, axis=0, keepdims=True)
        both = query_back[:, NOPE:]
        lane = lax.broadcasted_iota(jnp.int32, both.shape, 1)
        both = jnp.where(lane < ROPE, both, pltpu.roll(keys_back[:, NOPE:], 64, 1))
        both = both * cosine[at, :] - swap_halves(both) * sine[at, :]
        rows = jnp.concatenate([content_grad, query_back[:, :NOPE], both], axis=1).astype(bf16)
        project_grad[at, :] = rows
        back = jnp.dot(rows, project[pl.ds(0, RANK + 256), :], preferred_element_type=f32)
        normed_grad[at, :] = back.astype(bf16)
        first_sum[...] += jnp.sum(
            back * (input_rows[at, :].astype(f32) * scale[at, :]), axis=0, keepdims=True
        )
    each = narrow.shape[0] // 4
    lat = each - 16
    for k in range(4):
        lanes_at = pl.ds(512 * k, 512)
        part = over_units(project_grad[...], normed[:, lanes_at]).astype(bf16)
        query_part[:, lanes_at] = part[RANK : RANK + 192]
        latent_part = jnp.concatenate([part[:RANK], part[RANK + 192 :]], axis=0)
        extra = jnp.concatenate(
            [
                gain_sum[...],
                first_sum[:, lanes_at],
                router[pl.ds(0, EXPERTS), lanes_at].astype(f32),
                jnp.zeros((6, 512), f32),
            ],
            axis=0,
        ).astype(bf16)
        for r in range(4):
            narrow[pl.ds(r * each, lat), lanes_at] = latent_part[r * lat : (r + 1) * lat]
            narrow[pl.ds(r * each + lat, 16), lanes_at] = extra
    head_grad = over_units(attended_rows[...], residual_rows[...]).astype(bf16)
    for k in range(4):
        own = lax.rem(lax.rem(col, 2) + k % 2, 2) + 2 * lax.rem(col // 2 + k // 2, 2)
        start = pl.multiple_of(own * VDIM, VDIM)
        ready[pl.ds(start, VDIM), :] = head_grad[k * VDIM : (k + 1) * VDIM]
    ready[pl.ds(4 * VDIM, 256), :] = over_units(pair_grad[...], compact[...]).astype(bf16)


def attend_back_step(*arguments):
    tokens, width = arguments[15].shape
    return pl.pallas_call(
        attend_back_kernel,
        out_shape=(
            jax.ShapeDtypeStruct((tokens, width), bf16),
            jax.ShapeDtypeStruct((RANK + ROPE + 64, width), bf16),
            jax.ShapeDtypeStruct((192, width), bf16),
            jax.ShapeDtypeStruct((768, 512), bf16),
        ),
        in_specs=[VMEM] * 20,
        out_specs=(VMEM,) * 4,
        scratch_shapes=[
            pltpu.VMEM((tokens, 256), f32),
            pltpu.VMEM((tokens, 256), f32),
            pltpu.VMEM((tokens, VDIM), f32),
            pltpu.VMEM((tokens, 256), bf16),
            pltpu.VMEM((tokens, RANK + 256), bf16),
            pltpu.VMEM((1, width), f32),
            pltpu.VMEM((1, RANK), f32),
        ],
        compiler_params=pltpu.CompilerParams(vmem_limit_bytes=56 << 20),
        cost_estimate=cost(1 << 34, 40),
        name="attend_back_step",
    )(*arguments)


def rotary_tables(length, half_width):
    position = jnp.arange(length, dtype=f32)[:, None]
    frequency = jnp.exp(jnp.arange(half_width, dtype=f32) * (-math.log(10000.0) / half_width))
    angles = position * frequency[None, :]
    return (jnp.cos(angles), jnp.sin(angles))


def pad_to(values, axis, size):
    widths = [(0, 0)] * values.ndim
    widths[axis] = (0, size - values.shape[axis])
    return jnp.pad(values, widths)


def on_device(
    inputs,
    attention_gain,
    query_weight,
    latent_weight,
    latent_gain,
    expand_weight,
    output_weight,
    feedforward_gain,
    router_weight,
    shared_gate,
    shared_up,
    shared_down,
    expert_gate,
    expert_up,
    expert_down,
    routes,
    prefix,
    cotangent,
):
    row = lax.axis_index("row")
    col = lax.axis_index("col")
    prefix_len = prefix[0]
    cos_table, sin_table = rotary_tables(SEQ, ROPE // 2)
    first_gain = attention_gain.astype(f32)
    second_gain = feedforward_gain.astype(f32)
    compact_gain = latent_gain.astype(f32)
    rows = inputs.shape[0]
    ff = expert_gate.shape[2]
    low = shared_down.shape[0] // 4
    cosine = jnp.tile(cos_table, (1, 4))
    sine = jnp.tile(jnp.concatenate([-sin_table, sin_table], axis=1), (1, 2))
    early = (jnp.arange(SEQ, dtype=jnp.int32) < prefix_len).astype(f32)[None, :]

    gains = jnp.stack([attention_gain, feedforward_gain])
    common = jnp.concatenate([latent_weight.T, pad_to(gains, 0, 16)], axis=0)
    input_rows, project_all, gates = start_step(
        inputs, common, query_weight.T, expert_gate.transpose(0, 2, 1)
    )
    second_all = project_all[RANK + 257].astype(f32)
    out_weight = jnp.concatenate(
        [lax.dynamic_slice_in_dim(output_weight, (col ^ k) * VDIM, VDIM, 0) for k in range(4)],
        axis=0,
    )
    (
        residual_mid,
        middle_rows,
        attended_rows,
        out_grad,
        normed,
        scale_one,
        content,
        latent_scale,
        compact,
        queries,
        keys,
        values,
        log_total,
        ups,
        downs,
        lows,
    ) = front_step(
        input_rows,
        project_all,
        expand_weight,
        out_weight,
        inputs,
        cotangent,
        cosine,
        sine,
        early,
        compact_gain[None, :],
        expert_up.transpose(0, 2, 1),
        expert_down,
        shared_gate.T,
        shared_up.T,
        pad_to(router_weight.T, 0, 16),
        shared_down,
    )

    experts = jnp.arange(EXPERTS, dtype=jnp.int32)
    named = jnp.any(routes.T[None, :, :] == experts[:, None, None], axis=1).astype(f32)
    mine = (experts[:, None] == 2 * col + jnp.arange(128, dtype=jnp.int32)[None, :]).astype(f32)
    hidden, scale_two, act, delta, combined = expert_step(
        middle_rows, out_grad, gates, ups, downs, lows, second_all[None, :], named, mine
    )
    expert_grad, shared_grad, router_part, combined_sum, hidden_grad = grads_step(
        hidden, out_grad, delta, act, combined, gates, ups, lows
    )
    output = (residual_mid + combined_sum).astype(bf16)
    expert_sum = lax.psum_scatter(expert_grad, "dp", scatter_dimension=0, tiled=True)[0]

    my_scale_one = lax.dynamic_slice_in_dim(scale_one, row * rows, rows, 0)
    my_scale_two = lax.dynamic_slice_in_dim(scale_two[:, :1], row * rows, rows, 0)
    residual_grad, residual_rows, attended_grad, second_gain_part, shared_all = middle_step(
        hidden_grad,
        residual_mid,
        cotangent,
        my_scale_two,
        second_gain[None, :],
        out_weight,
        shared_grad,
    )
    normed_grad, narrow_part, query_part, ready = attend_back_step(
        queries,
        keys,
        values,
        log_total,
        attended_grad,
        early,
        compact,
        content,
        latent_scale,
        compact_gain[None, :],
        expand_weight,
        cosine,
        sine,
        project_all,
        normed,
        input_rows,
        scale_one,
        attended_rows,
        residual_rows,
        router_part,
    )
    inputs_grad, sums, narrow, gains, latent_small = tail_step(
        normed_grad,
        narrow_part,
        query_part,
        ready,
        residual_grad,
        inputs,
        my_scale_one,
        first_gain[None, :],
        second_gain_part,
    )
    sums, narrow, shared_all, expert_sum = lax.optimization_barrier(
        (sums, narrow, shared_all, expert_sum)
    )
    pairs = [
        (dp * 4 + c, (2 * c + dp // 4) * 4 + (c ^ (dp % 4))) for dp in range(8) for c in range(4)
    ]
    expert_sum = lax.ppermute(expert_sum, ("dp", "col"), pairs)
    output_weight_grad = sums[:512].astype(f32)
    expand_grad = sums[512:768].T.astype(f32)
    query_weight_grad = sums[768:].T.astype(f32)
    latent_weight_grad = narrow.reshape(-1, 512).T.astype(f32)
    latent_gain_grad = latent_small[0, 0].astype(f32)
    own_small = lax.dynamic_index_in_dim(latent_small, col, 0, False).astype(f32)
    first_gain_grad = own_small[1]
    router_grad = own_small[2 : 2 + EXPERTS].T
    second_gain_grad = gains[0]

    expert_sum = expert_sum.astype(f32)
    expert_gate_grad = expert_sum[None, :ff].transpose(0, 2, 1)
    expert_up_grad = expert_sum[None, ff : 2 * ff].transpose(0, 2, 1)
    expert_down_grad = expert_sum[None, 2 * ff :]
    shared_sum = shared_all.astype(f32)
    shared_gate_grad = shared_sum[:, :low].reshape(4 * low, 512).T
    shared_up_grad = shared_sum[:, low : 2 * low].reshape(4 * low, 512).T
    shared_down_grad = shared_sum[:, 2 * low : 3 * low].reshape(4 * low, 512)
    return (
        output,
        inputs_grad,
        first_gain_grad,
        query_weight_grad,
        latent_weight_grad,
        latent_gain_grad,
        expand_grad,
        output_weight_grad,
        second_gain_grad,
        router_grad,
        shared_gate_grad,
        shared_up_grad,
        shared_down_grad,
        expert_gate_grad,
        expert_up_grad,
        expert_down_grad,
    )


def solution(mesh):
    placed = (
        P(("dp", "row"), "col"),
        P("col"),
        P("col", "row"),
        P("col", None),
        P(),
        P(None, ("row", "col")),
        P("row", "col"),
        P("col"),
        P("col", None),
        P("col", "row"),
        P("col", "row"),
        P("row", "col"),
        P(None, "col", "row"),
        P(None, "col", "row"),
        P(None, "row", "col"),
        P("dp", None),
        P("dp"),
        P(("dp", "row"), "col"),
    )
    return jax.shard_map(
        on_device,
        mesh=mesh,
        in_specs=placed,
        out_specs=(
            P(("dp", "row"), "col"),
            P(("dp", "row"), "col"),
            P("col"),
            P("col", "row"),
            P("col", None),
            P(),
            P(None, ("row", "col")),
            P("row", "col"),
            P("col"),
            P("col", None),
            P("col", "row"),
            P("col", "row"),
            P("row", "col"),
            P("dp", "col", "row"),
            P("dp", "col", "row"),
            P("dp", "row", "col"),
        ),
        check_vma=False,
    )
```

```python
import functools
import math

import jax
import jax.numpy as jnp
from jax import lax
from jax.experimental import pallas as pl
from jax.experimental.pallas import tpu as pltpu
from jax.sharding import PartitionSpec as P

D = 2048
NOPE = 128
ROPE = 64
VDIM = 128
RANK = 512
TOPK = 6
EXPERTS = 8
SEQ = 1024

norm_eps = 1e-06
masked_score = -1e30
bf16 = jnp.bfloat16
f32 = jnp.float32
MESH = pl.DeviceIdType.MESH
DMA = pltpu.SemaphoreType.DMA
VMEM = pl.BlockSpec(memory_space=pltpu.VMEM)
HBM = pl.BlockSpec(memory_space=pl.ANY)


def place():
    row = lax.axis_index("row")
    col = lax.axis_index("col")
    sibling = col + 1 - 2 * lax.rem(col, 2)
    across = lax.rem(col + 2, 4)
    return (row, sibling, across, lax.rem(sibling + 2, 4))


def greet(columns, row, others=()):
    barrier = pltpu.get_barrier_semaphore()
    targets = [{"col": column} for column in columns]
    targets += [{"row": lax.rem(row + step, 4)} for step in (1, 2, 3)]
    targets += list(others)
    for target in targets:
        pl.semaphore_signal(barrier, inc=1, device_id=target, device_id_type=MESH)
    pl.semaphore_wait(barrier, len(targets))


def along_z(dp, step):
    return dp // 4 * 4 + lax.rem(lax.rem(dp, 4) + step, 4)


def remote(source, target, sems, at, **device):
    return pltpu.make_async_remote_copy(
        src_ref=source,
        dst_ref=target,
        send_sem=sems[0].at[at],
        recv_sem=sems[1].at[at],
        device_id=device,
        device_id_type=MESH,
    )


def starter(pending):
    def go(*arguments, **device):
        copy = remote(*arguments, **device)
        copy.start()
        pending.append(copy)
        return copy

    return go


def pair(*shape):
    return [DMA(shape), DMA(shape)]


def params(collective):
    return pltpu.CompilerParams(
        collective_id=collective, has_side_effects=True, vmem_limit_bytes=52 << 20
    )


def cost(flops, mebibytes):
    return pl.CostEstimate(flops=flops, bytes_accessed=mebibytes << 20, transcendentals=0)


class Gather:
    def __init__(self, own, full, sems, go, row, sibling, across):
        self.own, self.full, self.go = own, full, go
        self.xs, self.ys, self.cs = sems[0:2], sems[2:4], sems[4:6]
        self.row, self.sibling, self.across = row, sibling, across
        self.arrivals, self.halves = [], []

    def block(self, at_row, at_col):
        rows, columns = self.own.shape
        start = pl.multiple_of(at_row * rows, rows)
        return self.full.at[pl.ds(start, rows), pl.ds(at_col * columns, columns)]

    def along(self, source, target, base):
        return [
            self.go(source, target, self.ys, base + n, row=lax.rem(self.row + k, 4))
            for n, k in enumerate((1, 3))
        ]

    def over(self, source, target):
        count = len(self.arrivals)
        self.arrivals.append(self.go(source, target, self.cs, count, col=self.sibling))

    def begin(self):
        row = self.row
        rows, columns = self.own.shape
        self.side = self.go(self.own, self.block(row, 2), self.xs, 0, col=self.across)
        self.first = self.along(self.own, self.block(row, 0), 0)
        self.over(self.own, self.block(row, 1))
        start = pl.multiple_of(row * rows, rows)
        self.full[pl.ds(start, rows), pl.ds(0, columns)] = self.own[...]

    def second(self):
        self.side.wait_recv()
        here = self.block(self.row, 2)
        self.rest = self.along(here, here, 2)
        self.over(here, self.block(self.row, 3))

    def forward(self, group, at_col, base):
        rows, columns = self.own.shape
        for n, k in enumerate((1, 3)):
            group[n].wait_recv()
            source = lax.rem(self.row + 4 - k, 4)
            start = pl.multiple_of(source * rows + n * (rows // 2), rows // 2)
            half = self.full.at[pl.ds(start, rows // 2), pl.ds(at_col * columns, columns)]
            self.halves.append(
                self.go(half, half, self.ys, base + n, row=lax.rem(self.row + k, 4))
            )
            self.over(self.block(source, at_col), self.block(source, at_col + 1))

    def forward_first(self):
        self.forward(self.first, 0, 4)

    def forward_rest(self):
        self.forward(self.rest, 2, 6)

    def finish(self):
        facing = lax.rem(self.row + 2, 4)
        for n, at_col in enumerate((0, 2)):
            for copy in self.halves[2 * n : 2 * n + 2]:
                copy.wait_recv()
            self.over(self.block(facing, at_col), self.block(facing, at_col + 1))
        for copy in self.arrivals:
            copy.wait_recv()


gather_scratch = pair(1) + pair(8) + pair(8)


def pair_along_z():
    dp = lax.axis_index("dp")
    return dp + 1 - 2 * lax.rem(dp, 2)


class Deal:
    def __init__(self, sems, local_sems, pending, col, peers):
        self.go, self.sems, self.local_sems = starter(pending), sems, local_sems
        self.col, self.peers = col, peers
        self.far = lax.rem(lax.axis_index("dp") + 4, 8)
        self.copies, self.local, self.open, self.count = [], [], [], 0

    def send(self, source, target, flip):
        n = self.count
        self.count += 1
        copy = pltpu.make_async_copy(source(self.col), target(0), self.local_sems.at[n])
        copy.start()
        self.local.append(copy)
        for k, peer in ((2, self.peers[1]), (3, self.peers[2]), (1, self.peers[0])):
            place_at = {"col": peer}
            if flip and k != 1:
                place_at["dp"] = self.far
            self.copies.append(
                self.go(source(peer), target(k), self.sems, (k - 1, n), **place_at)
            )

    def send_pair(self, source, array, size):
        n = self.count
        self.count += 2
        sibling, across, corner = self.peers
        z = lax.rem(lax.axis_index("dp"), 4)
        mine = lax.rem(z, 2)
        for e in (0, 1):
            at = pl.ds(e * size, size)
            copy = pltpu.make_async_copy(
                source(self.col, e), array.at[at, pl.ds(0, 512)], self.local_sems.at[n + e]
            )
            copy.start()
            self.local.append(copy)
            self.copies.append(
                self.go(
                    source(sibling, e),
                    array.at[at, pl.ds(512, 512)],
                    self.sems,
                    (0, n + e),
                    col=sibling,
                )
            )
        at = pl.ds(pl.multiple_of(mine * size, size), size)
        near = self.go(
            source(across, mine), array.at[at, pl.ds(1024, 512)], self.sems, (1, n), col=across
        )
        far = self.go(
            source(corner, mine),
            array.at[at, pl.ds(1536, 512)],
            self.sems,
            (2, n),
            col=corner,
            dp=self.far,
        )
        self.open.append((near, far, array.at[at, pl.ds(1024, 1024)], n + 1))

    def exchange(self):
        for near, far, view, n in self.open:
            near.wait_recv()
            far.wait_recv()
            self.copies.append(self.go(view, view, self.sems, (1, n), dp=pair_along_z()))
        self.open = []

    def finish(self):
        for copy in self.local:
            copy.wait()
        for copy in self.copies:
            copy.wait_recv()


def deal_scratch(count):
    return pair(3, count) + [DMA((count,))]


def deal_peers(peers):
    far = lax.rem(lax.axis_index("dp") + 4, 8)
    return [{"dp": far, "col": peer} for peer in peers[1:]]


def lanes(array, start, size):
    return lambda k: array.at[pl.ds(start, size), pl.ds(512 * k, 512)]


def rows_at(array, size):
    return lambda column: array.at[pl.ds(pl.multiple_of(column * size, size), size)]


def start_kernel(
    inputs, common, query, full, project, *sems,
):
    row, sibling, across, corner = place()
    col = lax.axis_index("col")
    peers = (sibling, across, corner)
    greet(peers, row, deal_peers(peers))
    pending = []
    go = starter(pending)
    gather = Gather(inputs, full, sems[0:6], go, row, sibling, across)
    deal = Deal(sems[6:8], sems[8], pending, col, peers)
    gather.begin()
    deal.send(lambda column: common.at[pl.ds(0, RANK)], lanes(project, 0, RANK), True)
    deal.send(rows_at(query, 192), lanes(project, RANK, 192), False)
    deal.send(lambda column: common.at[pl.ds(RANK, 80)], lanes(project, RANK + 192, 80), False)
    gather.second()
    gather.forward_first()
    gather.forward_rest()
    gather.finish()
    deal.finish()
    for copy in pending:
        copy.wait_send()


def start_step(inputs, common, query):
    rows, columns = inputs.shape
    return pl.pallas_call(
        start_kernel,
        out_shape=(
            jax.ShapeDtypeStruct((4 * rows, 4 * columns), bf16),
            jax.ShapeDtypeStruct((RANK + 272, 4 * columns), bf16),
        ),
        in_specs=[VMEM] + [HBM] * 2,
        out_specs=(VMEM, HBM),
        scratch_shapes=[*gather_scratch, *deal_scratch(3)],
        compiler_params=params(0),
        cost_estimate=cost(0, 150),
        name="start_step",
    )(inputs, common, query)


def reduce_scratch(rows, columns):
    return [
        pltpu.VMEM((4, 2, rows, columns), bf16),
        pltpu.VMEM((3, 2, rows, columns), bf16),
        pltpu.VMEM((3, 2, rows, columns), bf16),
        pltpu.VMEM((2, rows, columns), f32),
        pltpu.VMEM((2, rows, columns), bf16),
        *pair(1),
        *pair(3, 2),
        *pair(4, 2),
    ]


class Reduction:
    order = (2, 1, 3, 0)

    def __init__(self, part, scratch, row, sibling, across):
        self.part = part
        self.held, self.out_buf, self.in_buf, self.acc, self.side_buf = scratch[:5]
        self.xs, self.ys, self.cs = scratch[5:7], scratch[7:9], scratch[9:11]
        self.row, self.sibling, self.across = row, sibling, across
        self.rows, self.columns = self.acc.shape[1:]

    def rows_of(self, k):
        start = lax.rem(self.row + k, 4) * self.rows
        return pl.ds(pl.multiple_of(start, self.rows), self.rows)

    def pair_copy(self, k, x):
        return remote(
            self.part.at[self.rows_of(k), pl.ds((2 * x + 1) * self.columns, self.columns)],
            self.held.at[k, x],
            self.cs,
            (k, x),
            col=self.sibling,
        )

    def along_copy(self, k, x):
        return remote(
            self.out_buf.at[k - 1, x],
            self.in_buf.at[k - 1, x],
            self.ys,
            (k - 1, x),
            row=lax.rem(self.row + k, 4),
        )

    def side_copy(self):
        return remote(self.side_buf.at[0], self.side_buf.at[1], self.xs, 0, col=self.across)

    def start(self):
        for x in (1, 0):
            for k in self.order:
                self.pair_copy(k, x).start()

    def along_one(self, k, x):
        self.pair_copy(k, x).wait_recv()
        mine = self.part[self.rows_of(k), pl.ds(2 * x * self.columns, self.columns)]
        value = mine.astype(f32) + self.held[k, x].astype(f32)
        if k:
            self.out_buf[k - 1, x] = value.astype(bf16)
            self.along_copy(k, x).start()
        else:
            self.acc[x] = value

    def along(self):
        for x in (1, 0):
            for k in self.order:
                self.along_one(k, x)

    def collect(self, x):
        for k in (1, 3, 2):
            self.along_copy(k, x).wait_recv()
            self.acc[x] += self.in_buf[k - 1, x].astype(f32)

    def over(self):
        self.collect(1)
        self.side_buf[0] = self.acc[1].astype(bf16)
        self.side_copy().start()

    def side(self):
        self.over()
        self.collect(0)

    def total(self):
        self.side_copy().wait_recv()
        return self.acc[0] + self.side_buf[1].astype(f32)

    def finish(self):
        for k in self.order:
            for x in (0, 1):
                self.pair_copy(k, x).wait_send()
                if k:
                    self.along_copy(k, x).wait_send()
        self.side_copy().wait_send()


def product(left, right):
    return jnp.dot(left, right, preferred_element_type=f32).astype(bf16)


def times_rows(left, right):
    return lax.dot_general(left, right, (((1,), (1,)), ((), ())), preferred_element_type=f32)


def over_units(left, right):
    return lax.dot_general(left, right, (((0,), (0,)), ((), ())), preferred_element_type=f32)


def expert_kernel(
    middle, out_grad, gates, ups, downs, lows, gain, named, mine,
    hidden, scale, act, delta, combined,
):
    values = middle[...].astype(f32)
    scales = lax.rsqrt(jnp.mean(values * values, axis=1, keepdims=True) + norm_eps)
    scale[...] = jnp.broadcast_to(scales, scale.shape)
    normal = (values * scales * gain[...]).astype(bf16)
    hidden[...] = normal
    upstream = out_grad[...]
    ff = gates.shape[0] // 2
    low = (lows.shape[0] - 16) // 3
    low_pre = times_rows(lows[pl.ds(0, 2 * low + 16), :], normal)
    logits = low_pre[2 * low : 2 * low + EXPERTS]
    powers = jnp.exp(logits - jnp.max(logits, axis=0, keepdims=True))
    probs = powers / jnp.sum(powers, axis=0, keepdims=True)
    names = named[...]
    probs_part = jnp.zeros_like(probs)
    for e in range(3):
        if e < 2:
            size, at = ff, pl.ds(e * ff, ff)
            gate_pre = times_rows(gates[at, :], normal)
            up_pre = times_rows(ups[at, :], normal)
            act_grad = times_rows(downs[at, :], upstream)
            own = mine[:, e : e + 1]
            weight = jnp.sum(probs * names * own, axis=0, keepdims=True)
            gate_at, up_at, act_at = e * ff, (2 + e) * ff, e * ff
        else:
            size = low
            gate_pre, up_pre = low_pre[:low], low_pre[low : 2 * low]
            act_grad = times_rows(lows[pl.ds(2 * low + 16, low), :], upstream)
            weight = 1.0
            gate_at, up_at, act_at = 4 * ff, 4 * ff + low, 2 * ff
        sig = 1.0 / (1.0 + jnp.exp(-gate_pre))
        silu = gate_pre * sig
        both = silu * up_pre
        act[pl.ds(act_at, size), :] = (weight * both).astype(bf16)
        weighted = weight * act_grad
        delta[pl.ds(gate_at, size), :] = (
            weighted * up_pre * (sig * (1.0 + gate_pre * (1.0 - sig)))
        ).astype(bf16)
        delta[pl.ds(up_at, size), :] = (weighted * silu).astype(bf16)
        if e < 2:
            named_sum = jnp.sum(act_grad * both, axis=0, keepdims=True)
            probs_part = probs_part + named_sum * own * names
    logits_part = probs * (probs_part - jnp.sum(probs * probs_part, axis=0, keepdims=True))
    delta[pl.ds(4 * ff + 2 * low, 16), :] = jnp.concatenate(
        [logits_part, jnp.zeros_like(logits_part)], axis=0
    ).astype(bf16)
    combined[...] = (
        over_units(act[pl.ds(0, 2 * ff), :], downs[...])
        + over_units(act[pl.ds(2 * ff, low), :], lows[pl.ds(2 * low + 16, low), :])
    ).astype(bf16)


def whole(value):
    return pl.BlockSpec(value.shape, lambda i: (0,) * len(value.shape))


def once(value):
    return pl.BlockSpec(
        value.shape, lambda i: (0,) * len(value.shape), pipeline_mode=pl.Buffered(1)
    )


def expert_step(middle, out_grad, gates, ups, downs, lows, gain, named, mine):
    tile = 256
    tokens, width = middle.shape
    wide = pl.BlockSpec((tile, width), lambda i: (i, 0))

    def tall(rows):
        return pl.BlockSpec((rows, tile), lambda i: (0, i))

    acts = downs.shape[0] + (lows.shape[0] - 16) // 3
    deltas = gates.shape[0] + ups.shape[0] + 2 * (lows.shape[0] - 16) // 3 + 16
    return pl.pallas_call(
        expert_kernel,
        grid=(tokens // tile,),
        out_shape=(
            jax.ShapeDtypeStruct((tokens, width), bf16),
            jax.ShapeDtypeStruct((tokens, 128), f32),
            jax.ShapeDtypeStruct((acts, tokens), bf16),
            jax.ShapeDtypeStruct((deltas, tokens), bf16),
            jax.ShapeDtypeStruct((tokens, width), bf16),
        ),
        in_specs=[
            wide,
            wide,
            whole(gates),
            whole(ups),
            whole(downs),
            whole(lows),
            whole(gain),
            tall(EXPERTS),
            whole(mine),
        ],
        out_specs=(
            wide,
            pl.BlockSpec((tile, 128), lambda i: (i, 0)),
            tall(acts),
            tall(deltas),
            wide,
        ),
        compiler_params=pltpu.CompilerParams(vmem_limit_bytes=56 << 20),
        cost_estimate=cost(2 * 5 * gates.shape[0] * width * tokens, 30),
        name="expert_step",
    )(middle, out_grad, gates, ups, downs, lows, gain, named, mine)


def grads_kernel(
    hidden, out_grad, delta, act, combined, gates, ups, lows,
    grads, shared, router, total, hidden_grad,
    own_shared, chunk_in, ps, pr, *scratch, ff, low,
):
    step = pl.program_id(0)
    row, sibling, across, corner = place()
    dp = lax.axis_index("dp")
    z = lax.rem(dp, 4)
    steps = Reduction(combined, scratch, row, sibling, across)
    piece = shared.shape[1]

    def quarter(at):
        return pl.ds(pl.multiple_of(at * piece, piece), piece)

    def scattered(k):
        return remote(
            own_shared.at[:, quarter(lax.rem(z + k, 4))],
            chunk_in.at[k - 1],
            (ps, pr),
            k - 1,
            dp=along_z(dp, k),
        )

    @pl.when(step == 0)
    def _():
        greet((sibling, across), row, [{"dp": along_z(dp, k)} for k in (1, 2, 3)])
        steps.start()

    for at, blocks in (
        (1, ((2, 1), (1, 1), (3, 1))),
        (2, ((0, 1), (2, 0), (1, 0))),
        (3, ((3, 0), (0, 0))),
    ):

        @pl.when(step == at)
        def _(blocks=blocks):
            for k, x in blocks:
                steps.along_one(k, x)

    @pl.when(step == 8)
    def _():
        steps.over()

    for k in range(4):

        @pl.when(step == k)
        def _(k=k):
            base = 4 * ff
            own_shared[k, pl.ds(0, low), :] = product(delta[pl.ds(base, low), :], hidden[...])
            own_shared[k, pl.ds(low, low), :] = product(
                delta[pl.ds(base + low, low), :], hidden[...]
            )
            router[...] = product(delta[pl.ds(base + 2 * low, 16), :], hidden[...])
            own_shared[k, pl.ds(2 * low, low), :] = product(
                act[pl.ds(2 * ff, low), :], out_grad[...]
            )
            spare = 4 * piece - 3 * low
            own_shared[k, pl.ds(3 * low, spare), :] = jnp.zeros((spare, 512), bf16)

    @pl.when(step == 3)
    def _():
        for k in (1, 2, 3):
            scattered(k).start()

    for e in (0, 1):

        @pl.when(step // 4 == e + 1)
        def _(e=e):
            at = e * ff
            grads[0, pl.ds(0, ff), :] = product(delta[pl.ds(at, ff), :], hidden[...])
            grads[0, pl.ds(ff, ff), :] = product(delta[pl.ds(2 * ff + at, ff), :], hidden[...])
            grads[0, pl.ds(2 * ff, ff), :] = product(act[pl.ds(at, ff), :], out_grad[...])

    @pl.when(step >= 12)
    def _():
        at = pl.ds(pl.multiple_of((step - 12) * 256, 256), 256)
        hidden_grad[...] = (
            over_units(delta[pl.ds(0, 2 * ff), at], gates[...])
            + over_units(delta[pl.ds(2 * ff, 2 * ff), at], ups[...])
            + over_units(delta[pl.ds(4 * ff, 2 * low + 16), at], lows[pl.ds(0, 2 * low + 16), :])
        ).astype(bf16)

    @pl.when(step == 15)
    def _():
        steps.collect(0)
        total[...] = steps.total()
        summed = own_shared[:, quarter(z), :].astype(f32)
        for k in (1, 2, 3):
            scattered(k).wait_recv()
            summed += chunk_in[k - 1].astype(f32)
        shared[...] = summed.astype(bf16)
        for k in (1, 2, 3):
            scattered(k).wait_send()
        steps.finish()


def grads_step(hidden, out_grad, delta, act, combined, gates, ups, lows):
    tokens = hidden.shape[0]
    ff, low = gates.shape[0] // 2, (lows.shape[0] - 16) // 3
    piece = -(-3 * low // 64) * 16
    wide = pl.BlockSpec((tokens, 512), lambda i: (0, i % 4))
    return pl.pallas_call(
        functools.partial(grads_kernel, ff=ff, low=low),
        grid=(16,),
        out_shape=(
            jax.ShapeDtypeStruct((8, 3 * ff, 512), bf16),
            jax.ShapeDtypeStruct((4, piece, 512), bf16),
            jax.ShapeDtypeStruct((16, D), bf16),
            jax.ShapeDtypeStruct((tokens // 4, 512), f32),
            jax.ShapeDtypeStruct((tokens, D), bf16),
        ),
        in_specs=[wide, wide] + [once(v) for v in (delta, act, combined, gates, ups, lows)],
        out_specs=(
            pl.BlockSpec((1, 3 * ff, 512), lambda i: (jnp.clip(i - 4, 0, 7), 0, 0)),
            pl.BlockSpec((4, piece, 512), lambda i: (0, 0, 0)),
            pl.BlockSpec((16, 512), lambda i: (0, jnp.minimum(i, 3))),
            pl.BlockSpec((tokens // 4, 512), lambda i: (0, 0)),
            pl.BlockSpec((256, D), lambda i: (jnp.maximum(i - 12, 0), 0)),
        ),
        scratch_shapes=[
            pltpu.VMEM((4, 4 * piece, 512), bf16),
            pltpu.VMEM((3, 4, piece, 512), bf16),
            *pair(3),
            *reduce_scratch(tokens // 4, 512),
        ],
        compiler_params=params(1),
        cost_estimate=cost(2 * 8 * 4 * ff * 512 * tokens, 60),
        name="grads_step",
    )(hidden, out_grad, delta, act, combined, gates, ups, lows)


class ColumnSum:
    def __init__(self, value, buf, sems, go, peers):
        self.buf = buf
        buf[0] = jnp.broadcast_to(value, (value.shape[0], 128)).T[:8]
        self.sent = [
            go(buf.at[0], buf.at[k + 1], sems, k, col=peer) for k, peer in enumerate(peers)
        ]

    def total(self):
        for copy in self.sent:
            copy.wait_recv()
        buf = self.buf
        total = (buf[0] + buf[1]) + (buf[2] + buf[3])
        return jnp.broadcast_to(total[:1], (128, total.shape[1])).T[:, :1]


def middle_kernel(
    part, middle, cotangent, scale, gain, weight, shared,
    residual_grad, residual_rows, attended_grad, gain_part, shared_all,
    sum_buf, out_buf, in_buf, acc, chunk_in, both, ss, sr, rs, rr, hs, hr, ps, pr, *scratch,
):
    row, sibling, across, corner = place()
    dp = lax.axis_index("dp")
    z = lax.rem(dp, 4)
    col = lax.axis_index("col")
    piece = shared.shape[1]
    quarter = pl.ds(pl.multiple_of(z * piece, piece), piece)
    far = lax.rem(dp + 4, 8)
    peers = (sibling, across, corner)
    greet(peers, row, [{"dp": along_z(dp, k)} for k in (1, 2, 3)] + [{"dp": far}])
    pending = []
    go = starter(pending)
    steps = Reduction(part, scratch, row, sibling, across)
    rows, columns = middle.shape
    head = attended_grad.shape[1]
    steps.start()
    halves = go(shared, chunk_in, (ps, pr), 0, dp=far)
    steps.along()
    steps.over()
    halves.wait_recv()
    both[...] = (shared[...].astype(f32) + chunk_in[...].astype(f32)).astype(bf16)
    shared_all[col, quarter, :] = both[0]
    home = [
        go(both.at[j + 1], shared_all.at[col, quarter], (ps, pr), 1 + j, col=peer)
        for j, peer in enumerate(peers)
    ]
    steps.collect(0)
    upstream = steps.total()
    weighted = upstream * gain[...]
    values = middle[...]
    scales = scale[...]
    inner = ColumnSum(
        jnp.sum(weighted * values, axis=1, keepdims=True), sum_buf, (ss, sr), go, peers
    )
    gain_part[...] = jnp.sum(upstream * values * scales, axis=0, keepdims=True)
    for copy in home:
        copy.wait_recv()
    spread = [
        go(
            shared_all.at[:, quarter],
            shared_all.at[:, quarter],
            (ps, pr),
            3 + k,
            dp=along_z(dp, k),
        )
        for k in (1, 2, 3)
    ]
    base = cotangent[...].astype(f32) + scales * weighted
    grad = base - values * (scales * scales * scales * inner.total() / D)
    residual_grad[...] = grad

    def block(at_row):
        return pl.ds(pl.multiple_of(at_row * rows, rows), rows)

    residual_rows[block(row), :] = grad.astype(bf16)
    sent = [
        go(
            residual_rows.at[block(row)],
            residual_rows.at[block(row)],
            (rs, rr),
            k - 1,
            row=lax.rem(row + k, 4),
        )
        for k in (1, 2, 3)
    ]
    got = []
    for k in (0, 1, 3, 2):
        source = lax.rem(row + 4 - k, 4)
        if k:
            sent[k - 1].wait_recv()
        result = times_rows(residual_rows[block(source), :], weight[...])
        acc[block(source), :] = result[:, :head]
        for j, peer in enumerate(peers):
            out_buf[j, block(source), :] = result[:, (j + 1) * head : (j + 2) * head].astype(bf16)
            got.append(
                go(
                    out_buf.at[j, block(source)],
                    in_buf.at[j, block(source)],
                    (hs, hr),
                    (j, k),
                    col=peer,
                )
            )
    for copy in got:
        copy.wait_recv()
    attended_grad[...] = (
        acc[...] + in_buf[0].astype(f32) + in_buf[1].astype(f32) + in_buf[2].astype(f32)
    ).astype(bf16)
    for copy in spread:
        copy.wait_recv()
    for copy in pending:
        copy.wait_send()
    steps.finish()


def middle_step(part, middle, cotangent, scale, gain, weight, shared):
    rows, columns = middle.shape
    piece = shared.shape[1]
    return pl.pallas_call(
        middle_kernel,
        out_shape=(
            jax.ShapeDtypeStruct((rows, columns), f32),
            jax.ShapeDtypeStruct((4 * rows, columns), bf16),
            jax.ShapeDtypeStruct((4 * rows, VDIM), bf16),
            jax.ShapeDtypeStruct((1, columns), f32),
            jax.ShapeDtypeStruct((4, 4 * piece, columns), bf16),
        ),
        in_specs=[VMEM] * 7,
        out_specs=(VMEM,) * 5,
        scratch_shapes=[
            pltpu.VMEM((4, 8, rows), f32),
            pltpu.VMEM((3, 4 * rows, VDIM), bf16),
            pltpu.VMEM((3, 4 * rows, VDIM), bf16),
            pltpu.VMEM((4 * rows, VDIM), f32),
            pltpu.VMEM((4, piece, columns), bf16),
            pltpu.VMEM((4, piece, columns), bf16),
            *pair(3),
            *pair(3),
            *pair(3, 4),
            *pair(7),
            *reduce_scratch(rows, columns),
        ],
        compiler_params=params(3),
        cost_estimate=cost(1 << 29, 200),
        name="middle_step",
    )(part, middle, cotangent, scale, gain, weight, shared)


def tail_kernel(
    part, narrow_part, query, ready, residual_grad, inputs, scale, gain, gain_part,
    inputs_grad, sums, narrow, gains, latent_gain,
    chunk_in, all_parts, narrow_all, lat_buf, lat_half, sum_buf,
    qs, qr, ps, pr, as_, ar, ls, lr, ns, nr, ss, sr, gs, gr, *scratch,
):
    row, sibling, across, corner = place()
    col = lax.axis_index("col")
    dp = lax.axis_index("dp")
    z = lax.rem(dp, 4)
    far = lax.rem(dp + 4, 8)
    peers = (sibling, across, corner)
    greet(peers, row, [{"dp": along_z(dp, k)} for k in (1, 2, 3)] + [{"dp": far}])
    pending = []
    go = starter(pending)
    count = len(scratch) // 2
    steps = Reduction(part, scratch[:count], row, sibling, across)
    before = Reduction(narrow_part, scratch[count:], row, sibling, across)
    rows, columns = inputs.shape
    piece = query.shape[0]
    lat = narrow_all.shape[1]
    keep = lat - 32

    def head(at):
        return pl.ds(pl.multiple_of(at * piece, piece), piece)

    def chunk(at):
        return pl.ds(pl.multiple_of(at * 2 * piece, 2 * piece), 2 * piece)

    before.start()
    dealt = [
        go(
            query.at[:, pl.ds((j + 1) * columns, columns)],
            all_parts.at[head(4 + col)],
            (qs, qr),
            j,
            col=peer,
        )
        for j, peer in enumerate(peers)
    ]
    steps.start()
    all_parts[pl.ds(0, 4 * piece), :] = ready[...]
    all_parts[head(4 + col), :] = query[:, pl.ds(0, columns)]
    before.along()
    for copy in dealt:
        copy.wait_recv()
    scattered = [
        go(
            all_parts.at[chunk(lax.rem(z + k, 4))],
            chunk_in.at[k - 1],
            (ps, pr),
            k - 1,
            dp=along_z(dp, k),
        )
        for k in (1, 2, 3)
    ]
    steps.along()
    before.side()
    lat_buf[z] = jnp.concatenate(
        [before.total(), gain_part[...], jnp.zeros((15, columns), f32)], axis=0
    ).astype(bf16)
    along = [
        go(lat_buf.at[z], lat_buf.at[z], (ls, lr), k - 1, dp=along_z(dp, k)) for k in (1, 2, 3)
    ]
    total = all_parts[chunk(z), :].astype(f32)
    for k in (1, 2, 3):
        scattered[k - 1].wait_recv()
        total += chunk_in[k - 1].astype(f32)
    chunk_in[3] = total.astype(bf16)
    halves = go(chunk_in.at[3], chunk_in.at[4], (ps, pr), 3, dp=far)
    steps.over()
    for copy in along:
        copy.wait_recv()
    lat_half[0] = (
        (lat_buf[0].astype(f32) + lat_buf[1].astype(f32))
        + (lat_buf[2].astype(f32) + lat_buf[3].astype(f32))
    ).astype(bf16)
    other = go(lat_half.at[0], lat_half.at[1], (ls, lr), 3, dp=far)
    steps.collect(0)
    halves.wait_recv()
    sums[chunk(z), :] = (chunk_in[3].astype(f32) + chunk_in[4].astype(f32)).astype(bf16)
    shared = [
        go(sums.at[chunk(z)], sums.at[chunk(z)], (as_, ar), k - 1, dp=along_z(dp, k))
        for k in (1, 2, 3)
    ]
    upstream = steps.total()
    weighted = upstream * gain[...]
    values = inputs[...].astype(f32)
    scales = scale[...]
    inner = ColumnSum(
        jnp.sum(weighted * values, axis=1, keepdims=True), sum_buf, (ss, sr), go, peers
    )
    other.wait_recv()
    narrow_all[row] = (lat_half[0].astype(f32) + lat_half[1].astype(f32)).astype(bf16)
    spread = [
        go(narrow_all.at[row], narrow_all.at[row], (ns, nr), k - 1, row=lax.rem(row + k, 4))
        for k in (1, 2, 3)
    ]
    inputs_grad[...] = (
        residual_grad[...]
        + scales * weighted
        - values * (scales * scales * scales * inner.total() / D)
    ).astype(bf16)
    for copy in spread:
        copy.wait_recv()
    narrow[...] = narrow_all[:, :keep, :]
    latent_gain[col] = narrow_all[0, pl.ds(keep, 16), :]
    last = [
        go(latent_gain.at[col], latent_gain.at[col], (gs, gr), j, col=peer)
        for j, peer in enumerate(peers)
    ]
    edge = pl.ds(keep + 16, 16)
    gains[...] = (
        narrow_all[0, edge, :].astype(f32)
        + narrow_all[1, edge, :].astype(f32)
        + narrow_all[2, edge, :].astype(f32)
        + narrow_all[3, edge, :].astype(f32)
    )
    for copy in last + shared:
        copy.wait_recv()
    for copy in pending:
        copy.wait_send()
    steps.finish()
    before.finish()


def tail_step(
    part, narrow_part, query, ready, residual_grad, inputs, scale, gain, gain_part
):
    rows, columns = inputs.shape
    piece = query.shape[0]
    narrow_rows = narrow_part.shape[0] // 4
    lat = narrow_rows + 16
    return pl.pallas_call(
        tail_kernel,
        out_shape=(
            jax.ShapeDtypeStruct((rows, columns), bf16),
            jax.ShapeDtypeStruct((8 * piece, columns), bf16),
            jax.ShapeDtypeStruct((4, lat - 32, columns), bf16),
            jax.ShapeDtypeStruct((16, columns), f32),
            jax.ShapeDtypeStruct((4, 16, columns), bf16),
        ),
        in_specs=[VMEM] * 9,
        out_specs=(VMEM,) * 5,
        scratch_shapes=[
            pltpu.VMEM((5, 2 * piece, columns), bf16),
            pltpu.VMEM((8 * piece, columns), bf16),
            pltpu.VMEM((4, lat, columns), bf16),
            pltpu.VMEM((4, lat, columns), bf16),
            pltpu.VMEM((2, lat, columns), bf16),
            pltpu.VMEM((4, 8, rows), f32),
            *pair(3),
            *pair(4),
            *pair(3),
            *pair(4),
            *pair(3),
            *pair(3),
            *pair(3),
            *reduce_scratch(rows, columns),
            *reduce_scratch(narrow_rows, columns),
        ],
        compiler_params=params(4),
        cost_estimate=cost(1 << 20, 200),
        name="tail_step",
    )(part, narrow_part, query, ready, residual_grad, inputs, scale, gain, gain_part)


score_scale = (NOPE + ROPE) ** (-0.5)


def swap_halves(values):
    lane = lax.broadcasted_iota(jnp.int32, values.shape, 1)
    return jnp.where(
        lax.rem(lane, 64) < 32, pltpu.roll(values, 96, 1), pltpu.roll(values, 32, 1)
    )


def masked_scores(queries, keys, early, start):
    scores = times_rows(queries, keys) * score_scale
    query_pos = start + lax.broadcasted_iota(jnp.int32, scores.shape, 0)
    key_pos = lax.broadcasted_iota(jnp.int32, scores.shape, 1)
    return jnp.where((key_pos <= query_pos) | (early > 0.0), scores, masked_score)


def front_kernel(
    input_rows, project, expand, weight, inputs, cotangent, cosine, sine, early, gain,
    gate, up, down, low_gate, low_up, router, low_down,
    middle, full, attended_rows, out_grad, normed, scale, content, latent_scale, compact,
    queries, keys, values, log_total, gates, ups, downs, lows,
    attended, own, out_buf, in_buf, acc, as_, ar, ps, pr, *sems,
):
    row, sibling, across, corner = place()
    peers = (sibling, across, corner)
    greet(peers, row, deal_peers(peers) + [{"dp": pair_along_z()}])
    pending = []
    go = starter(pending)
    rows, columns = inputs.shape
    head = attended.shape[1]
    order = (2, 1, 3, 0)
    beside = Gather(cotangent, out_grad, sems[6:12], go, row, sibling, across)
    deal = Deal(sems[12:14], sems[14], pending, lax.axis_index("col"), peers)
    ff = up.shape[1]
    low = low_down.shape[0] // 4
    beside.begin()
    deal.send_pair(lambda column, e: gate.at[2 * column + e], gates, ff)
    deal.send_pair(lambda column, e: up.at[2 * column + e], ups, ff)

    first_gain = project[pl.ds(RANK + 256, 16), :].astype(f32)[:1]
    for i in range(4):
        at = pl.ds(i * rows, rows)
        wide = input_rows[at, :].astype(f32)
        scales = lax.rsqrt(jnp.mean(wide * wide, axis=1, keepdims=True) + norm_eps)
        scale[at, :] = scales
        normal = (wide * scales * first_gain).astype(bf16)
        normed[at, :] = normal
        projected = times_rows(normal, project[pl.ds(0, RANK + 256), :])
        inner = projected[:, :RANK]
        inner_scale = lax.rsqrt(jnp.mean(inner * inner, axis=1, keepdims=True) + norm_eps)
        content[at, :] = inner
        latent_scale[at, :] = inner_scale
        narrow = (inner * inner_scale * gain[...]).astype(bf16)
        compact[at, :] = narrow
        pair_rows = jnp.dot(narrow, expand[...], preferred_element_type=f32)
        both = projected[:, RANK + NOPE :]
        both = both * cosine[at, :] + swap_halves(both) * sine[at, :]
        lane = lax.broadcasted_iota(jnp.int32, both.shape, 1)
        queries[at, pl.ds(0, NOPE)] = projected[:, RANK : RANK + NOPE].astype(bf16)
        queries[at, pl.ds(NOPE, 128)] = jnp.where(lane < ROPE, both, 0.0).astype(bf16)
        keys[at, pl.ds(0, NOPE)] = pair_rows[:, :NOPE].astype(bf16)
        keys[at, pl.ds(NOPE, 128)] = jnp.where(
            lane < ROPE, pltpu.roll(both, 64, 1), 0.0
        ).astype(bf16)
        values[at, :] = pair_rows[:, NOPE:].astype(bf16)
    beside.second()
    deal.send(rows_at(low_gate, low), lanes(lows, 0, low), True)
    deal.send(rows_at(low_up, low), lanes(lows, low, low), False)
    deal.send(lambda column: router, lanes(lows, 2 * low, 16), True)
    deal.send(rows_at(low_down, low), lanes(lows, 2 * low + 16, low), True)

    def start_of(k):
        return pl.multiple_of(lax.rem(row + k, 4) * rows, rows)

    def block(k):
        return pl.ds(start_of(k), rows)

    def slot(k):
        return pl.ds(k * head, head)

    got = {}
    for k in order:
        scores = masked_scores(queries[block(k), :], keys[...], early[...], start_of(k))
        top = jnp.max(scores, axis=1, keepdims=True)
        powers = jnp.exp(scores - top)
        power_sum = jnp.sum(powers, axis=1, keepdims=True)
        log_total[block(k), :] = top + jnp.log(power_sum)
        probs = (powers / power_sum).astype(bf16)
        attended[block(k), :] = jnp.dot(
            probs, values[...], preferred_element_type=f32
        ).astype(bf16)
        for j, peer in ((2, across), (1, sibling)):
            got[j, k] = go(
                attended.at[block(k)],
                attended_rows.at[block(k), slot(j)],
                (as_, ar),
                (j - 1, k),
                col=peer,
            )
        attended_rows[block(k), slot(0)] = attended[block(k), :]
    deal.exchange()
    beside.forward_first()
    for k in order:
        got[2, k].wait_recv()
        view = attended_rows.at[block(k), slot(2)]
        got[3, k] = go(view, attended_rows.at[block(k), slot(3)], (as_, ar), (2, k), col=sibling)
    deal.send_pair(lambda column, e: down.at[2 * column + e], downs, ff)
    sent = {}
    for k in order:
        got[1, k].wait_recv()
        got[3, k].wait_recv()
        result = jnp.dot(attended_rows[block(k), :], weight[...], preferred_element_type=f32)
        if k:
            out_buf[k - 1] = result.astype(bf16)
            sent[k] = go(
                out_buf.at[k - 1], in_buf.at[k - 1], (ps, pr), k - 1, row=lax.rem(row + k, 4)
            )
        else:
            acc[...] = result + inputs[...].astype(f32)
    total = acc[...]
    for k in (1, 3, 2):
        sent[k].wait_recv()
        total += in_buf[k - 1].astype(f32)
    middle[...] = total
    own[...] = total.astype(bf16)
    gather = Gather(own, full, sems[:6], go, row, sibling, across)
    gather.begin()
    beside.forward_rest()
    gather.second()
    deal.exchange()
    gather.forward_first()
    gather.forward_rest()
    beside.finish()
    gather.finish()
    deal.finish()
    for copy in pending:
        copy.wait_send()


def front_step(
    input_rows, project, expand, weight, inputs, cotangent, cosine, sine, early, gain,
    gate, up, down, low_gate, low_up, router, low_down,
):
    rows, columns = inputs.shape
    tokens, width = input_rows.shape
    low = low_down.shape[0] // 4

    def array(*shape, kind=bf16):
        return jax.ShapeDtypeStruct(shape, kind)

    return pl.pallas_call(
        front_kernel,
        out_shape=(
            array(rows, columns, kind=f32),
            array(tokens, width),
            array(tokens, columns),
            array(tokens, width),
            array(tokens, width),
            array(tokens, 1, kind=f32),
            array(tokens, RANK, kind=f32),
            array(tokens, 1, kind=f32),
            array(tokens, RANK),
            array(tokens, 256),
            array(tokens, 256),
            array(tokens, VDIM),
            array(tokens, 1, kind=f32),
            array(2 * up.shape[1], width),
            array(2 * up.shape[1], width),
            array(2 * up.shape[1], width),
            array(3 * low + 16, width),
        ),
        in_specs=[VMEM] * 10 + [HBM] * 7,
        out_specs=(VMEM,) * 13 + (HBM,) * 4,
        scratch_shapes=[
            pltpu.VMEM((tokens, VDIM), bf16),
            pltpu.VMEM((rows, columns), bf16),
            pltpu.VMEM((3, rows, columns), bf16),
            pltpu.VMEM((3, rows, columns), bf16),
            pltpu.VMEM((rows, columns), f32),
            *pair(3, 4),
            *pair(3),
            *gather_scratch,
            *gather_scratch,
            *deal_scratch(10),
        ],
        compiler_params=params(5),
        cost_estimate=cost(1 << 33, 150),
        name="front_step",
    )(
        input_rows, project, expand, weight, inputs, cotangent, cosine, sine, early, gain,
        gate, up, down, low_gate, low_up, router, low_down,
    )


def attend_back_kernel(
    queries, keys, values, log_total, attended_grad, early, compact, content, latent_scale, gain,
    expand, cosine, sine, project, normed, input_rows, scale, attended_rows, residual_rows, router,
    normed_grad, narrow, query_part, ready,
    query_grad, key_grad, value_grad, pair_grad, project_grad, first_sum, gain_sum,
):
    tile = 256
    col = lax.axis_index("col")
    tokens = queries.shape[0]
    key_grad[...] = jnp.zeros_like(key_grad)
    value_grad[...] = jnp.zeros_like(value_grad)
    first_sum[...] = jnp.zeros_like(first_sum)
    gain_sum[...] = jnp.zeros_like(gain_sum)
    for i in range(tokens // tile):
        at = pl.ds(i * tile, tile)
        query = queries[at, :]
        upstream = attended_grad[at, :]
        scores = masked_scores(query, keys[...], early[...], i * tile)
        probs = jnp.exp(scores - log_total[at, :])
        value_grad[...] += over_units(probs.astype(bf16), upstream)
        weight_grad = times_rows(upstream, values[...])
        centre = jnp.sum(probs * weight_grad, axis=1, keepdims=True)
        score_grad = (probs * (weight_grad - centre)).astype(bf16)
        query_grad[at, :] = (
            jnp.dot(score_grad, keys[...], preferred_element_type=f32) * score_scale
        )
        key_grad[...] += over_units(score_grad, query)
    for i in range(tokens // tile):
        at = pl.ds(i * tile, tile)
        keys_back = key_grad[at, :] * score_scale
        query_back = query_grad[at, :]
        pair_rows = jnp.concatenate([keys_back[:, :NOPE], value_grad[at, :]], axis=1).astype(bf16)
        pair_grad[at, :] = pair_rows
        compact_grad = times_rows(pair_rows, expand[...])
        inner = content[at, :]
        scales = latent_scale[at, :]
        weighted = compact_grad * gain[...]
        inner_sum = jnp.sum(weighted * inner, axis=1, keepdims=True)
        content_grad = scales * weighted - inner * (scales * scales * scales * inner_sum / RANK)
        gain_sum[...] += jnp.sum(compact_grad * inner * scales, axis=0, keepdims=True)
        both = query_back[:, NOPE:]
        lane = lax.broadcasted_iota(jnp.int32, both.shape, 1)
        both = jnp.where(lane < ROPE, both, pltpu.roll(keys_back[:, NOPE:], 64, 1))
        both = both * cosine[at, :] - swap_halves(both) * sine[at, :]
        rows = jnp.concatenate([content_grad, query_back[:, :NOPE], both], axis=1).astype(bf16)
        project_grad[at, :] = rows
        back = jnp.dot(rows, project[pl.ds(0, RANK + 256), :], preferred_element_type=f32)
        normed_grad[at, :] = back.astype(bf16)
        first_sum[...] += jnp.sum(
            back * (input_rows[at, :].astype(f32) * scale[at, :]), axis=0, keepdims=True
        )
    each = narrow.shape[0] // 4
    lat = each - 16
    for k in range(4):
        lanes_at = pl.ds(512 * k, 512)
        part = over_units(project_grad[...], normed[:, lanes_at]).astype(bf16)
        query_part[:, lanes_at] = part[RANK : RANK + 192]
        latent_part = jnp.concatenate([part[:RANK], part[RANK + 192 :]], axis=0)
        extra = jnp.concatenate(
            [
                gain_sum[...],
                first_sum[:, lanes_at],
                router[pl.ds(0, EXPERTS), lanes_at].astype(f32),
                jnp.zeros((6, 512), f32),
            ],
            axis=0,
        ).astype(bf16)
        for r in range(4):
            narrow[pl.ds(r * each, lat), lanes_at] = latent_part[r * lat : (r + 1) * lat]
            narrow[pl.ds(r * each + lat, 16), lanes_at] = extra
    head_grad = over_units(attended_rows[...], residual_rows[...]).astype(bf16)
    for k in range(4):
        own = lax.rem(lax.rem(col, 2) + k % 2, 2) + 2 * lax.rem(col // 2 + k // 2, 2)
        start = pl.multiple_of(own * VDIM, VDIM)
        ready[pl.ds(start, VDIM), :] = head_grad[k * VDIM : (k + 1) * VDIM]
    ready[pl.ds(4 * VDIM, 256), :] = over_units(pair_grad[...], compact[...]).astype(bf16)


def attend_back_step(*arguments):
    tokens, width = arguments[15].shape
    return pl.pallas_call(
        attend_back_kernel,
        out_shape=(
            jax.ShapeDtypeStruct((tokens, width), bf16),
            jax.ShapeDtypeStruct((RANK + ROPE + 64, width), bf16),
            jax.ShapeDtypeStruct((192, width), bf16),
            jax.ShapeDtypeStruct((768, 512), bf16),
        ),
        in_specs=[VMEM] * 20,
        out_specs=(VMEM,) * 4,
        scratch_shapes=[
            pltpu.VMEM((tokens, 256), f32),
            pltpu.VMEM((tokens, 256), f32),
            pltpu.VMEM((tokens, VDIM), f32),
            pltpu.VMEM((tokens, 256), bf16),
            pltpu.VMEM((tokens, RANK + 256), bf16),
            pltpu.VMEM((1, width), f32),
            pltpu.VMEM((1, RANK), f32),
        ],
        compiler_params=pltpu.CompilerParams(vmem_limit_bytes=56 << 20),
        cost_estimate=cost(1 << 34, 40),
        name="attend_back_step",
    )(*arguments)


def rotary_tables(length, half_width):
    position = jnp.arange(length, dtype=f32)[:, None]
    frequency = jnp.exp(jnp.arange(half_width, dtype=f32) * (-math.log(10000.0) / half_width))
    angles = position * frequency[None, :]
    return (jnp.cos(angles), jnp.sin(angles))


def pad_to(values, axis, size):
    widths = [(0, 0)] * values.ndim
    widths[axis] = (0, size - values.shape[axis])
    return jnp.pad(values, widths)


def on_device(
    inputs,
    attention_gain,
    query_weight,
    latent_weight,
    latent_gain,
    expand_weight,
    output_weight,
    feedforward_gain,
    router_weight,
    shared_gate,
    shared_up,
    shared_down,
    expert_gate,
    expert_up,
    expert_down,
    routes,
    prefix,
    cotangent,
):
    row = lax.axis_index("row")
    col = lax.axis_index("col")
    prefix_len = prefix[0]
    cos_table, sin_table = rotary_tables(SEQ, ROPE // 2)
    first_gain = attention_gain.astype(f32)
    second_gain = feedforward_gain.astype(f32)
    compact_gain = latent_gain.astype(f32)
    rows = inputs.shape[0]
    ff = expert_gate.shape[2]
    low = shared_down.shape[0] // 4
    cosine = jnp.tile(cos_table, (1, 4))
    sine = jnp.tile(jnp.concatenate([-sin_table, sin_table], axis=1), (1, 2))
    early = (jnp.arange(SEQ, dtype=jnp.int32) < prefix_len).astype(f32)[None, :]

    gains = jnp.stack([attention_gain, feedforward_gain])
    common = jnp.concatenate([latent_weight.T, pad_to(gains, 0, 16)], axis=0)
    input_rows, project_all = start_step(inputs, common, query_weight.T)
    second_all = project_all[RANK + 257].astype(f32)
    out_weight = jnp.concatenate(
        [lax.dynamic_slice_in_dim(output_weight, (col ^ k) * VDIM, VDIM, 0) for k in range(4)],
        axis=0,
    )
    (
        residual_mid,
        middle_rows,
        attended_rows,
        out_grad,
        normed,
        scale_one,
        content,
        latent_scale,
        compact,
        queries,
        keys,
        values,
        log_total,
        gates,
        ups,
        downs,
        lows,
    ) = front_step(
        input_rows,
        project_all,
        expand_weight,
        out_weight,
        inputs,
        cotangent,
        cosine,
        sine,
        early,
        compact_gain[None, :],
        expert_gate.transpose(0, 2, 1),
        expert_up.transpose(0, 2, 1),
        expert_down,
        shared_gate.T,
        shared_up.T,
        pad_to(router_weight.T, 0, 16),
        shared_down,
    )

    experts = jnp.arange(EXPERTS, dtype=jnp.int32)
    named = jnp.any(routes.T[None, :, :] == experts[:, None, None], axis=1).astype(f32)
    mine = (experts[:, None] == 2 * col + jnp.arange(128, dtype=jnp.int32)[None, :]).astype(f32)
    hidden, scale_two, act, delta, combined = expert_step(
        middle_rows, out_grad, gates, ups, downs, lows, second_all[None, :], named, mine
    )
    expert_grad, shared_grad, router_part, combined_sum, hidden_grad = grads_step(
        hidden, out_grad, delta, act, combined, gates, ups, lows
    )
    output = (residual_mid + combined_sum).astype(bf16)
    expert_sum = lax.psum_scatter(expert_grad, "dp", scatter_dimension=0, tiled=True)[0]

    my_scale_one = lax.dynamic_slice_in_dim(scale_one, row * rows, rows, 0)
    my_scale_two = lax.dynamic_slice_in_dim(scale_two[:, :1], row * rows, rows, 0)
    residual_grad, residual_rows, attended_grad, second_gain_part, shared_all = middle_step(
        hidden_grad,
        residual_mid,
        cotangent,
        my_scale_two,
        second_gain[None, :],
        out_weight,
        shared_grad,
    )
    normed_grad, narrow_part, query_part, ready = attend_back_step(
        queries,
        keys,
        values,
        log_total,
        attended_grad,
        early,
        compact,
        content,
        latent_scale,
        compact_gain[None, :],
        expand_weight,
        cosine,
        sine,
        project_all,
        normed,
        input_rows,
        scale_one,
        attended_rows,
        residual_rows,
        router_part,
    )
    inputs_grad, sums, narrow, gains, latent_small = tail_step(
        normed_grad,
        narrow_part,
        query_part,
        ready,
        residual_grad,
        inputs,
        my_scale_one,
        first_gain[None, :],
        second_gain_part,
    )
    sums, narrow, shared_all, expert_sum = lax.optimization_barrier(
        (sums, narrow, shared_all, expert_sum)
    )
    pairs = [
        (dp * 4 + c, (2 * c + dp // 4) * 4 + (c ^ (dp % 4))) for dp in range(8) for c in range(4)
    ]
    expert_sum = lax.ppermute(expert_sum, ("dp", "col"), pairs)
    output_weight_grad = sums[:512].astype(f32)
    expand_grad = sums[512:768].T.astype(f32)
    query_weight_grad = sums[768:].T.astype(f32)
    latent_weight_grad = narrow.reshape(-1, 512).T.astype(f32)
    latent_gain_grad = latent_small[0, 0].astype(f32)
    own_small = lax.dynamic_index_in_dim(latent_small, col, 0, False).astype(f32)
    first_gain_grad = own_small[1]
    router_grad = own_small[2 : 2 + EXPERTS].T
    second_gain_grad = gains[0]

    expert_sum = expert_sum.astype(f32)
    expert_gate_grad = expert_sum[None, :ff].transpose(0, 2, 1)
    expert_up_grad = expert_sum[None, ff : 2 * ff].transpose(0, 2, 1)
    expert_down_grad = expert_sum[None, 2 * ff :]
    shared_sum = shared_all.astype(f32)
    shared_gate_grad = shared_sum[:, :low].reshape(4 * low, 512).T
    shared_up_grad = shared_sum[:, low : 2 * low].reshape(4 * low, 512).T
    shared_down_grad = shared_sum[:, 2 * low : 3 * low].reshape(4 * low, 512)
    return (
        output,
        inputs_grad,
        first_gain_grad,
        query_weight_grad,
        latent_weight_grad,
        latent_gain_grad,
        expand_grad,
        output_weight_grad,
        second_gain_grad,
        router_grad,
        shared_gate_grad,
        shared_up_grad,
        shared_down_grad,
        expert_gate_grad,
        expert_up_grad,
        expert_down_grad,
    )


def solution(mesh):
    placed = (
        P(("dp", "row"), "col"),
        P("col"),
        P("col", "row"),
        P("col", None),
        P(),
        P(None, ("row", "col")),
        P("row", "col"),
        P("col"),
        P("col", None),
        P("col", "row"),
        P("col", "row"),
        P("row", "col"),
        P(None, "col", "row"),
        P(None, "col", "row"),
        P(None, "row", "col"),
        P("dp", None),
        P("dp"),
        P(("dp", "row"), "col"),
    )
    return jax.shard_map(
        on_device,
        mesh=mesh,
        in_specs=placed,
        out_specs=(
            P(("dp", "row"), "col"),
            P(("dp", "row"), "col"),
            P("col"),
            P("col", "row"),
            P("col", None),
            P(),
            P(None, ("row", "col")),
            P("row", "col"),
            P("col"),
            P("col", None),
            P("col", "row"),
            P("col", "row"),
            P("row", "col"),
            P("dp", "col", "row"),
            P("dp", "col", "row"),
            P("dp", "row", "col"),
        ),
        check_vma=False,
    )
```
